128 devices in a mesh: space: 32 (over z, y_hi, x), vel: 4 (over y_lo, core).
Axes of the slice: x: 4, y: 4 (y_hi: 2, y_lo: 2; y = y_hi * 2 + y_lo), z: 4, core: 2. Of those that a mesh axis runs over, the one named last changes fastest.
Arguments:
- dist: float32 [128, 10, 32768], P('space', None, 'vel'), may hold values from 0.1 to 2
- phi: float32 [32768], replicated, may hold values from 0.5 to 2
- khat: float32 [32, 1024], replicated, may hold values from 0.2 to 2
- deriv: float32 [3, 10, 10], replicated, may hold values from -2 to 2
- lift: float32 [4, 10, 6], replicated, may hold values from -2.5 to 2.5
- normals: float32 [4, 3], replicated, may hold values from -1 to 1, as said below
- wall_maxw: float32 [32768], P('vel'), may hold values from 0.1 to 1
- free_stream: float32 [32768], P('vel'), may hold values from 0.1 to 1
- inject: float32 [4, 32768], P(None, 'vel'), may hold values from 0 to 1
- nb_local: int32 [128, 4], P('space'), may hold values from 0 to 3
- nb_side: int32 [128, 4], P('space'), may hold values from 0 to 3, as said below
- wall_flag: int32 [128, 4], P('space'), may hold values from 0 to 1
- inj_id: int32 [128, 4], P('space'), may hold values from 0 to 3
Outputs:
- rate: float32 [128, 10, 32768], P('space', None, 'vel')
The draws below stay inside these ranges and needn't reach their ends.
Inputs may be any that keep to these rules, and one draw needn't show every extreme that they name: nb_side: 0 the neighbour is on the same index of space, 1 on the index below, 2 on the index above, 3 the face lies on the boundary. On every index of space but the first, exactly one face has nb_side 1, and it is face 0 of its element; on every index but the last, exactly one face has nb_side 2, and it is face 1 of its element; no other face has nb_side 1 or 2. Where nb_side is 3, nb_local is 0. Faces are joined in pairs consistently. `normals`: every component has magnitude between 0.4 and 1.
All inputs are finite; a program needn't handle non-finite values.
Results may differ from the reference program's by a relative error of at most 0.0001.
Values sent between devices are 32-bit elements; how exact they have to be, the bound alone decides.
A program may use at most 128 MiB of HBM per device.

```python
import math
import jax
import jax.numpy as jnp
import numpy as np
from jax import lax

NV1 = 32
NV = 32768
E_DEV = 4
ELEMS = 128
NINJ = 4


def topology(key):
    devices = ELEMS // E_DEV
    base = jax.random.fold_in(key, 7)
    first, second, third = jax.random.split(base, 3)
    chain = jax.vmap(lambda sub: jax.random.permutation(sub, E_DEV))(jax.random.split(first, devices)).astype(jnp.int32)
    lateral = jax.vmap(lambda sub: jax.random.permutation(sub, E_DEV))(jax.random.split(second, devices)).astype(jnp.int32)
    links = jax.random.randint(third, (devices, E_DEV - 1), 0, 2).astype(jnp.int32)
    device = jnp.arange(devices).astype(jnp.int32)[:, None]
    place = jnp.arange(E_DEV).astype(jnp.int32)[None, :]
    next_first = jnp.roll(chain[:, 0], -1)[:, None]
    prev_last = jnp.roll(chain[:, -1], 1)[:, None]
    next_side = jnp.where(place < E_DEV - 1, 0, jnp.where(device < devices - 1, 2, 3))
    next_local = jnp.where(next_side == 3, 0, jnp.where(place < E_DEV - 1, jnp.roll(chain, -1, axis=1), next_first))
    prev_side = jnp.where(place > 0, 0, jnp.where(device > 0, 1, 3))
    prev_local = jnp.where(prev_side == 3, 0, jnp.where(place > 0, jnp.roll(chain, 1, axis=1), prev_last))
    zeros_col = jnp.zeros((devices, 1), jnp.int32)
    link_up = jnp.concatenate([links, zeros_col], axis=1)
    link_down = jnp.concatenate([zeros_col, links], axis=1)
    up_local = jnp.where(link_up == 1, jnp.roll(lateral, -1, axis=1), 0)
    up_side = jnp.where(link_up == 1, 0, 3)
    down_local = jnp.where(link_down == 1, jnp.roll(lateral, 1, axis=1), 0)
    down_side = jnp.where(link_down == 1, 0, 3)
    local = jnp.zeros((devices, E_DEV, 4), jnp.int32)
    side = jnp.zeros((devices, E_DEV, 4), jnp.int32)
    local = local.at[device, chain, 0].set(prev_local.astype(jnp.int32))
    local = local.at[device, chain, 1].set(next_local.astype(jnp.int32))
    local = local.at[device, lateral, 2].set(down_local.astype(jnp.int32))
    local = local.at[device, lateral, 3].set(up_local.astype(jnp.int32))
    side = side.at[device, chain, 0].set(prev_side.astype(jnp.int32))
    side = side.at[device, chain, 1].set(next_side.astype(jnp.int32))
    side = side.at[device, lateral, 2].set(down_side.astype(jnp.int32))
    side = side.at[device, lateral, 3].set(up_side.astype(jnp.int32))
    return (local.reshape(ELEMS, 4), side.reshape(ELEMS, 4))


def draw_nb_local(key, part):
    return topology(key)[0]


def draw_nb_side(key, part):
    return topology(key)[1]


def draw_normals(key, part):
    first, second = jax.random.split(jax.random.fold_in(key, 11))
    signs = jnp.where(jax.random.randint(first, (4, 3), 0, 2) == 1, 1.0, -1.0)
    magnitude = jnp.exp(jax.random.uniform(second, (4, 3), jnp.float32, math.log(0.4), 0.0))
    return (signs * magnitude).astype(jnp.float32)


def plant(drawn, key, least, high):
    shape = drawn.shape
    spot = [jax.random.randint(jax.random.fold_in(key, axis), (), 0, shape[axis]) for axis in range(len(shape))]
    drawn = drawn.at[tuple(spot)].set(least)
    longest = shape.index(max(shape))
    spot[longest] = (spot[longest] + 1) % shape[longest]
    return drawn.at[tuple(spot)].set(high)


def level_of(stream_key, extent, shards, least, top_value):
    factor_of, own = 1.0, jax.random.fold_in(stream_key, 6)
    for dim, blocks in shards:
        heights = jnp.exp(jax.random.uniform(jax.random.fold_in(own, dim), (blocks,), jnp.float32, least / len(shards), top_value / len(shards)))
        factor_of = factor_of * jnp.repeat(heights, extent[dim] // blocks).reshape([-1 if axis == dim else 1 for axis in range(len(extent))])
    return factor_of


def bell_draw(own_key, shape, spread, reach, kind=jnp.bfloat16):
    return jnp.clip(spread * jax.random.normal(own_key, shape, jnp.float32), -reach, reach).astype(kind)


def setup_inputs(seed: int = 0) -> dict:
    seeds = jax.random.split(jax.random.key(seed), 14)
    return {
        "dist": jnp.clip(jnp.exp(math.log(2.0) - 2.9957323 * jax.random.uniform(seeds[0], (ELEMS, 10, NV), jnp.float32) ** level_of(seeds[0], (ELEMS, 10, NV), ((0, 32), (2, 4)), -0.2, 0.2)), 0.1, 2.0),
        "phi": jnp.clip(jnp.exp(jax.random.uniform(seeds[1], (NV,), jnp.float32, math.log(0.5), math.log(2.0))), 0.5, 2.0),
        "khat": jnp.clip(jnp.exp(jax.random.uniform(seeds[2], (NV1, NV1 * NV1), jnp.float32, math.log(0.2), math.log(2.0))), 0.2, 2.0),
        "deriv": bell_draw(seeds[3], (3, 10, 10), 10 ** -0.5, 2.0, jnp.float32),
        "lift": bell_draw(seeds[4], (4, 10, 6), 6 ** -0.5, 2.5, jnp.float32),
        "normals": draw_normals(jax.random.fold_in(seeds[13], 71), 0),
        "wall_maxw": jnp.clip(jnp.exp(math.log(1.0) - 2.3025851 * jax.random.uniform(seeds[6], (NV,), jnp.float32) ** level_of(seeds[6], (NV,), ((0, 4),), -0.2, 0.2)), 0.1, 1.0),
        "free_stream": jnp.clip(jnp.exp(math.log(1.0) - 2.3025851 * jax.random.uniform(seeds[7], (NV,), jnp.float32) ** level_of(seeds[7], (NV,), ((0, 4),), -0.2, 0.2)), 0.1, 1.0),
        "inject": jnp.clip(1.0 * jax.random.uniform(seeds[8], (NINJ, NV), jnp.float32) ** level_of(seeds[8], (NINJ, NV), ((1, 4),), -0.2, 0.2), 0.0, 1.0),
        "nb_local": draw_nb_local(jax.random.fold_in(seeds[13], 71), 0),
        "nb_side": draw_nb_side(jax.random.fold_in(seeds[13], 71), 0),
        "wall_flag": plant(jax.random.randint(seeds[11], (ELEMS, 4), 0, 2), jax.random.fold_in(seeds[11], 1), 0, 1).astype(jnp.int32),
        "inj_id": plant(jax.random.randint(seeds[12], (ELEMS, 4), 0, NINJ), jax.random.fold_in(seeds[12], 1), 0, NINJ - 1).astype(jnp.int32),
    }


face_table = np.array([[1, 2, 3, 5, 8, 9], [0, 2, 3, 6, 7, 9], [0, 1, 3, 4, 7, 8], [0, 1, 2, 4, 5, 6]], dtype=np.int32)
partner_faces = np.array([1, 0, 3, 2], dtype=np.int32)
speed_limit = 3.0


def reference(dist, phi, khat, deriv, lift, normals, wall_maxw, free_stream, inject, nb_local, nb_side, wall_flag, inj_id):
    points = NV1
    plane = points * points
    total = points * plane
    grid = speed_limit * ((2.0 * jnp.arange(points).astype(jnp.float32) + 1.0) / points - 1.0)
    vgrid = jnp.stack([jnp.repeat(grid, plane), jnp.tile(jnp.repeat(grid, points), points), jnp.tile(grid, plane)])
    hi = lax.Precision.HIGHEST
    vnorm = jnp.dot(normals, vgrid, precision=hi)
    posv = jnp.maximum(vnorm, 0.0)
    negv = jnp.minimum(vnorm, 0.0)
    traces = dist[:, face_table.reshape(-1), :].reshape(ELEMS, 4, 6, total)
    num = jnp.einsum('jv,ejkv->ejk', posv, traces, precision=hi)
    den = jnp.dot(-negv, wall_maxw, precision=hi)
    sigma = num / den[None, :, None]
    device = (jnp.arange(ELEMS) // E_DEV).astype(jnp.int32)
    offset = jnp.where(nb_side == 1, -1, jnp.where(nb_side == 2, 1, 0)).astype(jnp.int32)
    neighbour = jnp.clip((device[:, None] + offset) * E_DEV + nb_local, 0, ELEMS - 1).astype(jnp.int32)
    outer_int = traces[neighbour, jnp.asarray(partner_faces)[None, :]]
    injected = inject[inj_id]
    boundary = jnp.where(wall_flag[:, :, None, None] == 1, sigma[..., None] * wall_maxw + injected[:, :, None, :], free_stream)
    outer = jnp.where(nb_side[:, :, None, None] == 3, boundary, outer_int)
    transport = jnp.einsum('jnk,ejkv->env', lift, negv[None, :, None, :] * (traces - outer), precision=hi)
    for dim in range(3):
        transport = transport - vgrid[dim] * jnp.einsum('nm,emv->env', deriv[dim], dist, precision=hi)
    phi_cube = phi.reshape(points, points, points)
    kernel = khat.reshape(points, points, points)

    def collide_one(field):
        cube = field.reshape(-1, points, points, points)
        weighted = jnp.fft.fftn(phi_cube * cube, axes=(1, 2, 3))
        spectrum = jnp.fft.fftn(cube, axes=(1, 2, 3))
        gain = jnp.real(jnp.fft.ifftn(weighted * spectrum, axes=(1, 2, 3))) / total
        lossc = jnp.real(jnp.fft.ifftn(kernel * spectrum, axes=(1, 2, 3)))
        return (gain - cube * lossc).reshape(field.shape).astype(field.dtype)

    collide = lax.map(collide_one, dist)
    return transport + collide
```

```python
import math

import jax
import jax.numpy as jnp
import numpy as np
import ml_dtypes
from jax import lax
from jax.experimental import pallas as pl
from jax.experimental.pallas import tpu as pltpu
from jax.sharding import PartitionSpec as P

FACES = ((1, 2, 3, 5, 8, 9), (0, 2, 3, 6, 7, 9), (0, 1, 3, 4, 7, 8), (0, 1, 2, 4, 5, 6))
SPEED = 3.0
NODES = 10
ELEMS = 4
GROUP = 4
SLAB = 64
BLOCK = 256
HALF = 136
PACK = 128
TABLE = ELEMS * NODES * 8
HALO = TABLE + 5 * 8
POOL = HALO + 2 * NODES * 8


def split(x):
    hi = x.astype(ml_dtypes.bfloat16)
    lo = (x - hi.astype(np.float64)).astype(ml_dtypes.bfloat16)
    return hi, lo


def tables():
    turn = 2.0 * np.pi
    ka = np.repeat(np.arange(17), 8)
    kl = np.tile(np.arange(8), 17)
    a = np.repeat(np.arange(32), 8)
    bh = np.tile(np.arange(8), 32)
    bl = np.repeat(np.arange(4), 32)
    c = np.tile(np.arange(32), 4)
    angle = turn * ((np.outer(ka, a) % 32) / 32.0 + (np.outer(kl, bh) % 8) / 8.0)
    rows_fwd = np.concatenate([np.cos(angle), -np.sin(angle)], axis=0)
    angle = turn * ((np.outer(bl, bl) % 4) / 4.0 + (np.outer(c, c) % 32) / 32.0)
    co, si = np.cos(angle), np.sin(angle)
    lanes_fwd = np.concatenate(
        [np.concatenate([co, -si], axis=1), np.concatenate([si, co], axis=1)], axis=0
    )
    lanes_bwd = np.concatenate(
        [np.concatenate([co, si], axis=1), np.concatenate([-si, co], axis=1)], axis=0
    )
    angle = turn * ((np.outer(a, ka[:PACK]) % 32) / 32.0 + (np.outer(bh, kl[:PACK]) % 8) / 8.0)
    re, im = 2.0 * np.cos(angle), -2.0 * np.sin(angle)
    sign = np.where(a % 2 == 0, 1.0, -1.0)[:, None]
    angle = turn * ((np.outer(bh, np.arange(8)) % 8) / 8.0)
    re[:, :8] = np.cos(angle) + sign * np.sin(angle)
    im[:, :8] = -np.sin(angle) + sign * np.cos(angle)
    rows_bwd = np.concatenate([re, im], axis=1) * 2.0**-15

    def left(x):
        hi, lo = split(x)
        return np.concatenate([hi, hi, lo], axis=1)

    def right(x):
        hi, lo = split(x)
        return np.concatenate([hi, hi, lo], axis=0)

    angle = turn * np.outer(np.arange(8), bl) / 32.0
    twiddle = np.concatenate([np.cos(angle), np.sin(angle)], axis=0).astype(np.float32)
    lane = np.arange(128)
    mirror = (lane // 32) * 32 + (32 - lane % 32) % 32
    reverse = (lane[:, None] == mirror[None, :]).astype(ml_dtypes.bfloat16)
    return (left(rows_fwd), right(lanes_fwd), right(lanes_bwd), left(rows_bwd), twiddle, reverse)


def halves(x):
    hi = x.astype(jnp.bfloat16)
    lo = (x - hi.astype(jnp.float32)).astype(jnp.bfloat16)
    return hi, lo


def dot_left(table, x):
    hi, lo = halves(x)
    return jnp.dot(
        table, jnp.concatenate([hi, lo, hi], axis=0), preferred_element_type=jnp.float32
    )


def dot_right(x, table):
    hi, lo = halves(x)
    return jnp.dot(
        jnp.concatenate([hi, lo, hi], axis=1), table, preferred_element_type=jnp.float32
    )


def by_rows(x, y):
    return jnp.concatenate([x, y], axis=0)


def by_lanes(x, y):
    return jnp.concatenate([x, y], axis=1)


def turned(re, im, cos, sin):
    count = re.shape[0] // 8
    re = re.reshape(count, 8, 128)
    im = im.reshape(count, 8, 128)
    out_re = re * cos[None] - im * sin[None]
    out_im = re * sin[None] + im * cos[None]
    return out_re.reshape(count * 8, 128), out_im.reshape(count * 8, 128)


def collide(x, phi, sym, rows_fwd, lanes_fwd, lanes_bwd, rows_bwd, cos, sin):
    y = dot_left(rows_fwd, by_lanes(x * phi, x))
    wr, wi = turned(y[:HALF, :128], y[HALF:, :128], cos, -sin)
    fr, fi = turned(y[:HALF, 128:], y[HALF:, 128:], cos, -sin)
    s = dot_right(by_rows(by_lanes(wr, wi), by_lanes(fr, fi)), lanes_fwd)
    wr, wi, fr, fi = s[:HALF, :128], s[:HALF, 128:], s[HALF:, :128], s[HALF:, 128:]
    wr, wi = wr * 2.0**-15, wi * 2.0**-15

    def packed(re, im):
        first = re[:8] - im[PACK:]
        second = im[:8] + re[PACK:]
        return by_lanes(by_rows(first, re[8:PACK]), by_rows(second, im[8:PACK]))

    gain = packed(wr * fr - wi * fi, wr * fi + wi * fr)
    loss = packed(sym * fr, sym * fi)
    b = dot_right(by_rows(gain, loss), lanes_bwd)
    gr, gi = turned(b[:PACK, :128], b[:PACK, 128:], cos, sin)
    lr, li = turned(b[PACK:, :128], b[PACK:, 128:], cos, sin)
    z = dot_left(rows_bwd, by_rows(by_lanes(gr, lr), by_lanes(gi, li)))
    return z[:, :128] - x * z[:, 128:]


def kernel(
    space,
    dist,
    phi,
    khat,
    deriv,
    lift,
    normals,
    wall,
    free,
    inject,
    nb_local,
    nb_side,
    wall_flag,
    inj_id,
    rows_fwd,
    lanes_fwd,
    lanes_bwd,
    rows_bwd,
    twiddle,
    reverse,
    out,
    pool,
    block,
    result,
    back,
    moved,
    diff,
    negwall,
    straight,
    mirrored,
    sym,
    wallsum,
    halo_out,
    halo_in,
    sums_out,
    sums_in,
    fwd_send,
    fwd_recv,
    bwd_send,
    bwd_recv,
    halo_send,
    halo_recv,
    sums_send,
    sums_recv,
):
    f32 = jnp.float32
    me = lax.axis_index("vel")
    here = lax.axis_index("space")
    above = lax.rem(here + 1, space)
    below = lax.rem(here + space - 1, space)
    core = lax.rem(me, 2)
    flip = 1 - 2 * core
    across = lax.rem(me + 2, GROUP)
    partners = (across, across + flip, me + flip)

    def rows(start, count=8):
        return pl.ds(pl.multiple_of(start, 8), count)

    def forward(n, q):
        to = partners[q]
        return pltpu.make_async_remote_copy(
            src_ref=pool.at[pl.ds((to * NODES + n) * 8, 8)],
            dst_ref=block.at[pl.ds(n * 32 + me * 8, 8)],
            send_sem=fwd_send.at[n, q],
            recv_sem=fwd_recv.at[n, q],
            device_id={"vel": to},
        )

    def backward(n, q):
        to = partners[q]
        return pltpu.make_async_remote_copy(
            src_ref=result.at[rows(n * BLOCK + to * SLAB, SLAB)],
            dst_ref=back.at[rows((me * NODES + n) * SLAB, SLAB)],
            send_sem=bwd_send.at[n, q],
            recv_sem=bwd_recv.at[n, q],
            device_id={"vel": to},
        )

    def halo(side):
        return pltpu.make_async_remote_copy(
            src_ref=halo_out.at[side],
            dst_ref=halo_in.at[side],
            send_sem=halo_send.at[side],
            recv_sem=halo_recv.at[side],
            device_id={"space": below if side else above},
        )

    def sums(q):
        return pltpu.make_async_remote_copy(
            src_ref=sums_out,
            dst_ref=sums_in.at[q],
            send_sem=sums_send.at[q],
            recv_sem=sums_recv.at[q],
            device_id={"vel": partners[q]},
        )

    barrier = pltpu.get_barrier_semaphore()
    for to in partners:
        pl.semaphore_signal(barrier, inc=1, device_id={"vel": to})
    for to in (above, below):
        pl.semaphore_signal(barrier, inc=1, device_id={"space": to})
    pl.semaphore_wait(barrier, 5)

    @pl.loop(0, NODES)
    def _(n):
        for e in range(ELEMS):
            for a in range(8):
                pool[(e * NODES + n) * 8 + a] = dist[
                    pl.ds(n * BLOCK + a * 32 + e, 8, stride=4), :
                ]
        for q in range(3):
            forward(n, q).start()
        for a in range(8):
            block[n * 32 + me * 8 + a] = pool[(me * NODES + n) * 8 + a]

    up_elem = jnp.int32(0)
    down_elem = jnp.int32(0)
    for e in range(ELEMS):
        up_elem = up_elem + jnp.where(nb_side[e, 1] == 2, e, 0)
        down_elem = down_elem + jnp.where(nb_side[e, 0] == 1, e, 0)
    for side, elem, face in ((0, up_elem, 1), (1, down_elem, 0)):
        for k in range(6):
            for a in range(8):
                halo_out[side, k * 8 + a] = pool[(elem * NODES + FACES[face][k]) * 8 + a]
        halo(side).start()

    for q in range(4):
        for a in range(8):
            pool[TABLE + q * 8 + a] = inject[pl.ds(a * 32 + q, 8, stride=4), :]
    for a in range(8):
        pool[TABLE + 32 + a] = free[a * 8 : a * 8 + 8, :]

    sub = lax.broadcasted_iota(jnp.int32, (8, 128), 0)
    lane = lax.broadcasted_iota(jnp.int32, (8, 128), 1)

    def grid(i):
        return SPEED * ((2.0 * i.astype(f32) + 1.0) / 32.0 - 1.0)

    v2 = grid(lane % 32)
    v1 = grid(sub * 4 + lane // 32)

    def normal_speed(j, v0, v1):
        return normals[j, 0] * v0 + normals[j, 1] * v1 + normals[j, 2] * v2

    def partial_sums(i, carry):
        a = i // 4
        v0 = grid(me * 8 + a)
        b = (lax.rem(i, 4) * 2 + sub // 4) * 4 + lane // 32
        got = [dist[rows(n * BLOCK + i * 8), :] for n in range(NODES)]
        new = []
        for j in range(4):
            pos = jnp.maximum(normal_speed(j, v0, grid(b)), 0.0)
            for k in range(6):
                new.append(carry[j * 6 + k] + pos * got[FACES[j][k]])
        return tuple(new)

    zero = jnp.zeros((8, 128), f32)
    nums = lax.fori_loop(0, 32, partial_sums, (zero,) * 24)

    def partial_dens(a, carry):
        v0 = grid(me * 8 + a)
        new = []
        for j in range(4):
            value = jnp.minimum(normal_speed(j, v0, v1), 0.0) * wall[rows(a * 8), :]
            negwall[rows((j * 8 + a) * 8), :] = value
            new.append(carry[j] - value)
        return tuple(new)

    dens = lax.fori_loop(0, 8, partial_dens, (zero,) * 4)
    mine = zero
    for i, x in enumerate(nums):
        x = x + pltpu.roll(x, 4, 0)
        mine = jnp.where(lane == i, jnp.sum(x, axis=1, keepdims=True), mine)
    for j, x in enumerate(dens):
        x = jnp.broadcast_to(jnp.sum(x, axis=0, keepdims=True), (8, 128))
        mine = jnp.where(lane == 24 + j, jnp.sum(x, axis=1, keepdims=True), mine)
    sums_out[...] = mine
    for q in range(3):
        sums(q).start()

    for i in range(8):
        x = khat[:, i * 128 : (i + 1) * 128]
        straight[i * 32 : (i + 1) * 32, :] = x
    x = straight[...]
    x0 = x.astype(jnp.bfloat16)
    x = x - x0.astype(f32)
    x1 = x.astype(jnp.bfloat16)
    x2 = (x - x1.astype(f32)).astype(jnp.bfloat16)
    rev = reverse[...]
    mirrored[...] = (
        jnp.dot(x0, rev, preferred_element_type=f32) + jnp.dot(x1, rev, preferred_element_type=f32)
    ) + jnp.dot(x2, rev, preferred_element_type=f32)
    group = lax.broadcasted_iota(jnp.int32, (32, 128), 1) // 32

    def regroup(source, place):
        total = jnp.zeros((32, 128), f32)
        for kh in range(4):
            kb = place(kh)
            tile, offset = kb // 4, kb % 4
            x = source[tile * 32 : (tile + 1) * 32, :]
            shift = (kh - offset) % 4 * 32
            if shift:
                x = pltpu.roll(x, shift, 1)
            total = jnp.where(group == kh, x, total)
        return total

    for kl in range(8):
        even = regroup(straight, lambda kh: kl + 8 * kh)
        odd = regroup(mirrored, lambda kh: (32 - kl - 8 * kh) % 32)
        moved[pl.ds(kl, 32, stride=8), :] = even
        moved[pl.ds(BLOCK + kl, 32, stride=8), :] = odd
    for ka in range(17):
        other = BLOCK + (32 - ka) % 32 * 8
        sym[ka * 8 : ka * 8 + 8, :] = 0.5 * (
            moved[ka * 8 : ka * 8 + 8, :] + moved[other : other + 8, :]
        )

    for side, face in ((0, 1), (1, 0)):
        halo(side).wait_recv()
        for k in range(6):
            start = HALO + (side * NODES + FACES[face][k]) * 8
            for a in range(8):
                pool[start + a] = halo_in[side, k * 8 + a]

    @pl.loop(0, 8)
    def _(a):
        v0 = grid(me * 8 + a)
        negs = [jnp.minimum(normal_speed(j, v0, v1), 0.0) for j in range(4)]

        @pl.loop(0, ELEMS)
        def _(e):
            for j in range(4):
                side = nb_side[e, j]
                inner = jnp.where(side == 3, 0, 8)
                edge = TABLE + jnp.where(wall_flag[e, j] == 1, inj_id[e, j], 4) * 8
                near = nb_local[e, j] * (NODES * 8)
                far = HALO + jnp.where(side == 2, NODES * 8, 0)
                base = jnp.where(side == 3, edge, jnp.where(side == 0, near, far)) + a
                for k in range(6):
                    outer = pool[base + inner * FACES[j ^ 1][k]]
                    trace = pool[(e * NODES + FACES[j][k]) * 8 + a]
                    diff[j * 6 + k, rows(e * 8), :] = negs[j] * (trace - outer)

        @pl.loop(0, NODES // 2)
        def _(pair):
            acc = [[zero] * ELEMS for _ in range(2)]
            for m in range(NODES):
                for i in range(2):
                    n = pair * 2 + i
                    c = deriv[n, 0, m] * v0 + deriv[n, 1, m] * v1 + deriv[n, 2, m] * v2
                    for e in range(ELEMS):
                        f = pool[(e * NODES + m) * 8 + a]
                        acc[i][e] = acc[i][e] - c * f
            for j in range(4):
                for k in range(6):
                    for i in range(2):
                        c = lift[k, j, pair * 2 + i]
                        for e in range(ELEMS):
                            d = diff[j * 6 + k, e * 8 : e * 8 + 8, :]
                            acc[i][e] = acc[i][e] + c * d
            for i in range(2):
                for e in range(ELEMS):
                    moved[rows((e * NODES + pair * 2 + i) * SLAB + a * 8), :] = acc[i][e]

    cos = twiddle[0:8, :]
    sin = twiddle[8:16, :]

    @pl.loop(0, NODES)
    def _(n):
        for q in range(3):
            forward_in(n, q, block, pool, fwd_send, fwd_recv, partners, rows).wait_recv()
        result[rows(n * BLOCK, BLOCK), :] = collide(
            block[pl.ds(n * 32, 32)].reshape(BLOCK, 128),
            phi[...],
            sym[...],
            rows_fwd[...],
            lanes_fwd[...],
            lanes_bwd[...],
            rows_bwd[...],
            cos,
            sin,
        )
        for q in range(3):
            backward(n, q).start()

    total = sums_out[...]
    for q in range(3):
        sums(q).wait_recv()
    for q in range(3):
        total = total + sums_in[q]
    for j in range(4):
        mask = zero
        for e in range(ELEMS):
            on = jnp.where(nb_side[e, j] == 3, jnp.where(wall_flag[e, j] == 1, 1.0, 0.0), 0.0)
            mask = jnp.where(sub % 4 == e, on, mask)
        den = jnp.broadcast_to(total[:, 24 + j : 25 + j], (8, 128))
        sigma = [
            jnp.broadcast_to(total[:, j * 6 + k : j * 6 + k + 1], (8, 128)) / den * mask
            for k in range(6)
        ]
        for n in range(NODES):
            part = lift[0, j, n] * sigma[0]
            for k in range(1, 6):
                part = part + lift[k, j, n] * sigma[k]
            wallsum[(j * NODES + n) * 8 : (j * NODES + n) * 8 + 8, :] = part

    @pl.loop(0, ELEMS)
    def _(e):
        @pl.loop(0, NODES)
        def _(n):
            parts = [
                jnp.broadcast_to(wallsum[pl.ds((j * NODES + n) * 8 + e, 1), :], (8, 128))
                for j in range(4)
            ]
            for a in range(8):
                x = moved[rows((e * NODES + n) * SLAB + a * 8), :]
                for j in range(4):
                    x = x - parts[j] * negwall[(j * 8 + a) * 8 : (j * 8 + a) * 8 + 8, :]
                moved[rows((e * NODES + n) * SLAB + a * 8), :] = x

    @pl.loop(0, NODES)
    def _(n):
        for a in range(8):
            out[pl.ds(n * BLOCK + a * 32 + me, 8, stride=4), :] = (
                result[rows(n * BLOCK + me * SLAB + a * 8), :]
                + moved[rows((me * NODES + n) * SLAB + a * 8), :]
            )
        for q in range(3):
            backward_in(n, q, back, result, bwd_send, bwd_recv, partners, rows).wait_recv()
            e = partners[q]
            for a in range(8):
                at = rows((e * NODES + n) * SLAB + a * 8)
                out[pl.ds(n * BLOCK + a * 32 + e, 8, stride=4), :] = back[at, :] + moved[at, :]

    @pl.loop(0, NODES)
    def _(n):
        for q in range(3):
            forward(n, q).wait_send()
            backward(n, q).wait_send()

    for side in range(2):
        halo(side).wait_send()
    for q in range(3):
        sums(q).wait_send()


def forward_in(n, q, block, pool, send, recv, partners, rows):
    return pltpu.make_async_remote_copy(
        src_ref=pool.at[pl.ds(0, 8)],
        dst_ref=block.at[pl.ds(n * 32 + partners[q] * 8, 8)],
        send_sem=send.at[n, q],
        recv_sem=recv.at[n, q],
        device_id={"vel": partners[q]},
    )


def backward_in(n, q, back, result, send, recv, partners, rows):
    return pltpu.make_async_remote_copy(
        src_ref=result.at[rows(0, SLAB)],
        dst_ref=back.at[rows((partners[q] * NODES + n) * SLAB, SLAB)],
        send_sem=send.at[n, q],
        recv_sem=recv.at[n, q],
        device_id={"vel": partners[q]},
    )


def solution(mesh):
    space = mesh.shape["space"]
    constants = tables()

    def local(
        dist,
        phi,
        khat,
        deriv,
        lift,
        normals,
        wall_maxw,
        free_stream,
        inject,
        nb_local,
        nb_side,
        wall_flag,
        inj_id,
    ):
        lines = dist.transpose(1, 0, 2).reshape(NODES, ELEMS, SLAB, 128)
        lines = lines.transpose(0, 2, 1, 3).reshape(NODES * BLOCK, 128)
        profiles = inject.reshape(4, SLAB, 128).transpose(1, 0, 2).reshape(BLOCK, 128)
        vmem = pl.BlockSpec(memory_space=pltpu.VMEM)
        smem = pl.BlockSpec(memory_space=pltpu.SMEM)
        f32 = jnp.float32
        dma = pltpu.SemaphoreType.DMA

        def body(*refs):
            kernel(space, *refs)

        rate = pl.pallas_call(
            body,
            out_shape=jax.ShapeDtypeStruct((NODES * BLOCK, 128), f32),
            in_specs=[vmem] * 3 + [smem] * 3 + [vmem] * 3 + [smem] * 4 + [vmem] * 6,
            out_specs=vmem,
            scratch_shapes=[
                pltpu.VMEM((POOL, 8, 128), f32),
                pltpu.VMEM((NODES * 32, 8, 128), f32),
                pltpu.VMEM((NODES * BLOCK, 128), f32),
                pltpu.VMEM((ELEMS * NODES * SLAB, 128), f32),
                pltpu.VMEM((ELEMS * NODES * SLAB, 128), f32),
                pltpu.VMEM((24, ELEMS * 8, 128), f32),
                pltpu.VMEM((4 * SLAB, 128), f32),
                pltpu.VMEM((BLOCK, 128), f32),
                pltpu.VMEM((BLOCK, 128), f32),
                pltpu.VMEM((HALF, 128), f32),
                pltpu.VMEM((4 * NODES * 8, 128), f32),
                pltpu.VMEM((2, 6 * 8, 8, 128), f32),
                pltpu.VMEM((2, 6 * 8, 8, 128), f32),
                pltpu.VMEM((8, 128), f32),
                pltpu.VMEM((3, 8, 128), f32),
                dma((NODES, 3)),
                dma((NODES, 3)),
                dma((NODES, 3)),
                dma((NODES, 3)),
                dma((2,)),
                dma((2,)),
                dma((3,)),
                dma((3,)),
            ],
            compiler_params=pltpu.CompilerParams(
                collective_id=0, has_side_effects=True, vmem_limit_bytes=40 * 2**20
            ),
            name="rate",
        )(
            lines,
            phi.reshape(BLOCK, 128),
            khat,
            deriv.transpose(1, 0, 2),
            lift.transpose(2, 0, 1),
            normals,
            wall_maxw.reshape(SLAB, 128),
            free_stream.reshape(SLAB, 128),
            profiles,
            nb_local,
            nb_side,
            wall_flag,
            inj_id,
            *[jnp.asarray(c) for c in constants],
        )
        rate = rate.reshape(NODES, SLAB, ELEMS, 128).transpose(0, 2, 1, 3)
        return rate.reshape(NODES, ELEMS, SLAB * 128).transpose(1, 0, 2)

    return jax.shard_map(
        local,
        mesh=mesh,
        in_specs=(
            P("space", None, "vel"),
            P(),
            P(),
            P(),
            P(),
            P(),
            P("vel"),
            P("vel"),
            P(None, "vel"),
            P("space", None),
            P("space", None),
            P("space", None),
            P("space", None),
        ),
        out_specs=P("space", None, "vel"),
        check_vma=False,
    )
```

```python
import math

import jax
import jax.numpy as jnp
import numpy as np
import ml_dtypes
from jax import lax
from jax.experimental import pallas as pl
from jax.experimental.pallas import tpu as pltpu
from jax.sharding import PartitionSpec as P

FACES = ((1, 2, 3, 5, 8, 9), (0, 2, 3, 6, 7, 9), (0, 1, 3, 4, 7, 8), (0, 1, 2, 4, 5, 6))
SPEED = 3.0
NODES = 10
ELEMS = 4
GROUP = 4
SLAB = 64
BLOCK = 256
HALF = 136
PACK = 128
TABLE = ELEMS * NODES * 8
HALO = TABLE + 5 * 8
POOL = HALO + 2 * NODES * 8


def split(x):
    hi = x.astype(ml_dtypes.bfloat16)
    lo = (x - hi.astype(np.float64)).astype(ml_dtypes.bfloat16)
    return hi, lo


def tables():
    turn = 2.0 * np.pi
    ka = np.repeat(np.arange(17), 8)
    kl = np.tile(np.arange(8), 17)
    a = np.repeat(np.arange(32), 8)
    bh = np.tile(np.arange(8), 32)
    bl = np.repeat(np.arange(4), 32)
    c = np.tile(np.arange(32), 4)
    angle = turn * ((np.outer(ka, a) % 32) / 32.0 + (np.outer(kl, bh) % 8) / 8.0)
    rows_fwd = np.concatenate([np.cos(angle), -np.sin(angle)], axis=0)
    angle = turn * ((np.outer(bl, bl) % 4) / 4.0 + (np.outer(c, c) % 32) / 32.0)
    co, si = np.cos(angle), np.sin(angle)
    lanes_fwd = np.concatenate(
        [np.concatenate([co, -si], axis=1), np.concatenate([si, co], axis=1)], axis=0
    )
    lanes_bwd = np.concatenate(
        [np.concatenate([co, si], axis=1), np.concatenate([-si, co], axis=1)], axis=0
    )
    angle = turn * ((np.outer(a, ka[:PACK]) % 32) / 32.0 + (np.outer(bh, kl[:PACK]) % 8) / 8.0)
    re, im = 2.0 * np.cos(angle), -2.0 * np.sin(angle)
    sign = np.where(a % 2 == 0, 1.0, -1.0)[:, None]
    angle = turn * ((np.outer(bh, np.arange(8)) % 8) / 8.0)
    re[:, :8] = np.cos(angle) + sign * np.sin(angle)
    im[:, :8] = -np.sin(angle) + sign * np.cos(angle)
    rows_bwd = np.concatenate([re, im], axis=1) * 2.0**-15

    def left(x):
        hi, lo = split(x)
        return np.concatenate([hi, hi, lo], axis=1)

    def right(x):
        hi, lo = split(x)
        return np.concatenate([hi, hi, lo], axis=0)

    angle = turn * np.outer(np.arange(8), bl) / 32.0
    twiddle = np.concatenate([np.cos(angle), np.sin(angle)], axis=0).astype(np.float32)
    lane = np.arange(128)
    mirror = (lane // 32) * 32 + (32 - lane % 32) % 32
    reverse = (lane[:, None] == mirror[None, :]).astype(ml_dtypes.bfloat16)
    return (left(rows_fwd), right(lanes_fwd), right(lanes_bwd), left(rows_bwd), twiddle, reverse)


def halves(x):
    hi = x.astype(jnp.bfloat16)
    lo = (x - hi.astype(jnp.float32)).astype(jnp.bfloat16)
    return hi, lo


def dot_left(table, x):
    hi, lo = halves(x)
    return jnp.dot(
        table, jnp.concatenate([hi, lo, hi], axis=0), preferred_element_type=jnp.float32
    )


def dot_right(x, table):
    hi, lo = halves(x)
    return jnp.dot(
        jnp.concatenate([hi, lo, hi], axis=1), table, preferred_element_type=jnp.float32
    )


def by_rows(x, y):
    return jnp.concatenate([x, y], axis=0)


def by_lanes(x, y):
    return jnp.concatenate([x, y], axis=1)


def turned(re, im, cos, sin):
    count = re.shape[0] // 8
    re = re.reshape(count, 8, 128)
    im = im.reshape(count, 8, 128)
    out_re = re * cos[None] - im * sin[None]
    out_im = re * sin[None] + im * cos[None]
    return out_re.reshape(count * 8, 128), out_im.reshape(count * 8, 128)


def collide(x, phi, sym, rows_fwd, lanes_fwd, lanes_bwd, rows_bwd, cos, sin):
    y = dot_left(rows_fwd, by_lanes(x * phi, x))
    wr, wi = turned(y[:HALF, :128], y[HALF:, :128], cos, -sin)
    fr, fi = turned(y[:HALF, 128:], y[HALF:, 128:], cos, -sin)
    s = dot_right(by_rows(by_lanes(wr, wi), by_lanes(fr, fi)), lanes_fwd)
    wr, wi, fr, fi = s[:HALF, :128], s[:HALF, 128:], s[HALF:, :128], s[HALF:, 128:]
    wr, wi = wr * 2.0**-15, wi * 2.0**-15

    def packed(re, im):
        first = re[:8] - im[PACK:]
        second = im[:8] + re[PACK:]
        return by_lanes(by_rows(first, re[8:PACK]), by_rows(second, im[8:PACK]))

    gain = packed(wr * fr - wi * fi, wr * fi + wi * fr)
    loss = packed(sym * fr, sym * fi)
    b = dot_right(by_rows(gain, loss), lanes_bwd)
    gr, gi = turned(b[:PACK, :128], b[:PACK, 128:], cos, sin)
    lr, li = turned(b[PACK:, :128], b[PACK:, 128:], cos, sin)
    z = dot_left(rows_bwd, by_rows(by_lanes(gr, lr), by_lanes(gi, li)))
    return z[:, :128] - x * z[:, 128:]


def kernel(
    space,
    dist_in,
    phi_in,
    khat_in,
    wall_in,
    free_in,
    inject_in,
    rows_fwd_in,
    lanes_fwd_in,
    lanes_bwd_in,
    rows_bwd_in,
    twiddle_in,
    reverse_in,
    deriv_in,
    lift_in,
    normals_in,
    nb_local_in,
    nb_side_in,
    wall_flag_in,
    inj_id_in,
    out,
    dist,
    phi,
    khat,
    wall,
    free,
    inject,
    rows_fwd,
    lanes_fwd,
    lanes_bwd,
    rows_bwd,
    twiddle,
    reverse,
    deriv,
    lift,
    normals,
    nb_local,
    nb_side,
    wall_flag,
    inj_id,
    pool,
    block,
    result,
    back,
    moved,
    diff,
    negwall,
    straight,
    mirrored,
    sym,
    wallsum,
    halo_out,
    halo_in,
    sums_out,
    sums_in,
    dist_sem,
    load_sem,
    fwd_send,
    fwd_recv,
    bwd_send,
    bwd_recv,
    halo_send,
    halo_recv,
    sums_send,
    sums_recv,
):
    f32 = jnp.float32
    me = lax.axis_index("vel")
    here = lax.axis_index("space")
    above = lax.rem(here + 1, space)
    below = lax.rem(here + space - 1, space)
    core = lax.rem(me, 2)
    flip = 1 - 2 * core
    across = lax.rem(me + 2, GROUP)
    partners = (across, across + flip, me + flip)

    def rows(start, count=8):
        return pl.ds(pl.multiple_of(start, 8), count)

    def forward(n, q):
        to = partners[q]
        return pltpu.make_async_remote_copy(
            src_ref=pool.at[pl.ds((to * NODES + n) * 8, 8)],
            dst_ref=block.at[pl.ds(n * 32 + me * 8, 8)],
            send_sem=fwd_send.at[n, q],
            recv_sem=fwd_recv.at[n, q],
            device_id={"vel": to},
        )

    def backward(n, q):
        to = partners[q]
        return pltpu.make_async_remote_copy(
            src_ref=result.at[rows(n * BLOCK + to * SLAB, SLAB)],
            dst_ref=back.at[rows((me * NODES + n) * SLAB, SLAB)],
            send_sem=bwd_send.at[n, q],
            recv_sem=bwd_recv.at[n, q],
            device_id={"vel": to},
        )

    def halo(side):
        return pltpu.make_async_remote_copy(
            src_ref=halo_out.at[side],
            dst_ref=halo_in.at[side],
            send_sem=halo_send.at[side],
            recv_sem=halo_recv.at[side],
            device_id={"space": below if side else above},
        )

    def sums(q):
        return pltpu.make_async_remote_copy(
            src_ref=sums_out,
            dst_ref=sums_in.at[q],
            send_sem=sums_send.at[q],
            recv_sem=sums_recv.at[q],
            device_id={"vel": partners[q]},
        )

    def dist_load(n):
        part = rows(n * BLOCK, BLOCK)
        return pltpu.make_async_copy(dist_in.at[part], dist.at[part], dist_sem.at[n])

    pairs = (
        (nb_side_in, nb_side),
        (inject_in, inject),
        (free_in, free),
        (normals_in, normals),
        (wall_in, wall),
        (khat_in, khat),
        (reverse_in, reverse),
        (nb_local_in, nb_local),
        (wall_flag_in, wall_flag),
        (inj_id_in, inj_id),
        (deriv_in, deriv),
        (lift_in, lift),
        (phi_in, phi),
        (rows_fwd_in, rows_fwd),
        (lanes_fwd_in, lanes_fwd),
        (twiddle_in, twiddle),
        (lanes_bwd_in, lanes_bwd),
        (rows_bwd_in, rows_bwd),
    )
    loads = [
        pltpu.make_async_copy(source, target, load_sem.at[i])
        for i, (source, target) in enumerate(pairs)
    ]

    barrier = pltpu.get_barrier_semaphore()
    for to in partners:
        pl.semaphore_signal(barrier, inc=1, device_id={"vel": to})
    for to in (above, below):
        pl.semaphore_signal(barrier, inc=1, device_id={"space": to})
    for n in range(NODES):
        dist_load(n).start()
    for load in loads:
        load.start()
    pl.semaphore_wait(barrier, 5)

    @pl.loop(0, NODES)
    def _(n):
        dist_load(n).wait()
        for e in range(ELEMS):
            for a in range(8):
                pool[(e * NODES + n) * 8 + a] = dist[
                    pl.ds(n * BLOCK + a * 32 + e, 8, stride=4), :
                ]
        for q in range(3):
            forward(n, q).start()
        for a in range(8):
            block[n * 32 + me * 8 + a] = pool[(me * NODES + n) * 8 + a]

    for load in loads:
        load.wait()

    up_elem = jnp.int32(0)
    down_elem = jnp.int32(0)
    for e in range(ELEMS):
        up_elem = up_elem + jnp.where(nb_side[e, 1] == 2, e, 0)
        down_elem = down_elem + jnp.where(nb_side[e, 0] == 1, e, 0)
    for side, elem, face in ((0, up_elem, 1), (1, down_elem, 0)):
        for k in range(6):
            for a in range(8):
                halo_out[side, k * 8 + a] = pool[(elem * NODES + FACES[face][k]) * 8 + a]
        halo(side).start()

    for q in range(4):
        for a in range(8):
            pool[TABLE + q * 8 + a] = inject[pl.ds(a * 32 + q, 8, stride=4), :]
    for a in range(8):
        pool[TABLE + 32 + a] = free[a * 8 : a * 8 + 8, :]

    sub = lax.broadcasted_iota(jnp.int32, (8, 128), 0)
    lane = lax.broadcasted_iota(jnp.int32, (8, 128), 1)

    def grid(i):
        return SPEED * ((2.0 * i.astype(f32) + 1.0) / 32.0 - 1.0)

    v2 = grid(lane % 32)
    v1 = grid(sub * 4 + lane // 32)

    def normal_speed(j, v0, v1):
        return normals[j, 0] * v0 + normals[j, 1] * v1 + normals[j, 2] * v2

    def partial_sums(i, carry):
        a = i // 4
        v0 = grid(me * 8 + a)
        b = (lax.rem(i, 4) * 2 + sub // 4) * 4 + lane // 32
        got = [dist[rows(n * BLOCK + i * 8), :] for n in range(NODES)]
        new = []
        for j in range(4):
            pos = jnp.maximum(normal_speed(j, v0, grid(b)), 0.0)
            for k in range(6):
                new.append(carry[j * 6 + k] + pos * got[FACES[j][k]])
        return tuple(new)

    zero = jnp.zeros((8, 128), f32)
    nums = lax.fori_loop(0, 32, partial_sums, (zero,) * 24)

    def partial_dens(a, carry):
        v0 = grid(me * 8 + a)
        new = []
        for j in range(4):
            value = jnp.minimum(normal_speed(j, v0, v1), 0.0) * wall[rows(a * 8), :]
            negwall[rows((j * 8 + a) * 8), :] = value
            new.append(carry[j] - value)
        return tuple(new)

    dens = lax.fori_loop(0, 8, partial_dens, (zero,) * 4)
    mine = zero
    for i, x in enumerate(nums):
        x = x + pltpu.roll(x, 4, 0)
        mine = jnp.where(lane == i, jnp.sum(x, axis=1, keepdims=True), mine)
    for j, x in enumerate(dens):
        x = jnp.broadcast_to(jnp.sum(x, axis=0, keepdims=True), (8, 128))
        mine = jnp.where(lane == 24 + j, jnp.sum(x, axis=1, keepdims=True), mine)
    sums_out[...] = mine
    for q in range(3):
        sums(q).start()

    for i in range(8):
        x = khat[:, i * 128 : (i + 1) * 128]
        straight[i * 32 : (i + 1) * 32, :] = x
    x = straight[...]
    x0 = x.astype(jnp.bfloat16)
    x = x - x0.astype(f32)
    x1 = x.astype(jnp.bfloat16)
    x2 = (x - x1.astype(f32)).astype(jnp.bfloat16)
    rev = reverse[...]
    mirrored[...] = (
        jnp.dot(x0, rev, preferred_element_type=f32) + jnp.dot(x1, rev, preferred_element_type=f32)
    ) + jnp.dot(x2, rev, preferred_element_type=f32)
    group = lax.broadcasted_iota(jnp.int32, (32, 128), 1) // 32

    def regroup(source, place):
        total = jnp.zeros((32, 128), f32)
        for kh in range(4):
            kb = place(kh)
            tile, offset = kb // 4, kb % 4
            x = source[tile * 32 : (tile + 1) * 32, :]
            shift = (kh - offset) % 4 * 32
            if shift:
                x = pltpu.roll(x, shift, 1)
            total = jnp.where(group == kh, x, total)
        return total

    for kl in range(8):
        even = regroup(straight, lambda kh: kl + 8 * kh)
        odd = regroup(mirrored, lambda kh: (32 - kl - 8 * kh) % 32)
        moved[pl.ds(kl, 32, stride=8), :] = even
        moved[pl.ds(BLOCK + kl, 32, stride=8), :] = odd
    for ka in range(17):
        other = BLOCK + (32 - ka) % 32 * 8
        sym[ka * 8 : ka * 8 + 8, :] = 0.5 * (
            moved[ka * 8 : ka * 8 + 8, :] + moved[other : other + 8, :]
        )

    for side, face in ((0, 1), (1, 0)):
        halo(side).wait_recv()
        for k in range(6):
            start = HALO + (side * NODES + FACES[face][k]) * 8
            for a in range(8):
                pool[start + a] = halo_in[side, k * 8 + a]

    @pl.loop(0, 8)
    def _(a):
        v0 = grid(me * 8 + a)
        negs = [jnp.minimum(normal_speed(j, v0, v1), 0.0) for j in range(4)]

        @pl.loop(0, ELEMS)
        def _(e):
            for j in range(4):
                side = nb_side[e, j]
                inner = jnp.where(side == 3, 0, 8)
                edge = TABLE + jnp.where(wall_flag[e, j] == 1, inj_id[e, j], 4) * 8
                near = nb_local[e, j] * (NODES * 8)
                far = HALO + jnp.where(side == 2, NODES * 8, 0)
                base = jnp.where(side == 3, edge, jnp.where(side == 0, near, far)) + a
                for k in range(6):
                    outer = pool[base + inner * FACES[j ^ 1][k]]
                    trace = pool[(e * NODES + FACES[j][k]) * 8 + a]
                    diff[j * 6 + k, rows(e * 8), :] = negs[j] * (trace - outer)

        @pl.loop(0, NODES // 2)
        def _(pair):
            acc = [[zero] * ELEMS for _ in range(2)]
            for m in range(NODES):
                for i in range(2):
                    n = pair * 2 + i
                    c = deriv[n, 0, m] * v0 + deriv[n, 1, m] * v1 + deriv[n, 2, m] * v2
                    for e in range(ELEMS):
                        f = pool[(e * NODES + m) * 8 + a]
                        acc[i][e] = acc[i][e] - c * f
            for j in range(4):
                for k in range(6):
                    for i in range(2):
                        c = lift[k, j, pair * 2 + i]
                        for e in range(ELEMS):
                            d = diff[j * 6 + k, e * 8 : e * 8 + 8, :]
                            acc[i][e] = acc[i][e] + c * d
            for i in range(2):
                for e in range(ELEMS):
                    moved[rows((e * NODES + pair * 2 + i) * SLAB + a * 8), :] = acc[i][e]

    cos = twiddle[0:8, :]
    sin = twiddle[8:16, :]

    @pl.loop(0, NODES)
    def _(n):
        for q in range(3):
            forward_in(n, q, block, pool, fwd_send, fwd_recv, partners, rows).wait_recv()
        result[rows(n * BLOCK, BLOCK), :] = collide(
            block[pl.ds(n * 32, 32)].reshape(BLOCK, 128),
            phi[...],
            sym[...],
            rows_fwd[...],
            lanes_fwd[...],
            lanes_bwd[...],
            rows_bwd[...],
            cos,
            sin,
        )
        for q in range(3):
            backward(n, q).start()

    total = sums_out[...]
    for q in range(3):
        sums(q).wait_recv()
    for q in range(3):
        total = total + sums_in[q]
    for j in range(4):
        mask = zero
        for e in range(ELEMS):
            on = jnp.where(nb_side[e, j] == 3, jnp.where(wall_flag[e, j] == 1, 1.0, 0.0), 0.0)
            mask = jnp.where(sub % 4 == e, on, mask)
        den = jnp.broadcast_to(total[:, 24 + j : 25 + j], (8, 128))
        sigma = [
            jnp.broadcast_to(total[:, j * 6 + k : j * 6 + k + 1], (8, 128)) / den * mask
            for k in range(6)
        ]
        for n in range(NODES):
            part = lift[0, j, n] * sigma[0]
            for k in range(1, 6):
                part = part + lift[k, j, n] * sigma[k]
            wallsum[(j * NODES + n) * 8 : (j * NODES + n) * 8 + 8, :] = part

    @pl.loop(0, ELEMS)
    def _(e):
        @pl.loop(0, NODES)
        def _(n):
            parts = [
                jnp.broadcast_to(wallsum[pl.ds((j * NODES + n) * 8 + e, 1), :], (8, 128))
                for j in range(4)
            ]
            for a in range(8):
                x = moved[rows((e * NODES + n) * SLAB + a * 8), :]
                for j in range(4):
                    x = x - parts[j] * negwall[(j * 8 + a) * 8 : (j * 8 + a) * 8 + 8, :]
                moved[rows((e * NODES + n) * SLAB + a * 8), :] = x

    @pl.loop(0, NODES)
    def _(n):
        for a in range(8):
            out[pl.ds(n * BLOCK + a * 32 + me, 8, stride=4), :] = (
                result[rows(n * BLOCK + me * SLAB + a * 8), :]
                + moved[rows((me * NODES + n) * SLAB + a * 8), :]
            )
        for q in range(3):
            backward_in(n, q, back, result, bwd_send, bwd_recv, partners, rows).wait_recv()
            e = partners[q]
            for a in range(8):
                at = rows((e * NODES + n) * SLAB + a * 8)
                out[pl.ds(n * BLOCK + a * 32 + e, 8, stride=4), :] = back[at, :] + moved[at, :]

    @pl.loop(0, NODES)
    def _(n):
        for q in range(3):
            forward(n, q).wait_send()
            backward(n, q).wait_send()

    for side in range(2):
        halo(side).wait_send()
    for q in range(3):
        sums(q).wait_send()


def forward_in(n, q, block, pool, send, recv, partners, rows):
    return pltpu.make_async_remote_copy(
        src_ref=pool.at[pl.ds(0, 8)],
        dst_ref=block.at[pl.ds(n * 32 + partners[q] * 8, 8)],
        send_sem=send.at[n, q],
        recv_sem=recv.at[n, q],
        device_id={"vel": partners[q]},
    )


def backward_in(n, q, back, result, send, recv, partners, rows):
    return pltpu.make_async_remote_copy(
        src_ref=result.at[rows(0, SLAB)],
        dst_ref=back.at[rows((partners[q] * NODES + n) * SLAB, SLAB)],
        send_sem=send.at[n, q],
        recv_sem=recv.at[n, q],
        device_id={"vel": partners[q]},
    )


def solution(mesh):
    space = mesh.shape["space"]
    constants = tables()

    def local(
        dist,
        phi,
        khat,
        deriv,
        lift,
        normals,
        wall_maxw,
        free_stream,
        inject,
        nb_local,
        nb_side,
        wall_flag,
        inj_id,
    ):
        lines = dist.transpose(1, 0, 2).reshape(NODES, ELEMS, SLAB, 128)
        lines = lines.transpose(0, 2, 1, 3).reshape(NODES * BLOCK, 128)
        profiles = inject.reshape(4, SLAB, 128).transpose(1, 0, 2).reshape(BLOCK, 128)
        vmem = pl.BlockSpec(memory_space=pltpu.VMEM)
        hbm = pl.BlockSpec(memory_space=pltpu.HBM)
        f32 = jnp.float32
        dma = pltpu.SemaphoreType.DMA

        tables = [jnp.asarray(c) for c in constants]
        operands = [
            lines,
            phi.reshape(BLOCK, 128),
            khat,
            wall_maxw.reshape(SLAB, 128),
            free_stream.reshape(SLAB, 128),
            profiles,
            *tables,
            deriv.transpose(1, 0, 2),
            lift.transpose(2, 0, 1),
            normals,
            nb_local,
            nb_side,
            wall_flag,
            inj_id,
        ]

        def body(*refs):
            kernel(space, *refs)

        rate = pl.pallas_call(
            body,
            out_shape=jax.ShapeDtypeStruct((NODES * BLOCK, 128), f32),
            in_specs=[hbm] * len(operands),
            out_specs=vmem,
            scratch_shapes=[pltpu.VMEM(x.shape, x.dtype) for x in operands[:12]]
            + [pltpu.SMEM(x.shape, x.dtype) for x in operands[12:]]
            + [
                pltpu.VMEM((POOL, 8, 128), f32),
                pltpu.VMEM((NODES * 32, 8, 128), f32),
                pltpu.VMEM((NODES * BLOCK, 128), f32),
                pltpu.VMEM((ELEMS * NODES * SLAB, 128), f32),
                pltpu.VMEM((ELEMS * NODES * SLAB, 128), f32),
                pltpu.VMEM((24, ELEMS * 8, 128), f32),
                pltpu.VMEM((4 * SLAB, 128), f32),
                pltpu.VMEM((BLOCK, 128), f32),
                pltpu.VMEM((BLOCK, 128), f32),
                pltpu.VMEM((HALF, 128), f32),
                pltpu.VMEM((4 * NODES * 8, 128), f32),
                pltpu.VMEM((2, 6 * 8, 8, 128), f32),
                pltpu.VMEM((2, 6 * 8, 8, 128), f32),
                pltpu.VMEM((8, 128), f32),
                pltpu.VMEM((3, 8, 128), f32),
                dma((NODES,)),
                dma((len(operands) - 1,)),
                dma((NODES, 3)),
                dma((NODES, 3)),
                dma((NODES, 3)),
                dma((NODES, 3)),
                dma((2,)),
                dma((2,)),
                dma((3,)),
                dma((3,)),
            ],
            compiler_params=pltpu.CompilerParams(
                collective_id=0, has_side_effects=True, vmem_limit_bytes=40 * 2**20
            ),
            name="rate",
        )(*operands)
        rate = rate.reshape(NODES, SLAB, ELEMS, 128).transpose(0, 2, 1, 3)
        return rate.reshape(NODES, ELEMS, SLAB * 128).transpose(1, 0, 2)

    return jax.shard_map(
        local,
        mesh=mesh,
        in_specs=(
            P("space", None, "vel"),
            P(),
            P(),
            P(),
            P(),
            P(),
            P("vel"),
            P("vel"),
            P(None, "vel"),
            P("space", None),
            P("space", None),
            P("space", None),
            P("space", None),
        ),
        out_specs=P("space", None, "vel"),
        check_vma=False,
    )
```

```python
import math

import jax
import jax.numpy as jnp
import numpy as np
import ml_dtypes
from jax import lax
from jax.experimental import pallas as pl
from jax.experimental.pallas import tpu as pltpu
from jax.sharding import PartitionSpec as P

FACES = ((1, 2, 3, 5, 8, 9), (0, 2, 3, 6, 7, 9), (0, 1, 3, 4, 7, 8), (0, 1, 2, 4, 5, 6))
SPEED = 3.0
NODES = 10
ELEMS = 4
GROUP = 4
SLAB = 64
BLOCK = 256
HALF = 136
PACK = 128
TABLE = ELEMS * NODES * 8
HALO = TABLE + 5 * 8
POOL = HALO + 2 * NODES * 8


def split(x):
    hi = x.astype(ml_dtypes.bfloat16)
    lo = (x - hi.astype(np.float64)).astype(ml_dtypes.bfloat16)
    return hi, lo


def tables():
    turn = 2.0 * np.pi
    ka = np.repeat(np.arange(17), 8)
    kl = np.tile(np.arange(8), 17)
    a = np.repeat(np.arange(32), 8)
    bh = np.tile(np.arange(8), 32)
    bl = np.repeat(np.arange(4), 32)
    c = np.tile(np.arange(32), 4)
    angle = turn * ((np.outer(ka, a) % 32) / 32.0 + (np.outer(kl, bh) % 8) / 8.0)
    rows_fwd = np.concatenate([np.cos(angle), -np.sin(angle)], axis=0)
    angle = turn * ((np.outer(bl, bl) % 4) / 4.0 + (np.outer(c, c) % 32) / 32.0)
    co, si = np.cos(angle), np.sin(angle)
    lanes_fwd = np.concatenate(
        [np.concatenate([co, -si], axis=1), np.concatenate([si, co], axis=1)], axis=0
    )
    lanes_bwd = np.concatenate(
        [np.concatenate([co, si], axis=1), np.concatenate([-si, co], axis=1)], axis=0
    )
    angle = turn * ((np.outer(a, ka[:PACK]) % 32) / 32.0 + (np.outer(bh, kl[:PACK]) % 8) / 8.0)
    re, im = 2.0 * np.cos(angle), -2.0 * np.sin(angle)
    sign = np.where(a % 2 == 0, 1.0, -1.0)[:, None]
    angle = turn * ((np.outer(bh, np.arange(8)) % 8) / 8.0)
    re[:, :8] = np.cos(angle) + sign * np.sin(angle)
    im[:, :8] = -np.sin(angle) + sign * np.cos(angle)
    rows_bwd = np.concatenate([re, im], axis=1) * 2.0**-15

    def left(x):
        hi, lo = split(x)
        return np.concatenate([hi, hi, lo], axis=1)

    def right(x):
        hi, lo = split(x)
        return np.concatenate([hi, hi, lo], axis=0)

    angle = turn * np.outer(np.arange(8), bl) / 32.0
    twiddle = np.concatenate([np.cos(angle), np.sin(angle)], axis=0).astype(np.float32)
    lane = np.arange(128)
    mirror = (lane // 32) * 32 + (32 - lane % 32) % 32
    reverse = (lane[:, None] == mirror[None, :]).astype(ml_dtypes.bfloat16)
    return (left(rows_fwd), right(lanes_fwd), right(lanes_bwd), left(rows_bwd), twiddle, reverse)


def halves(x):
    hi = x.astype(jnp.bfloat16)
    lo = (x - hi.astype(jnp.float32)).astype(jnp.bfloat16)
    return hi, lo


def dot_left(table, x):
    hi, lo = halves(x)
    return jnp.dot(
        table, jnp.concatenate([hi, lo, hi], axis=0), preferred_element_type=jnp.float32
    )


def dot_right(x, table):
    hi, lo = halves(x)
    return jnp.dot(
        jnp.concatenate([hi, lo, hi], axis=1), table, preferred_element_type=jnp.float32
    )


def by_rows(x, y):
    return jnp.concatenate([x, y], axis=0)


def by_lanes(x, y):
    return jnp.concatenate([x, y], axis=1)


def turned(re, im, cos, sin):
    count = re.shape[0] // 8
    re = re.reshape(count, 8, 128)
    im = im.reshape(count, 8, 128)
    out_re = re * cos[None] - im * sin[None]
    out_im = re * sin[None] + im * cos[None]
    return out_re.reshape(count * 8, 128), out_im.reshape(count * 8, 128)


def collide(x, phi, sym, rows_fwd, lanes_fwd, lanes_bwd, rows_bwd, cos, sin):
    y = dot_left(rows_fwd, by_lanes(x * phi, x))
    wr, wi = turned(y[:HALF, :128], y[HALF:, :128], cos, -sin)
    fr, fi = turned(y[:HALF, 128:], y[HALF:, 128:], cos, -sin)
    s = dot_right(by_rows(by_lanes(wr, wi), by_lanes(fr, fi)), lanes_fwd)
    wr, wi, fr, fi = s[:HALF, :128], s[:HALF, 128:], s[HALF:, :128], s[HALF:, 128:]
    wr, wi = wr * 2.0**-15, wi * 2.0**-15

    def packed(re, im):
        first = re[:8] - im[PACK:]
        second = im[:8] + re[PACK:]
        return by_lanes(by_rows(first, re[8:PACK]), by_rows(second, im[8:PACK]))

    gain = packed(wr * fr - wi * fi, wr * fi + wi * fr)
    loss = packed(sym * fr, sym * fi)
    b = dot_right(by_rows(gain, loss), lanes_bwd)
    gr, gi = turned(b[:PACK, :128], b[:PACK, 128:], cos, sin)
    lr, li = turned(b[PACK:, :128], b[PACK:, 128:], cos, sin)
    z = dot_left(rows_bwd, by_rows(by_lanes(gr, lr), by_lanes(gi, li)))
    return z[:, :128] - x * z[:, 128:]


def kernel(
    space,
    dist_in,
    phi_in,
    khat_in,
    wall_in,
    free_in,
    inject_in,
    rows_fwd_in,
    lanes_fwd_in,
    lanes_bwd_in,
    rows_bwd_in,
    twiddle_in,
    reverse_in,
    deriv_in,
    lift_in,
    normals_in,
    nb_local_in,
    nb_side_in,
    wall_flag_in,
    inj_id_in,
    out_hbm,
    out,
    dist,
    phi,
    khat,
    wall,
    free,
    inject,
    rows_fwd,
    lanes_fwd,
    lanes_bwd,
    rows_bwd,
    twiddle,
    reverse,
    deriv,
    lift,
    normals,
    nb_local,
    nb_side,
    wall_flag,
    inj_id,
    pool,
    block,
    result,
    back,
    moved,
    diff,
    negwall,
    straight,
    mirrored,
    sym,
    wallsum,
    halo_out,
    halo_in,
    sums_out,
    sums_in,
    dist_sem,
    out_sem,
    load_sem,
    fwd_send,
    fwd_recv,
    bwd_send,
    bwd_recv,
    halo_send,
    halo_recv,
    sums_send,
    sums_recv,
):
    f32 = jnp.float32
    me = lax.axis_index("vel")
    here = lax.axis_index("space")
    above = lax.rem(here + 1, space)
    below = lax.rem(here + space - 1, space)
    core = lax.rem(me, 2)
    flip = 1 - 2 * core
    across = lax.rem(me + 2, GROUP)
    partners = (across, across + flip, me + flip)

    def rows(start, count=8):
        return pl.ds(pl.multiple_of(start, 8), count)

    def forward(n, q):
        to = partners[q]
        return pltpu.make_async_remote_copy(
            src_ref=pool.at[pl.ds((to * NODES + n) * 8, 8)],
            dst_ref=block.at[pl.ds(n * 32 + me * 8, 8)],
            send_sem=fwd_send.at[n, q],
            recv_sem=fwd_recv.at[n, q],
            device_id={"vel": to},
        )

    def backward(n, q):
        to = partners[q]
        return pltpu.make_async_remote_copy(
            src_ref=result.at[rows(n * BLOCK + to * SLAB, SLAB)],
            dst_ref=back.at[rows((me * NODES + n) * SLAB, SLAB)],
            send_sem=bwd_send.at[n, q],
            recv_sem=bwd_recv.at[n, q],
            device_id={"vel": to},
        )

    def halo(side):
        return pltpu.make_async_remote_copy(
            src_ref=halo_out.at[side],
            dst_ref=halo_in.at[side],
            send_sem=halo_send.at[side],
            recv_sem=halo_recv.at[side],
            device_id={"space": below if side else above},
        )

    def sums(q):
        return pltpu.make_async_remote_copy(
            src_ref=sums_out,
            dst_ref=sums_in.at[q],
            send_sem=sums_send.at[q],
            recv_sem=sums_recv.at[q],
            device_id={"vel": partners[q]},
        )

    def dist_load(n):
        part = rows(n * BLOCK, BLOCK)
        return pltpu.make_async_copy(dist_in.at[part], dist.at[part], dist_sem.at[n])

    def store(n):
        part = rows(n * BLOCK, BLOCK)
        return pltpu.make_async_copy(out.at[part], out_hbm.at[part], out_sem.at[n])

    pairs = (
        (nb_side_in, nb_side),
        (inject_in, inject),
        (free_in, free),
        (normals_in, normals),
        (wall_in, wall),
        (khat_in, khat),
        (reverse_in, reverse),
        (nb_local_in, nb_local),
        (wall_flag_in, wall_flag),
        (inj_id_in, inj_id),
        (deriv_in, deriv),
        (lift_in, lift),
        (phi_in, phi),
        (rows_fwd_in, rows_fwd),
        (lanes_fwd_in, lanes_fwd),
        (twiddle_in, twiddle),
        (lanes_bwd_in, lanes_bwd),
        (rows_bwd_in, rows_bwd),
    )
    loads = [
        pltpu.make_async_copy(source, target, load_sem.at[i])
        for i, (source, target) in enumerate(pairs)
    ]

    barrier = pltpu.get_barrier_semaphore()
    for to in partners:
        pl.semaphore_signal(barrier, inc=1, device_id={"vel": to})
    for to in (above, below):
        pl.semaphore_signal(barrier, inc=1, device_id={"space": to})
    for n in range(NODES):
        dist_load(n).start()
    for load in loads:
        load.start()
    pl.semaphore_wait(barrier, 5)

    @pl.loop(0, NODES)
    def _(n):
        dist_load(n).wait()
        for e in range(ELEMS):
            for a in range(8):
                pool[(e * NODES + n) * 8 + a] = dist[
                    pl.ds(n * BLOCK + a * 32 + e, 8, stride=4), :
                ]
        for q in range(3):
            forward(n, q).start()
        for a in range(8):
            block[n * 32 + me * 8 + a] = pool[(me * NODES + n) * 8 + a]

    for load in loads:
        load.wait()

    up_elem = jnp.int32(0)
    down_elem = jnp.int32(0)
    for e in range(ELEMS):
        up_elem = up_elem + jnp.where(nb_side[e, 1] == 2, e, 0)
        down_elem = down_elem + jnp.where(nb_side[e, 0] == 1, e, 0)
    for side, elem, face in ((0, up_elem, 1), (1, down_elem, 0)):
        for k in range(6):
            for a in range(8):
                halo_out[side, k * 8 + a] = pool[(elem * NODES + FACES[face][k]) * 8 + a]
        halo(side).start()

    for q in range(4):
        for a in range(8):
            pool[TABLE + q * 8 + a] = inject[pl.ds(a * 32 + q, 8, stride=4), :]
    for a in range(8):
        pool[TABLE + 32 + a] = free[a * 8 : a * 8 + 8, :]

    sub = lax.broadcasted_iota(jnp.int32, (8, 128), 0)
    lane = lax.broadcasted_iota(jnp.int32, (8, 128), 1)

    def grid(i):
        return SPEED * ((2.0 * i.astype(f32) + 1.0) / 32.0 - 1.0)

    v2 = grid(lane % 32)
    v1 = grid(sub * 4 + lane // 32)

    def normal_speed(j, v0, v1):
        return normals[j, 0] * v0 + normals[j, 1] * v1 + normals[j, 2] * v2

    def partial_sums(i, carry):
        a = i // 4
        v0 = grid(me * 8 + a)
        b = (lax.rem(i, 4) * 2 + sub // 4) * 4 + lane // 32
        got = [dist[rows(n * BLOCK + i * 8), :] for n in range(NODES)]
        new = []
        for j in range(4):
            pos = jnp.maximum(normal_speed(j, v0, grid(b)), 0.0)
            for k in range(6):
                new.append(carry[j * 6 + k] + pos * got[FACES[j][k]])
        return tuple(new)

    zero = jnp.zeros((8, 128), f32)
    nums = lax.fori_loop(0, 32, partial_sums, (zero,) * 24)

    def partial_dens(a, carry):
        v0 = grid(me * 8 + a)
        new = []
        for j in range(4):
            value = jnp.minimum(normal_speed(j, v0, v1), 0.0) * wall[rows(a * 8), :]
            negwall[rows((j * 8 + a) * 8), :] = value
            new.append(carry[j] - value)
        return tuple(new)

    dens = lax.fori_loop(0, 8, partial_dens, (zero,) * 4)
    mine = zero
    for i, x in enumerate(nums):
        x = x + pltpu.roll(x, 4, 0)
        mine = jnp.where(lane == i, jnp.sum(x, axis=1, keepdims=True), mine)
    for j, x in enumerate(dens):
        x = jnp.broadcast_to(jnp.sum(x, axis=0, keepdims=True), (8, 128))
        mine = jnp.where(lane == 24 + j, jnp.sum(x, axis=1, keepdims=True), mine)
    sums_out[...] = mine
    for q in range(3):
        sums(q).start()

    for i in range(8):
        x = khat[:, i * 128 : (i + 1) * 128]
        straight[i * 32 : (i + 1) * 32, :] = x
    x = straight[...]
    x0 = x.astype(jnp.bfloat16)
    x = x - x0.astype(f32)
    x1 = x.astype(jnp.bfloat16)
    x2 = (x - x1.astype(f32)).astype(jnp.bfloat16)
    rev = reverse[...]
    mirrored[...] = (
        jnp.dot(x0, rev, preferred_element_type=f32) + jnp.dot(x1, rev, preferred_element_type=f32)
    ) + jnp.dot(x2, rev, preferred_element_type=f32)
    group = lax.broadcasted_iota(jnp.int32, (32, 128), 1) // 32

    def regroup(source, place):
        total = jnp.zeros((32, 128), f32)
        for kh in range(4):
            kb = place(kh)
            tile, offset = kb // 4, kb % 4
            x = source[tile * 32 : (tile + 1) * 32, :]
            shift = (kh - offset) % 4 * 32
            if shift:
                x = pltpu.roll(x, shift, 1)
            total = jnp.where(group == kh, x, total)
        return total

    for kl in range(8):
        even = regroup(straight, lambda kh: kl + 8 * kh)
        odd = regroup(mirrored, lambda kh: (32 - kl - 8 * kh) % 32)
        moved[pl.ds(kl, 32, stride=8), :] = even
        moved[pl.ds(BLOCK + kl, 32, stride=8), :] = odd
    for ka in range(17):
        other = BLOCK + (32 - ka) % 32 * 8
        sym[ka * 8 : ka * 8 + 8, :] = 0.5 * (
            moved[ka * 8 : ka * 8 + 8, :] + moved[other : other + 8, :]
        )

    for side, face in ((0, 1), (1, 0)):
        halo(side).wait_recv()
        for k in range(6):
            start = HALO + (side * NODES + FACES[face][k]) * 8
            for a in range(8):
                pool[start + a] = halo_in[side, k * 8 + a]

    @pl.loop(0, 8)
    def _(a):
        v0 = grid(me * 8 + a)
        negs = [jnp.minimum(normal_speed(j, v0, v1), 0.0) for j in range(4)]

        @pl.loop(0, ELEMS)
        def _(e):
            for j in range(4):
                side = nb_side[e, j]
                inner = jnp.where(side == 3, 0, 8)
                edge = TABLE + jnp.where(wall_flag[e, j] == 1, inj_id[e, j], 4) * 8
                near = nb_local[e, j] * (NODES * 8)
                far = HALO + jnp.where(side == 2, NODES * 8, 0)
                base = jnp.where(side == 3, edge, jnp.where(side == 0, near, far)) + a
                for k in range(6):
                    outer = pool[base + inner * FACES[j ^ 1][k]]
                    trace = pool[(e * NODES + FACES[j][k]) * 8 + a]
                    diff[j * 6 + k, rows(e * 8), :] = negs[j] * (trace - outer)

        @pl.loop(0, NODES // 2)
        def _(pair):
            acc = [[zero] * ELEMS for _ in range(2)]
            for m in range(NODES):
                for i in range(2):
                    n = pair * 2 + i
                    c = deriv[n, 0, m] * v0 + deriv[n, 1, m] * v1 + deriv[n, 2, m] * v2
                    for e in range(ELEMS):
                        f = pool[(e * NODES + m) * 8 + a]
                        acc[i][e] = acc[i][e] - c * f
            for j in range(4):
                for k in range(6):
                    for i in range(2):
                        c = lift[k, j, pair * 2 + i]
                        for e in range(ELEMS):
                            d = diff[j * 6 + k, e * 8 : e * 8 + 8, :]
                            acc[i][e] = acc[i][e] + c * d
            for i in range(2):
                for e in range(ELEMS):
                    moved[rows((e * NODES + pair * 2 + i) * SLAB + a * 8), :] = acc[i][e]

    cos = twiddle[0:8, :]
    sin = twiddle[8:16, :]

    @pl.loop(0, NODES)
    def _(n):
        for q in range(3):
            forward_in(n, q, block, pool, fwd_send, fwd_recv, partners, rows).wait_recv()
        result[rows(n * BLOCK, BLOCK), :] = collide(
            block[pl.ds(n * 32, 32)].reshape(BLOCK, 128),
            phi[...],
            sym[...],
            rows_fwd[...],
            lanes_fwd[...],
            lanes_bwd[...],
            rows_bwd[...],
            cos,
            sin,
        )
        for q in range(3):
            backward(n, q).start()

    total = sums_out[...]
    for q in range(3):
        sums(q).wait_recv()
    for q in range(3):
        total = total + sums_in[q]
    for j in range(4):
        mask = zero
        for e in range(ELEMS):
            on = jnp.where(nb_side[e, j] == 3, jnp.where(wall_flag[e, j] == 1, 1.0, 0.0), 0.0)
            mask = jnp.where(sub % 4 == e, on, mask)
        den = jnp.broadcast_to(total[:, 24 + j : 25 + j], (8, 128))
        sigma = [
            jnp.broadcast_to(total[:, j * 6 + k : j * 6 + k + 1], (8, 128)) / den * mask
            for k in range(6)
        ]
        for n in range(NODES):
            part = lift[0, j, n] * sigma[0]
            for k in range(1, 6):
                part = part + lift[k, j, n] * sigma[k]
            wallsum[(j * NODES + n) * 8 : (j * NODES + n) * 8 + 8, :] = part

    @pl.loop(0, ELEMS)
    def _(e):
        @pl.loop(0, NODES)
        def _(n):
            parts = [
                jnp.broadcast_to(wallsum[pl.ds((j * NODES + n) * 8 + e, 1), :], (8, 128))
                for j in range(4)
            ]
            for a in range(8):
                x = moved[rows((e * NODES + n) * SLAB + a * 8), :]
                for j in range(4):
                    x = x - parts[j] * negwall[(j * 8 + a) * 8 : (j * 8 + a) * 8 + 8, :]
                moved[rows((e * NODES + n) * SLAB + a * 8), :] = x

    @pl.loop(0, NODES)
    def _(n):
        for a in range(8):
            out[pl.ds(n * BLOCK + a * 32 + me, 8, stride=4), :] = (
                result[rows(n * BLOCK + me * SLAB + a * 8), :]
                + moved[rows((me * NODES + n) * SLAB + a * 8), :]
            )
        for q in range(3):
            backward_in(n, q, back, result, bwd_send, bwd_recv, partners, rows).wait_recv()
            e = partners[q]
            for a in range(8):
                at = rows((e * NODES + n) * SLAB + a * 8)
                out[pl.ds(n * BLOCK + a * 32 + e, 8, stride=4), :] = back[at, :] + moved[at, :]
        store(n).start()

    @pl.loop(0, NODES)
    def _(n):
        for q in range(3):
            forward(n, q).wait_send()
            backward(n, q).wait_send()
        store(n).wait()

    for side in range(2):
        halo(side).wait_send()
    for q in range(3):
        sums(q).wait_send()


def forward_in(n, q, block, pool, send, recv, partners, rows):
    return pltpu.make_async_remote_copy(
        src_ref=pool.at[pl.ds(0, 8)],
        dst_ref=block.at[pl.ds(n * 32 + partners[q] * 8, 8)],
        send_sem=send.at[n, q],
        recv_sem=recv.at[n, q],
        device_id={"vel": partners[q]},
    )


def backward_in(n, q, back, result, send, recv, partners, rows):
    return pltpu.make_async_remote_copy(
        src_ref=result.at[rows(0, SLAB)],
        dst_ref=back.at[rows((partners[q] * NODES + n) * SLAB, SLAB)],
        send_sem=send.at[n, q],
        recv_sem=recv.at[n, q],
        device_id={"vel": partners[q]},
    )


def solution(mesh):
    space = mesh.shape["space"]
    constants = tables()

    def local(
        dist,
        phi,
        khat,
        deriv,
        lift,
        normals,
        wall_maxw,
        free_stream,
        inject,
        nb_local,
        nb_side,
        wall_flag,
        inj_id,
    ):
        lines = dist.transpose(1, 0, 2).reshape(NODES, ELEMS, SLAB, 128)
        lines = lines.transpose(0, 2, 1, 3).reshape(NODES * BLOCK, 128)
        profiles = inject.reshape(4, SLAB, 128).transpose(1, 0, 2).reshape(BLOCK, 128)
        hbm = pl.BlockSpec(memory_space=pltpu.HBM)
        f32 = jnp.float32
        dma = pltpu.SemaphoreType.DMA

        tables = [jnp.asarray(c) for c in constants]
        operands = [
            lines,
            phi.reshape(BLOCK, 128),
            khat,
            wall_maxw.reshape(SLAB, 128),
            free_stream.reshape(SLAB, 128),
            profiles,
            *tables,
            deriv.transpose(1, 0, 2),
            lift.transpose(2, 0, 1),
            normals,
            nb_local,
            nb_side,
            wall_flag,
            inj_id,
        ]

        def body(*refs):
            kernel(space, *refs)

        rate = pl.pallas_call(
            body,
            out_shape=jax.ShapeDtypeStruct((NODES * BLOCK, 128), f32),
            in_specs=[hbm] * len(operands),
            out_specs=hbm,
            scratch_shapes=[pltpu.VMEM((NODES * BLOCK, 128), f32)]
            + [pltpu.VMEM(x.shape, x.dtype) for x in operands[:12]]
            + [pltpu.SMEM(x.shape, x.dtype) for x in operands[12:]]
            + [
                pltpu.VMEM((POOL, 8, 128), f32),
                pltpu.VMEM((NODES * 32, 8, 128), f32),
                pltpu.VMEM((NODES * BLOCK, 128), f32),
                pltpu.VMEM((ELEMS * NODES * SLAB, 128), f32),
                pltpu.VMEM((ELEMS * NODES * SLAB, 128), f32),
                pltpu.VMEM((24, ELEMS * 8, 128), f32),
                pltpu.VMEM((4 * SLAB, 128), f32),
                pltpu.VMEM((BLOCK, 128), f32),
                pltpu.VMEM((BLOCK, 128), f32),
                pltpu.VMEM((HALF, 128), f32),
                pltpu.VMEM((4 * NODES * 8, 128), f32),
                pltpu.VMEM((2, 6 * 8, 8, 128), f32),
                pltpu.VMEM((2, 6 * 8, 8, 128), f32),
                pltpu.VMEM((8, 128), f32),
                pltpu.VMEM((3, 8, 128), f32),
                dma((NODES,)),
                dma((NODES,)),
                dma((len(operands) - 1,)),
                dma((NODES, 3)),
                dma((NODES, 3)),
                dma((NODES, 3)),
                dma((NODES, 3)),
                dma((2,)),
                dma((2,)),
                dma((3,)),
                dma((3,)),
            ],
            compiler_params=pltpu.CompilerParams(
                collective_id=0, has_side_effects=True, vmem_limit_bytes=60 * 2**20
            ),
            name="rate",
        )(*operands)
        rate = rate.reshape(NODES, SLAB, ELEMS, 128).transpose(0, 2, 1, 3)
        return rate.reshape(NODES, ELEMS, SLAB * 128).transpose(1, 0, 2)

    return jax.shard_map(
        local,
        mesh=mesh,
        in_specs=(
            P("space", None, "vel"),
            P(),
            P(),
            P(),
            P(),
            P(),
            P("vel"),
            P("vel"),
            P(None, "vel"),
            P("space", None),
            P("space", None),
            P("space", None),
            P("space", None),
        ),
        out_specs=P("space", None, "vel"),
        check_vma=False,
    )
```

```python
import math

import jax
import jax.numpy as jnp
import numpy as np
import ml_dtypes
from jax import lax
from jax.experimental import pallas as pl
from jax.experimental.pallas import tpu as pltpu
from jax.sharding import PartitionSpec as P

FACES = ((1, 2, 3, 5, 8, 9), (0, 2, 3, 6, 7, 9), (0, 1, 3, 4, 7, 8), (0, 1, 2, 4, 5, 6))
SPEED = 3.0
NODES = 10
ELEMS = 4
GROUP = 4
SLAB = 64
BLOCK = 256
HALF = 136
PACK = 128
TABLE = ELEMS * NODES * 8
HALO = TABLE + 5 * 8
POOL = HALO + 2 * NODES * 8


def split(x):
    hi = x.astype(ml_dtypes.bfloat16)
    lo = (x - hi.astype(np.float64)).astype(ml_dtypes.bfloat16)
    return hi, lo


def tables():
    turn = 2.0 * np.pi
    ka = np.repeat(np.arange(17), 8)
    kl = np.tile(np.arange(8), 17)
    a = np.repeat(np.arange(32), 8)
    bh = np.tile(np.arange(8), 32)
    bl = np.repeat(np.arange(4), 32)
    c = np.tile(np.arange(32), 4)
    angle = turn * ((np.outer(ka, a) % 32) / 32.0 + (np.outer(kl, bh) % 8) / 8.0)
    rows_fwd = np.concatenate([np.cos(angle), -np.sin(angle)], axis=0)
    angle = turn * ((np.outer(bl, bl) % 4) / 4.0 + (np.outer(c, c) % 32) / 32.0)
    co, si = np.cos(angle), np.sin(angle)
    lanes_fwd = np.concatenate(
        [np.concatenate([co, -si], axis=1), np.concatenate([si, co], axis=1)], axis=0
    )
    lanes_bwd = np.concatenate(
        [np.concatenate([co, si], axis=1), np.concatenate([-si, co], axis=1)], axis=0
    )
    angle = turn * ((np.outer(a, ka[:PACK]) % 32) / 32.0 + (np.outer(bh, kl[:PACK]) % 8) / 8.0)
    re, im = 2.0 * np.cos(angle), -2.0 * np.sin(angle)
    sign = np.where(a % 2 == 0, 1.0, -1.0)[:, None]
    angle = turn * ((np.outer(bh, np.arange(8)) % 8) / 8.0)
    re[:, :8] = np.cos(angle) + sign * np.sin(angle)
    im[:, :8] = -np.sin(angle) + sign * np.cos(angle)
    rows_bwd = np.concatenate([re, im], axis=1) * 2.0**-15

    def left(x):
        hi, lo = split(x)
        return np.concatenate([hi, hi, lo], axis=1)

    def right(x):
        hi, lo = split(x)
        return np.concatenate([hi, hi, lo], axis=0)

    angle = turn * np.outer(np.arange(8), bl) / 32.0
    twiddle = np.concatenate([np.cos(angle), np.sin(angle)], axis=0).astype(np.float32)
    lane = np.arange(128)
    mirror = (lane // 32) * 32 + (32 - lane % 32) % 32
    reverse = (lane[:, None] == mirror[None, :]).astype(ml_dtypes.bfloat16)
    return (left(rows_fwd), right(lanes_fwd), right(lanes_bwd), left(rows_bwd), twiddle, reverse)


def halves(x):
    hi = x.astype(jnp.bfloat16)
    lo = (x - hi.astype(jnp.float32)).astype(jnp.bfloat16)
    return hi, lo


def dot_left(table, x):
    hi, lo = halves(x)
    return jnp.dot(
        table, jnp.concatenate([hi, lo, hi], axis=0), preferred_element_type=jnp.float32
    )


def dot_right(x, table):
    hi, lo = halves(x)
    return jnp.dot(
        jnp.concatenate([hi, lo, hi], axis=1), table, preferred_element_type=jnp.float32
    )


def by_rows(x, y):
    return jnp.concatenate([x, y], axis=0)


def by_lanes(x, y):
    return jnp.concatenate([x, y], axis=1)


def turned(re, im, cos, sin):
    count = re.shape[0] // 8
    re = re.reshape(count, 8, 128)
    im = im.reshape(count, 8, 128)
    out_re = re * cos[None] - im * sin[None]
    out_im = re * sin[None] + im * cos[None]
    return out_re.reshape(count * 8, 128), out_im.reshape(count * 8, 128)


def collide(x, phi, sym, rows_fwd, lanes_fwd, lanes_bwd, rows_bwd, cos, sin):
    y = dot_left(rows_fwd, by_lanes(x * phi, x))
    wr, wi = turned(y[:HALF, :128], y[HALF:, :128], cos, -sin)
    fr, fi = turned(y[:HALF, 128:], y[HALF:, 128:], cos, -sin)
    s = dot_right(by_rows(by_lanes(wr, wi), by_lanes(fr, fi)), lanes_fwd)
    wr, wi, fr, fi = s[:HALF, :128], s[:HALF, 128:], s[HALF:, :128], s[HALF:, 128:]
    wr, wi = wr * 2.0**-15, wi * 2.0**-15

    def packed(re, im):
        first = re[:8] - im[PACK:]
        second = im[:8] + re[PACK:]
        return by_lanes(by_rows(first, re[8:PACK]), by_rows(second, im[8:PACK]))

    gain = packed(wr * fr - wi * fi, wr * fi + wi * fr)
    loss = packed(sym * fr, sym * fi)
    b = dot_right(by_rows(gain, loss), lanes_bwd)
    gr, gi = turned(b[:PACK, :128], b[:PACK, 128:], cos, sin)
    lr, li = turned(b[PACK:, :128], b[PACK:, 128:], cos, sin)
    z = dot_left(rows_bwd, by_rows(by_lanes(gr, lr), by_lanes(gi, li)))
    return z[:, :128] - x * z[:, 128:]


def kernel(
    space,
    dist_in,
    phi_in,
    khat_in,
    wall_in,
    free_in,
    inject_in,
    rows_fwd_in,
    lanes_fwd_in,
    lanes_bwd_in,
    rows_bwd_in,
    twiddle_in,
    reverse_in,
    deriv_in,
    lift_in,
    normals_in,
    nb_local_in,
    nb_side_in,
    wall_flag_in,
    inj_id_in,
    out_hbm,
    out,
    dist,
    phi,
    khat,
    wall,
    free,
    inject,
    rows_fwd,
    lanes_fwd,
    lanes_bwd,
    rows_bwd,
    twiddle,
    reverse,
    deriv,
    lift,
    normals,
    nb_local,
    nb_side,
    wall_flag,
    inj_id,
    pool,
    block,
    result,
    back,
    moved,
    diff,
    negwall,
    straight,
    mirrored,
    sym,
    wallsum,
    halo_out,
    halo_in,
    sums_out,
    sums_in,
    dist_sem,
    out_sem,
    load_sem,
    fwd_send,
    fwd_recv,
    bwd_send,
    bwd_recv,
    halo_send,
    halo_recv,
    sums_send,
    sums_recv,
):
    f32 = jnp.float32
    me = lax.axis_index("vel")
    here = lax.axis_index("space")
    parity = lax.rem(here, 2)
    has_above = here < space - 1
    has_below = here > 0
    beside = jnp.where(has_above, 1, 0) + jnp.where(has_below, 1, 0)
    core = lax.rem(me, 2)
    flip = 1 - 2 * core
    across = lax.rem(me + 2, GROUP)
    partners = (across, across + flip, me + flip)

    def rows(start, count=8):
        return pl.ds(pl.multiple_of(start, 8), count)

    def forward(n, q):
        to = partners[q]
        return pltpu.make_async_remote_copy(
            src_ref=pool.at[pl.ds((to * NODES + n) * 8, 8)],
            dst_ref=block.at[pl.ds(n * 32 + me * 8, 8)],
            send_sem=fwd_send.at[n, q],
            recv_sem=fwd_recv.at[n, q],
            device_id={"vel": to},
        )

    def backward(n, q):
        to = partners[q]
        return pltpu.make_async_remote_copy(
            src_ref=result.at[rows(n * BLOCK + to * SLAB, SLAB)],
            dst_ref=back.at[rows((me * NODES + n) * SLAB, SLAB)],
            send_sem=bwd_send.at[n, q],
            recv_sem=bwd_recv.at[n, q],
            device_id={"vel": to},
        )

    def halo(side):
        return pltpu.make_async_remote_copy(
            src_ref=halo_out.at[side],
            dst_ref=halo_in.at[side],
            send_sem=halo_send.at[side],
            recv_sem=halo_recv.at[side],
            device_id={"space": lax.rem(here + (space - 1 if side else 1), space)},
        )

    def sums(q):
        return pltpu.make_async_remote_copy(
            src_ref=sums_out,
            dst_ref=sums_in.at[q],
            send_sem=sums_send.at[q],
            recv_sem=sums_recv.at[q],
            device_id={"vel": partners[q]},
        )

    def dist_load(n):
        part = rows(n * BLOCK, BLOCK)
        return pltpu.make_async_copy(dist_in.at[part], dist.at[part], dist_sem.at[n])

    def store(n):
        part = rows(n * BLOCK, BLOCK)
        return pltpu.make_async_copy(out.at[part], out_hbm.at[part], out_sem.at[n])

    pairs = (
        (nb_side_in, nb_side),
        (inject_in, inject),
        (free_in, free),
        (normals_in, normals),
        (wall_in, wall),
        (khat_in, khat),
        (reverse_in, reverse),
        (nb_local_in, nb_local),
        (wall_flag_in, wall_flag),
        (inj_id_in, inj_id),
        (deriv_in, deriv),
        (lift_in, lift),
        (phi_in, phi),
        (rows_fwd_in, rows_fwd),
        (lanes_fwd_in, lanes_fwd),
        (twiddle_in, twiddle),
        (lanes_bwd_in, lanes_bwd),
        (rows_bwd_in, rows_bwd),
    )
    loads = [
        pltpu.make_async_copy(source, target, load_sem.at[i])
        for i, (source, target) in enumerate(pairs)
    ]

    barrier = pltpu.get_barrier_semaphore()
    for to in partners:
        pl.semaphore_signal(barrier, inc=1, device_id={"vel": to})
    for n in range(NODES):
        dist_load(n).start()

    def greet():
        @pl.when(has_above)
        def _():
            pl.semaphore_signal(barrier, inc=1, device_id={"space": here + 1})

        @pl.when(has_below)
        def _():
            pl.semaphore_signal(barrier, inc=1, device_id={"space": here - 1})

    @pl.when(parity == 1)
    def _():
        pl.semaphore_wait(barrier, 3 + beside)

    @pl.when(parity == 0)
    def _():
        pl.semaphore_wait(barrier, 3)

    greet()
    for load in loads:
        load.start()

    @pl.loop(0, NODES)
    def _(n):
        dist_load(n).wait()
        for e in range(ELEMS):
            for a in range(8):
                pool[(e * NODES + n) * 8 + a] = dist[
                    pl.ds(n * BLOCK + a * 32 + e, 8, stride=4), :
                ]
        for q in range(3):
            forward(n, q).start()
        for a in range(8):
            block[n * 32 + me * 8 + a] = pool[(me * NODES + n) * 8 + a]

    for load in loads:
        load.wait()

    for q in range(4):
        for a in range(8):
            pool[TABLE + q * 8 + a] = inject[pl.ds(a * 32 + q, 8, stride=4), :]
    for a in range(8):
        pool[TABLE + 32 + a] = free[a * 8 : a * 8 + 8, :]

    sub = lax.broadcasted_iota(jnp.int32, (8, 128), 0)
    lane = lax.broadcasted_iota(jnp.int32, (8, 128), 1)

    def grid(i):
        return SPEED * ((2.0 * i.astype(f32) + 1.0) / 32.0 - 1.0)

    v2 = grid(lane % 32)
    v1 = grid(sub * 4 + lane // 32)

    def normal_speed(j, v0, v1):
        return normals[j, 0] * v0 + normals[j, 1] * v1 + normals[j, 2] * v2

    def partial_sums(i, carry):
        a = i // 4
        v0 = grid(me * 8 + a)
        b = (lax.rem(i, 4) * 2 + sub // 4) * 4 + lane // 32
        got = [dist[rows(n * BLOCK + i * 8), :] for n in range(NODES)]
        new = []
        for j in range(4):
            pos = jnp.maximum(normal_speed(j, v0, grid(b)), 0.0)
            for k in range(6):
                new.append(carry[j * 6 + k] + pos * got[FACES[j][k]])
        return tuple(new)

    zero = jnp.zeros((8, 128), f32)
    nums = lax.fori_loop(0, 32, partial_sums, (zero,) * 24)

    def partial_dens(a, carry):
        v0 = grid(me * 8 + a)
        new = []
        for j in range(4):
            value = jnp.minimum(normal_speed(j, v0, v1), 0.0) * wall[rows(a * 8), :]
            negwall[rows((j * 8 + a) * 8), :] = value
            new.append(carry[j] - value)
        return tuple(new)

    dens = lax.fori_loop(0, 8, partial_dens, (zero,) * 4)
    mine = zero
    for i, x in enumerate(nums):
        x = x + pltpu.roll(x, 4, 0)
        mine = jnp.where(lane == i, jnp.sum(x, axis=1, keepdims=True), mine)
    for j, x in enumerate(dens):
        x = jnp.broadcast_to(jnp.sum(x, axis=0, keepdims=True), (8, 128))
        mine = jnp.where(lane == 24 + j, jnp.sum(x, axis=1, keepdims=True), mine)
    sums_out[...] = mine
    for q in range(3):
        sums(q).start()

    for i in range(8):
        x = khat[:, i * 128 : (i + 1) * 128]
        straight[i * 32 : (i + 1) * 32, :] = x
    x = straight[...]
    x0 = x.astype(jnp.bfloat16)
    x = x - x0.astype(f32)
    x1 = x.astype(jnp.bfloat16)
    x2 = (x - x1.astype(f32)).astype(jnp.bfloat16)
    rev = reverse[...]
    mirrored[...] = (
        jnp.dot(x0, rev, preferred_element_type=f32) + jnp.dot(x1, rev, preferred_element_type=f32)
    ) + jnp.dot(x2, rev, preferred_element_type=f32)
    group = lax.broadcasted_iota(jnp.int32, (32, 128), 1) // 32

    def regroup(source, place):
        total = jnp.zeros((32, 128), f32)
        for kh in range(4):
            kb = place(kh)
            tile, offset = kb // 4, kb % 4
            x = source[tile * 32 : (tile + 1) * 32, :]
            shift = (kh - offset) % 4 * 32
            if shift:
                x = pltpu.roll(x, shift, 1)
            total = jnp.where(group == kh, x, total)
        return total

    for kl in range(8):
        even = regroup(straight, lambda kh: kl + 8 * kh)
        odd = regroup(mirrored, lambda kh: (32 - kl - 8 * kh) % 32)
        moved[pl.ds(kl, 32, stride=8), :] = even
        moved[pl.ds(BLOCK + kl, 32, stride=8), :] = odd
    for ka in range(17):
        other = BLOCK + (32 - ka) % 32 * 8
        sym[ka * 8 : ka * 8 + 8, :] = 0.5 * (
            moved[ka * 8 : ka * 8 + 8, :] + moved[other : other + 8, :]
        )

    def send_halos():
        @pl.when(parity == 0)
        def _():
            pl.semaphore_wait(barrier, beside)


        up_elem = jnp.int32(0)
        down_elem = jnp.int32(0)
        for e in range(ELEMS):
            up_elem = up_elem + jnp.where(nb_side[e, 1] == 2, e, 0)
            down_elem = down_elem + jnp.where(nb_side[e, 0] == 1, e, 0)
        for side, elem, face in ((0, up_elem, 1), (1, down_elem, 0)):
            for k in range(6):
                for a in range(8):
                    halo_out[side, k * 8 + a] = pool[(elem * NODES + FACES[face][k]) * 8 + a]

            @pl.when(has_below if side else has_above)
            def _():
                halo(side).start()

    cos = twiddle[0:8, :]
    sin = twiddle[8:16, :]

    @pl.loop(0, NODES)
    def _(n):
        @pl.when(n == 3)
        def _():
            send_halos()

        for q in range(3):
            forward_in(n, q, block, pool, fwd_send, fwd_recv, partners, rows).wait_recv()
        result[rows(n * BLOCK, BLOCK), :] = collide(
            block[pl.ds(n * 32, 32)].reshape(BLOCK, 128),
            phi[...],
            sym[...],
            rows_fwd[...],
            lanes_fwd[...],
            lanes_bwd[...],
            rows_bwd[...],
            cos,
            sin,
        )
        for q in range(3):
            backward(n, q).start()

    for side, face in ((0, 1), (1, 0)):

        @pl.when(has_above if side else has_below)
        def _():
            halo(side).wait_recv()
            for k in range(6):
                start = HALO + (side * NODES + FACES[face][k]) * 8
                for a in range(8):
                    pool[start + a] = halo_in[side, k * 8 + a]

    @pl.loop(0, 8)
    def _(a):
        v0 = grid(me * 8 + a)
        negs = [jnp.minimum(normal_speed(j, v0, v1), 0.0) for j in range(4)]

        @pl.loop(0, ELEMS)
        def _(e):
            for j in range(4):
                side = nb_side[e, j]
                inner = jnp.where(side == 3, 0, 8)
                edge = TABLE + jnp.where(wall_flag[e, j] == 1, inj_id[e, j], 4) * 8
                near = nb_local[e, j] * (NODES * 8)
                far = HALO + jnp.where(side == 2, NODES * 8, 0)
                base = jnp.where(side == 3, edge, jnp.where(side == 0, near, far)) + a
                for k in range(6):
                    outer = pool[base + inner * FACES[j ^ 1][k]]
                    trace = pool[(e * NODES + FACES[j][k]) * 8 + a]
                    diff[j * 6 + k, rows(e * 8), :] = negs[j] * (trace - outer)

        @pl.loop(0, NODES // 2)
        def _(pair):
            acc = [[zero] * ELEMS for _ in range(2)]
            for m in range(NODES):
                for i in range(2):
                    n = pair * 2 + i
                    c = deriv[n, 0, m] * v0 + deriv[n, 1, m] * v1 + deriv[n, 2, m] * v2
                    for e in range(ELEMS):
                        f = pool[(e * NODES + m) * 8 + a]
                        acc[i][e] = acc[i][e] - c * f
            for j in range(4):
                for k in range(6):
                    for i in range(2):
                        c = lift[k, j, pair * 2 + i]
                        for e in range(ELEMS):
                            d = diff[j * 6 + k, e * 8 : e * 8 + 8, :]
                            acc[i][e] = acc[i][e] + c * d
            for i in range(2):
                for e in range(ELEMS):
                    moved[rows((e * NODES + pair * 2 + i) * SLAB + a * 8), :] = acc[i][e]

    total = sums_out[...]
    for q in range(3):
        sums(q).wait_recv()
    for q in range(3):
        total = total + sums_in[q]
    for j in range(4):
        mask = zero
        for e in range(ELEMS):
            on = jnp.where(nb_side[e, j] == 3, jnp.where(wall_flag[e, j] == 1, 1.0, 0.0), 0.0)
            mask = jnp.where(sub % 4 == e, on, mask)
        den = jnp.broadcast_to(total[:, 24 + j : 25 + j], (8, 128))
        sigma = [
            jnp.broadcast_to(total[:, j * 6 + k : j * 6 + k + 1], (8, 128)) / den * mask
            for k in range(6)
        ]
        for n in range(NODES):
            part = lift[0, j, n] * sigma[0]
            for k in range(1, 6):
                part = part + lift[k, j, n] * sigma[k]
            wallsum[(j * NODES + n) * 8 : (j * NODES + n) * 8 + 8, :] = part

    @pl.loop(0, ELEMS)
    def _(e):
        @pl.loop(0, NODES)
        def _(n):
            parts = [
                jnp.broadcast_to(wallsum[pl.ds((j * NODES + n) * 8 + e, 1), :], (8, 128))
                for j in range(4)
            ]
            for a in range(8):
                x = moved[rows((e * NODES + n) * SLAB + a * 8), :]
                for j in range(4):
                    x = x - parts[j] * negwall[(j * 8 + a) * 8 : (j * 8 + a) * 8 + 8, :]
                moved[rows((e * NODES + n) * SLAB + a * 8), :] = x

    @pl.loop(0, NODES)
    def _(n):
        for a in range(8):
            out[pl.ds(n * BLOCK + a * 32 + me, 8, stride=4), :] = (
                result[rows(n * BLOCK + me * SLAB + a * 8), :]
                + moved[rows((me * NODES + n) * SLAB + a * 8), :]
            )
        for q in range(3):
            backward_in(n, q, back, result, bwd_send, bwd_recv, partners, rows).wait_recv()
            e = partners[q]
            for a in range(8):
                at = rows((e * NODES + n) * SLAB + a * 8)
                out[pl.ds(n * BLOCK + a * 32 + e, 8, stride=4), :] = back[at, :] + moved[at, :]
        store(n).start()

    @pl.loop(0, NODES)
    def _(n):
        for q in range(3):
            forward(n, q).wait_send()
            backward(n, q).wait_send()
        store(n).wait()

    for side in range(2):

        @pl.when(has_below if side else has_above)
        def _():
            halo(side).wait_send()

    for q in range(3):
        sums(q).wait_send()


def forward_in(n, q, block, pool, send, recv, partners, rows):
    return pltpu.make_async_remote_copy(
        src_ref=pool.at[pl.ds(0, 8)],
        dst_ref=block.at[pl.ds(n * 32 + partners[q] * 8, 8)],
        send_sem=send.at[n, q],
        recv_sem=recv.at[n, q],
        device_id={"vel": partners[q]},
    )


def backward_in(n, q, back, result, send, recv, partners, rows):
    return pltpu.make_async_remote_copy(
        src_ref=result.at[rows(0, SLAB)],
        dst_ref=back.at[rows((partners[q] * NODES + n) * SLAB, SLAB)],
        send_sem=send.at[n, q],
        recv_sem=recv.at[n, q],
        device_id={"vel": partners[q]},
    )


def solution(mesh):
    space = mesh.shape["space"]
    constants = tables()

    def local(
        dist,
        phi,
        khat,
        deriv,
        lift,
        normals,
        wall_maxw,
        free_stream,
        inject,
        nb_local,
        nb_side,
        wall_flag,
        inj_id,
    ):
        lines = dist.transpose(1, 0, 2).reshape(NODES, ELEMS, SLAB, 128)
        lines = lines.transpose(0, 2, 1, 3).reshape(NODES * BLOCK, 128)
        profiles = inject.reshape(4, SLAB, 128).transpose(1, 0, 2).reshape(BLOCK, 128)
        hbm = pl.BlockSpec(memory_space=pltpu.HBM)
        f32 = jnp.float32
        dma = pltpu.SemaphoreType.DMA

        tables = [jnp.asarray(c) for c in constants]
        operands = [
            lines,
            phi.reshape(BLOCK, 128),
            khat,
            wall_maxw.reshape(SLAB, 128),
            free_stream.reshape(SLAB, 128),
            profiles,
            *tables,
            deriv.transpose(1, 0, 2),
            lift.transpose(2, 0, 1),
            normals,
            nb_local,
            nb_side,
            wall_flag,
            inj_id,
        ]

        def body(*refs):
            kernel(space, *refs)

        rate = pl.pallas_call(
            body,
            out_shape=jax.ShapeDtypeStruct((NODES * BLOCK, 128), f32),
            in_specs=[hbm] * len(operands),
            out_specs=hbm,
            scratch_shapes=[pltpu.VMEM((NODES * BLOCK, 128), f32)]
            + [pltpu.VMEM(x.shape, x.dtype) for x in operands[:12]]
            + [pltpu.SMEM(x.shape, x.dtype) for x in operands[12:]]
            + [
                pltpu.VMEM((POOL, 8, 128), f32),
                pltpu.VMEM((NODES * 32, 8, 128), f32),
                pltpu.VMEM((NODES * BLOCK, 128), f32),
                pltpu.VMEM((ELEMS * NODES * SLAB, 128), f32),
                pltpu.VMEM((ELEMS * NODES * SLAB, 128), f32),
                pltpu.VMEM((24, ELEMS * 8, 128), f32),
                pltpu.VMEM((4 * SLAB, 128), f32),
                pltpu.VMEM((BLOCK, 128), f32),
                pltpu.VMEM((BLOCK, 128), f32),
                pltpu.VMEM((HALF, 128), f32),
                pltpu.VMEM((4 * NODES * 8, 128), f32),
                pltpu.VMEM((2, 6 * 8, 8, 128), f32),
                pltpu.VMEM((2, 6 * 8, 8, 128), f32),
                pltpu.VMEM((8, 128), f32),
                pltpu.VMEM((3, 8, 128), f32),
                dma((NODES,)),
                dma((NODES,)),
                dma((len(operands) - 1,)),
                dma((NODES, 3)),
                dma((NODES, 3)),
                dma((NODES, 3)),
                dma((NODES, 3)),
                dma((2,)),
                dma((2,)),
                dma((3,)),
                dma((3,)),
            ],
            compiler_params=pltpu.CompilerParams(
                collective_id=0, has_side_effects=True, vmem_limit_bytes=60 * 2**20
            ),
            name="rate",
        )(*operands)
        rate = rate.reshape(NODES, SLAB, ELEMS, 128).transpose(0, 2, 1, 3)
        return rate.reshape(NODES, ELEMS, SLAB * 128).transpose(1, 0, 2)

    return jax.shard_map(
        local,
        mesh=mesh,
        in_specs=(
            P("space", None, "vel"),
            P(),
            P(),
            P(),
            P(),
            P(),
            P("vel"),
            P("vel"),
            P(None, "vel"),
            P("space", None),
            P("space", None),
            P("space", None),
            P("space", None),
        ),
        out_specs=P("space", None, "vel"),
        check_vma=False,
    )
```

```python
import math

import jax
import jax.numpy as jnp
import numpy as np
import ml_dtypes
from jax import lax
from jax.experimental import pallas as pl
from jax.experimental.pallas import tpu as pltpu
from jax.sharding import PartitionSpec as P

FACES = ((1, 2, 3, 5, 8, 9), (0, 2, 3, 6, 7, 9), (0, 1, 3, 4, 7, 8), (0, 1, 2, 4, 5, 6))
SPEED = 3.0
NODES = 10
ELEMS = 4
GROUP = 4
SLAB = 64
BLOCK = 256
HALF = 136
PACK = 128
TABLE = ELEMS * NODES * 8
HALO = TABLE + 5 * 8
POOL = HALO + 2 * NODES * 8


def split(x):
    hi = x.astype(ml_dtypes.bfloat16)
    lo = (x - hi.astype(np.float64)).astype(ml_dtypes.bfloat16)
    return hi, lo


def tables():
    turn = 2.0 * np.pi
    ka = np.repeat(np.arange(17), 8)
    kl = np.tile(np.arange(8), 17)
    a = np.repeat(np.arange(32), 8)
    bh = np.tile(np.arange(8), 32)
    bl = np.repeat(np.arange(4), 32)
    c = np.tile(np.arange(32), 4)
    angle = turn * ((np.outer(ka, a) % 32) / 32.0 + (np.outer(kl, bh) % 8) / 8.0)
    rows_fwd = np.concatenate([np.cos(angle), -np.sin(angle)], axis=0)
    angle = turn * ((np.outer(bl, bl) % 4) / 4.0 + (np.outer(c, c) % 32) / 32.0)
    co, si = np.cos(angle), np.sin(angle)
    lanes_fwd = np.concatenate(
        [np.concatenate([co, -si], axis=1), np.concatenate([si, co], axis=1)], axis=0
    )
    lanes_bwd = np.concatenate(
        [np.concatenate([co, si], axis=1), np.concatenate([-si, co], axis=1)], axis=0
    )
    angle = turn * ((np.outer(a, ka[:PACK]) % 32) / 32.0 + (np.outer(bh, kl[:PACK]) % 8) / 8.0)
    re, im = 2.0 * np.cos(angle), -2.0 * np.sin(angle)
    sign = np.where(a % 2 == 0, 1.0, -1.0)[:, None]
    angle = turn * ((np.outer(bh, np.arange(8)) % 8) / 8.0)
    re[:, :8] = np.cos(angle) + sign * np.sin(angle)
    im[:, :8] = -np.sin(angle) + sign * np.cos(angle)
    rows_bwd = np.concatenate([re, im], axis=1) * 2.0**-15

    def left(x):
        hi, lo = split(x)
        return np.concatenate([hi, hi, lo], axis=1)

    def right(x):
        hi, lo = split(x)
        return np.concatenate([hi, hi, lo], axis=0)

    angle = turn * np.outer(np.arange(8), bl) / 32.0
    twiddle = np.concatenate([np.cos(angle), np.sin(angle)], axis=0).astype(np.float32)
    lane = np.arange(128)
    mirror = (lane // 32) * 32 + (32 - lane % 32) % 32
    reverse = (lane[:, None] == mirror[None, :]).astype(ml_dtypes.bfloat16)
    return (left(rows_fwd), right(lanes_fwd), right(lanes_bwd), left(rows_bwd), twiddle, reverse)


def halves(x):
    hi = x.astype(jnp.bfloat16)
    lo = (x - hi.astype(jnp.float32)).astype(jnp.bfloat16)
    return hi, lo


def dot_left(table, x):
    hi, lo = halves(x)
    return jnp.dot(
        table, jnp.concatenate([hi, lo, hi], axis=0), preferred_element_type=jnp.float32
    )


def dot_right(x, table):
    hi, lo = halves(x)
    return jnp.dot(
        jnp.concatenate([hi, lo, hi], axis=1), table, preferred_element_type=jnp.float32
    )


def by_rows(x, y):
    return jnp.concatenate([x, y], axis=0)


def by_lanes(x, y):
    return jnp.concatenate([x, y], axis=1)


def turned(re, im, cos, sin):
    count = re.shape[0] // 8
    re = re.reshape(count, 8, 128)
    im = im.reshape(count, 8, 128)
    out_re = re * cos[None] - im * sin[None]
    out_im = re * sin[None] + im * cos[None]
    return out_re.reshape(count * 8, 128), out_im.reshape(count * 8, 128)


def collide(x, phi, sym, rows_fwd, lanes_fwd, lanes_bwd, rows_bwd, cos, sin):
    y = dot_left(rows_fwd, by_lanes(x * phi, x))
    wr, wi = turned(y[:HALF, :128], y[HALF:, :128], cos, -sin)
    fr, fi = turned(y[:HALF, 128:], y[HALF:, 128:], cos, -sin)
    s = dot_right(by_rows(by_lanes(wr, wi), by_lanes(fr, fi)), lanes_fwd)
    wr, wi, fr, fi = s[:HALF, :128], s[:HALF, 128:], s[HALF:, :128], s[HALF:, 128:]
    wr, wi = wr * 2.0**-15, wi * 2.0**-15

    def packed(re, im):
        first = re[:8] - im[PACK:]
        second = im[:8] + re[PACK:]
        return by_lanes(by_rows(first, re[8:PACK]), by_rows(second, im[8:PACK]))

    gain = packed(wr * fr - wi * fi, wr * fi + wi * fr)
    loss = packed(sym * fr, sym * fi)
    b = dot_right(by_rows(gain, loss), lanes_bwd)
    gr, gi = turned(b[:PACK, :128], b[:PACK, 128:], cos, sin)
    lr, li = turned(b[PACK:, :128], b[PACK:, 128:], cos, sin)
    z = dot_left(rows_bwd, by_rows(by_lanes(gr, lr), by_lanes(gi, li)))
    return z[:, :128] - x * z[:, 128:]


def kernel(
    space,
    dist_in,
    phi_in,
    khat_in,
    wall_in,
    free_in,
    inject_in,
    rows_fwd_in,
    lanes_fwd_in,
    lanes_bwd_in,
    rows_bwd_in,
    twiddle_in,
    reverse_in,
    deriv_in,
    lift_in,
    normals_in,
    nb_local_in,
    nb_side_in,
    wall_flag_in,
    inj_id_in,
    out,
    dist,
    phi,
    khat,
    wall,
    free,
    inject,
    rows_fwd,
    lanes_fwd,
    lanes_bwd,
    rows_bwd,
    twiddle,
    reverse,
    deriv,
    lift,
    normals,
    nb_local,
    nb_side,
    wall_flag,
    inj_id,
    pool,
    block,
    result,
    back,
    moved,
    diff,
    negwall,
    straight,
    mirrored,
    sym,
    wallsum,
    halo_out,
    halo_in,
    sums_out,
    sums_in,
    dist_sem,
    load_sem,
    fwd_send,
    fwd_recv,
    bwd_send,
    bwd_recv,
    halo_send,
    halo_recv,
    sums_send,
    sums_recv,
):
    f32 = jnp.float32
    me = lax.axis_index("vel")
    here = lax.axis_index("space")
    parity = lax.rem(here, 2)
    has_above = here < space - 1
    has_below = here > 0
    beside = jnp.where(has_above, 1, 0) + jnp.where(has_below, 1, 0)
    core = lax.rem(me, 2)
    flip = 1 - 2 * core
    across = lax.rem(me + 2, GROUP)
    partners = (across, across + flip, me + flip)

    def rows(start, count=8):
        return pl.ds(pl.multiple_of(start, 8), count)

    def forward(n, q):
        to = partners[q]
        return pltpu.make_async_remote_copy(
            src_ref=pool.at[pl.ds((to * NODES + n) * 8, 8)],
            dst_ref=block.at[pl.ds(n * 32 + me * 8, 8)],
            send_sem=fwd_send.at[n, q],
            recv_sem=fwd_recv.at[n, q],
            device_id={"vel": to},
        )

    def backward(n, q):
        to = partners[q]
        return pltpu.make_async_remote_copy(
            src_ref=result.at[rows(n * BLOCK + to * SLAB, SLAB)],
            dst_ref=back.at[rows((me * NODES + n) * SLAB, SLAB)],
            send_sem=bwd_send.at[n, q],
            recv_sem=bwd_recv.at[n, q],
            device_id={"vel": to},
        )

    def halo(side):
        return pltpu.make_async_remote_copy(
            src_ref=halo_out.at[side],
            dst_ref=halo_in.at[side],
            send_sem=halo_send.at[side],
            recv_sem=halo_recv.at[side],
            device_id={"space": lax.rem(here + (space - 1 if side else 1), space)},
        )

    def sums(q):
        return pltpu.make_async_remote_copy(
            src_ref=sums_out,
            dst_ref=sums_in.at[q],
            send_sem=sums_send.at[q],
            recv_sem=sums_recv.at[q],
            device_id={"vel": partners[q]},
        )

    def dist_load(n):
        part = rows(n * BLOCK, BLOCK)
        return pltpu.make_async_copy(dist_in.at[part], dist.at[part], dist_sem.at[n])

    pairs = (
        (nb_side_in, nb_side),
        (inject_in, inject),
        (free_in, free),
        (normals_in, normals),
        (wall_in, wall),
        (khat_in, khat),
        (reverse_in, reverse),
        (nb_local_in, nb_local),
        (wall_flag_in, wall_flag),
        (inj_id_in, inj_id),
        (deriv_in, deriv),
        (lift_in, lift),
        (phi_in, phi),
        (rows_fwd_in, rows_fwd),
        (lanes_fwd_in, lanes_fwd),
        (twiddle_in, twiddle),
        (lanes_bwd_in, lanes_bwd),
        (rows_bwd_in, rows_bwd),
    )
    loads = [
        pltpu.make_async_copy(source, target, load_sem.at[i])
        for i, (source, target) in enumerate(pairs)
    ]

    barrier = pltpu.get_barrier_semaphore()
    for to in partners:
        pl.semaphore_signal(barrier, inc=1, device_id={"vel": to})
    for n in range(NODES):
        dist_load(n).start()
    for load in loads:
        load.start()

    def greet():
        @pl.when(has_above)
        def _():
            pl.semaphore_signal(barrier, inc=1, device_id={"space": here + 1})

        @pl.when(has_below)
        def _():
            pl.semaphore_signal(barrier, inc=1, device_id={"space": here - 1})

    @pl.when(parity == 1)
    def _():
        pl.semaphore_wait(barrier, 3 + beside)

    @pl.when(parity == 0)
    def _():
        pl.semaphore_wait(barrier, 3)

    greet()

    @pl.loop(0, NODES)
    def _(n):
        dist_load(n).wait()
        for e in range(ELEMS):
            for a in range(8):
                pool[(e * NODES + n) * 8 + a] = dist[
                    pl.ds(n * BLOCK + a * 32 + e, 8, stride=4), :
                ]
        for q in range(3):
            forward(n, q).start()
        for a in range(8):
            block[n * 32 + me * 8 + a] = pool[(me * NODES + n) * 8 + a]

    for load in loads:
        load.wait()

    for q in range(4):
        for a in range(8):
            pool[TABLE + q * 8 + a] = inject[pl.ds(a * 32 + q, 8, stride=4), :]
    for a in range(8):
        pool[TABLE + 32 + a] = free[a * 8 : a * 8 + 8, :]

    sub = lax.broadcasted_iota(jnp.int32, (8, 128), 0)
    lane = lax.broadcasted_iota(jnp.int32, (8, 128), 1)

    def grid(i):
        return SPEED * ((2.0 * i.astype(f32) + 1.0) / 32.0 - 1.0)

    v2 = grid(lane % 32)
    v1 = grid(sub * 4 + lane // 32)

    def normal_speed(j, v0, v1):
        return normals[j, 0] * v0 + normals[j, 1] * v1 + normals[j, 2] * v2

    def partial_sums(i, carry):
        a = i // 4
        v0 = grid(me * 8 + a)
        b = (lax.rem(i, 4) * 2 + sub // 4) * 4 + lane // 32
        got = [dist[rows(n * BLOCK + i * 8), :] for n in range(NODES)]
        new = []
        for j in range(4):
            pos = jnp.maximum(normal_speed(j, v0, grid(b)), 0.0)
            for k in range(6):
                new.append(carry[j * 6 + k] + pos * got[FACES[j][k]])
        return tuple(new)

    zero = jnp.zeros((8, 128), f32)
    nums = lax.fori_loop(0, 32, partial_sums, (zero,) * 24)

    def partial_dens(a, carry):
        v0 = grid(me * 8 + a)
        new = []
        for j in range(4):
            value = jnp.minimum(normal_speed(j, v0, v1), 0.0) * wall[rows(a * 8), :]
            negwall[rows((j * 8 + a) * 8), :] = value
            new.append(carry[j] - value)
        return tuple(new)

    dens = lax.fori_loop(0, 8, partial_dens, (zero,) * 4)
    mine = zero
    for i, x in enumerate(nums):
        x = x + pltpu.roll(x, 4, 0)
        mine = jnp.where(lane == i, jnp.sum(x, axis=1, keepdims=True), mine)
    for j, x in enumerate(dens):
        x = jnp.broadcast_to(jnp.sum(x, axis=0, keepdims=True), (8, 128))
        mine = jnp.where(lane == 24 + j, jnp.sum(x, axis=1, keepdims=True), mine)
    sums_out[...] = mine
    for q in range(3):
        sums(q).start()

    for i in range(8):
        x = khat[:, i * 128 : (i + 1) * 128]
        straight[i * 32 : (i + 1) * 32, :] = x
    x = straight[...]
    x0 = x.astype(jnp.bfloat16)
    x = x - x0.astype(f32)
    x1 = x.astype(jnp.bfloat16)
    x2 = (x - x1.astype(f32)).astype(jnp.bfloat16)
    rev = reverse[...]
    mirrored[...] = (
        jnp.dot(x0, rev, preferred_element_type=f32) + jnp.dot(x1, rev, preferred_element_type=f32)
    ) + jnp.dot(x2, rev, preferred_element_type=f32)
    group = lax.broadcasted_iota(jnp.int32, (32, 128), 1) // 32

    def regroup(source, place):
        total = jnp.zeros((32, 128), f32)
        for kh in range(4):
            kb = place(kh)
            tile, offset = kb // 4, kb % 4
            x = source[tile * 32 : (tile + 1) * 32, :]
            shift = (kh - offset) % 4 * 32
            if shift:
                x = pltpu.roll(x, shift, 1)
            total = jnp.where(group == kh, x, total)
        return total

    for kl in range(8):
        even = regroup(straight, lambda kh: kl + 8 * kh)
        odd = regroup(mirrored, lambda kh: (32 - kl - 8 * kh) % 32)
        moved[pl.ds(kl, 32, stride=8), :] = even
        moved[pl.ds(BLOCK + kl, 32, stride=8), :] = odd
    for ka in range(17):
        other = BLOCK + (32 - ka) % 32 * 8
        sym[ka * 8 : ka * 8 + 8, :] = 0.5 * (
            moved[ka * 8 : ka * 8 + 8, :] + moved[other : other + 8, :]
        )

    def send_halos():
        @pl.when(parity == 0)
        def _():
            pl.semaphore_wait(barrier, beside)


        up_elem = jnp.int32(0)
        down_elem = jnp.int32(0)
        for e in range(ELEMS):
            up_elem = up_elem + jnp.where(nb_side[e, 1] == 2, e, 0)
            down_elem = down_elem + jnp.where(nb_side[e, 0] == 1, e, 0)
        for side, elem, face in ((0, up_elem, 1), (1, down_elem, 0)):
            for k in range(6):
                for a in range(8):
                    halo_out[side, k * 8 + a] = pool[(elem * NODES + FACES[face][k]) * 8 + a]

            @pl.when(has_below if side else has_above)
            def _():
                halo(side).start()

    cos = twiddle[0:8, :]
    sin = twiddle[8:16, :]

    @pl.loop(0, NODES)
    def _(n):
        @pl.when(n == 3)
        def _():
            send_halos()

        for q in range(3):
            forward_in(n, q, block, pool, fwd_send, fwd_recv, partners, rows).wait_recv()
        result[rows(n * BLOCK, BLOCK), :] = collide(
            block[pl.ds(n * 32, 32)].reshape(BLOCK, 128),
            phi[...],
            sym[...],
            rows_fwd[...],
            lanes_fwd[...],
            lanes_bwd[...],
            rows_bwd[...],
            cos,
            sin,
        )
        for q in range(3):
            backward(n, q).start()

    for side, face in ((0, 1), (1, 0)):

        @pl.when(has_above if side else has_below)
        def _():
            halo(side).wait_recv()
            for k in range(6):
                start = HALO + (side * NODES + FACES[face][k]) * 8
                for a in range(8):
                    pool[start + a] = halo_in[side, k * 8 + a]

    @pl.loop(0, 8)
    def _(a):
        v0 = grid(me * 8 + a)
        negs = [jnp.minimum(normal_speed(j, v0, v1), 0.0) for j in range(4)]

        @pl.loop(0, ELEMS)
        def _(e):
            for j in range(4):
                side = nb_side[e, j]
                inner = jnp.where(side == 3, 0, 8)
                edge = TABLE + jnp.where(wall_flag[e, j] == 1, inj_id[e, j], 4) * 8
                near = nb_local[e, j] * (NODES * 8)
                far = HALO + jnp.where(side == 2, NODES * 8, 0)
                base = jnp.where(side == 3, edge, jnp.where(side == 0, near, far)) + a
                for k in range(6):
                    outer = pool[base + inner * FACES[j ^ 1][k]]
                    trace = pool[(e * NODES + FACES[j][k]) * 8 + a]
                    diff[j * 6 + k, rows(e * 8), :] = negs[j] * (trace - outer)

        @pl.loop(0, NODES // 2)
        def _(pair):
            acc = [[zero] * ELEMS for _ in range(2)]
            for m in range(NODES):
                for i in range(2):
                    n = pair * 2 + i
                    c = deriv[n, 0, m] * v0 + deriv[n, 1, m] * v1 + deriv[n, 2, m] * v2
                    for e in range(ELEMS):
                        f = pool[(e * NODES + m) * 8 + a]
                        acc[i][e] = acc[i][e] - c * f
            for j in range(4):
                for k in range(6):
                    for i in range(2):
                        c = lift[k, j, pair * 2 + i]
                        for e in range(ELEMS):
                            d = diff[j * 6 + k, e * 8 : e * 8 + 8, :]
                            acc[i][e] = acc[i][e] + c * d
            for i in range(2):
                for e in range(ELEMS):
                    moved[rows((e * NODES + pair * 2 + i) * SLAB + a * 8), :] = acc[i][e]

    total = sums_out[...]
    for q in range(3):
        sums(q).wait_recv()
    for q in range(3):
        total = total + sums_in[q]
    for j in range(4):
        mask = zero
        for e in range(ELEMS):
            on = jnp.where(nb_side[e, j] == 3, jnp.where(wall_flag[e, j] == 1, 1.0, 0.0), 0.0)
            mask = jnp.where(sub % 4 == e, on, mask)
        den = jnp.broadcast_to(total[:, 24 + j : 25 + j], (8, 128))
        sigma = [
            jnp.broadcast_to(total[:, j * 6 + k : j * 6 + k + 1], (8, 128)) / den * mask
            for k in range(6)
        ]
        for n in range(NODES):
            part = lift[0, j, n] * sigma[0]
            for k in range(1, 6):
                part = part + lift[k, j, n] * sigma[k]
            wallsum[(j * NODES + n) * 8 : (j * NODES + n) * 8 + 8, :] = part

    @pl.loop(0, ELEMS)
    def _(e):
        @pl.loop(0, NODES)
        def _(n):
            parts = [
                jnp.broadcast_to(wallsum[pl.ds((j * NODES + n) * 8 + e, 1), :], (8, 128))
                for j in range(4)
            ]
            for a in range(8):
                x = moved[rows((e * NODES + n) * SLAB + a * 8), :]
                for j in range(4):
                    x = x - parts[j] * negwall[(j * 8 + a) * 8 : (j * 8 + a) * 8 + 8, :]
                moved[rows((e * NODES + n) * SLAB + a * 8), :] = x

    @pl.loop(0, NODES)
    def _(n):
        for a in range(8):
            out[pl.ds(n * BLOCK + a * 32 + me, 8, stride=4), :] = (
                result[rows(n * BLOCK + me * SLAB + a * 8), :]
                + moved[rows((me * NODES + n) * SLAB + a * 8), :]
            )
        for q in range(3):
            backward_in(n, q, back, result, bwd_send, bwd_recv, partners, rows).wait_recv()
            e = partners[q]
            for a in range(8):
                at = rows((e * NODES + n) * SLAB + a * 8)
                out[pl.ds(n * BLOCK + a * 32 + e, 8, stride=4), :] = back[at, :] + moved[at, :]

    @pl.loop(0, NODES)
    def _(n):
        for q in range(3):
            forward(n, q).wait_send()
            backward(n, q).wait_send()

    for side in range(2):

        @pl.when(has_below if side else has_above)
        def _():
            halo(side).wait_send()

    for q in range(3):
        sums(q).wait_send()


def forward_in(n, q, block, pool, send, recv, partners, rows):
    return pltpu.make_async_remote_copy(
        src_ref=pool.at[pl.ds(0, 8)],
        dst_ref=block.at[pl.ds(n * 32 + partners[q] * 8, 8)],
        send_sem=send.at[n, q],
        recv_sem=recv.at[n, q],
        device_id={"vel": partners[q]},
    )


def backward_in(n, q, back, result, send, recv, partners, rows):
    return pltpu.make_async_remote_copy(
        src_ref=result.at[rows(0, SLAB)],
        dst_ref=back.at[rows((partners[q] * NODES + n) * SLAB, SLAB)],
        send_sem=send.at[n, q],
        recv_sem=recv.at[n, q],
        device_id={"vel": partners[q]},
    )


def solution(mesh):
    space = mesh.shape["space"]
    constants = tables()

    def local(
        dist,
        phi,
        khat,
        deriv,
        lift,
        normals,
        wall_maxw,
        free_stream,
        inject,
        nb_local,
        nb_side,
        wall_flag,
        inj_id,
    ):
        lines = dist.transpose(1, 0, 2).reshape(NODES, ELEMS, SLAB, 128)
        lines = lines.transpose(0, 2, 1, 3).reshape(NODES * BLOCK, 128)
        profiles = inject.reshape(4, SLAB, 128).transpose(1, 0, 2).reshape(BLOCK, 128)
        hbm = pl.BlockSpec(memory_space=pltpu.HBM)
        f32 = jnp.float32
        dma = pltpu.SemaphoreType.DMA

        tables = [jnp.asarray(c) for c in constants]
        operands = [
            lines,
            phi.reshape(BLOCK, 128),
            khat,
            wall_maxw.reshape(SLAB, 128),
            free_stream.reshape(SLAB, 128),
            profiles,
            *tables,
            deriv.transpose(1, 0, 2),
            lift.transpose(2, 0, 1),
            normals,
            nb_local,
            nb_side,
            wall_flag,
            inj_id,
        ]

        def body(*refs):
            kernel(space, *refs)

        rate = pl.pallas_call(
            body,
            out_shape=jax.ShapeDtypeStruct((NODES * BLOCK, 128), f32),
            in_specs=[hbm] * len(operands),
            out_specs=pl.BlockSpec(memory_space=pltpu.VMEM),
            scratch_shapes=[pltpu.VMEM(x.shape, x.dtype) for x in operands[:12]]
            + [pltpu.SMEM(x.shape, x.dtype) for x in operands[12:]]
            + [
                pltpu.VMEM((POOL, 8, 128), f32),
                pltpu.VMEM((NODES * 32, 8, 128), f32),
                pltpu.VMEM((NODES * BLOCK, 128), f32),
                pltpu.VMEM((ELEMS * NODES * SLAB, 128), f32),
                pltpu.VMEM((ELEMS * NODES * SLAB, 128), f32),
                pltpu.VMEM((24, ELEMS * 8, 128), f32),
                pltpu.VMEM((4 * SLAB, 128), f32),
                pltpu.VMEM((BLOCK, 128), f32),
                pltpu.VMEM((BLOCK, 128), f32),
                pltpu.VMEM((HALF, 128), f32),
                pltpu.VMEM((4 * NODES * 8, 128), f32),
                pltpu.VMEM((2, 6 * 8, 8, 128), f32),
                pltpu.VMEM((2, 6 * 8, 8, 128), f32),
                pltpu.VMEM((8, 128), f32),
                pltpu.VMEM((3, 8, 128), f32),
                dma((NODES,)),
                dma((len(operands) - 1,)),
                dma((NODES, 3)),
                dma((NODES, 3)),
                dma((NODES, 3)),
                dma((NODES, 3)),
                dma((2,)),
                dma((2,)),
                dma((3,)),
                dma((3,)),
            ],
            compiler_params=pltpu.CompilerParams(
                collective_id=0, has_side_effects=True, vmem_limit_bytes=40 * 2**20
            ),
            name="rate",
        )(*[pltpu.with_memory_space_constraint(x, pltpu.HBM) for x in operands])
        rate = rate.reshape(NODES, SLAB, ELEMS, 128).transpose(0, 2, 1, 3)
        return rate.reshape(NODES, ELEMS, SLAB * 128).transpose(1, 0, 2)

    return jax.shard_map(
        local,
        mesh=mesh,
        in_specs=(
            P("space", None, "vel"),
            P(),
            P(),
            P(),
            P(),
            P(),
            P("vel"),
            P("vel"),
            P(None, "vel"),
            P("space", None),
            P("space", None),
            P("space", None),
            P("space", None),
        ),
        out_specs=P("space", None, "vel"),
        check_vma=False,
    )
```

```python
import math

import jax
import jax.numpy as jnp
import numpy as np
import ml_dtypes
from jax import lax
from jax.experimental import pallas as pl
from jax.experimental.pallas import tpu as pltpu
from jax.sharding import PartitionSpec as P

FACES = ((1, 2, 3, 5, 8, 9), (0, 2, 3, 6, 7, 9), (0, 1, 3, 4, 7, 8), (0, 1, 2, 4, 5, 6))
SPEED = 3.0
NODES = 10
ELEMS = 4
GROUP = 4
SLAB = 64
BLOCK = 256
HALF = 136
PACK = 128
TABLE = ELEMS * NODES * 8
HALO = TABLE + 5 * 8
POOL = HALO + 2 * NODES * 8
LINE = 4
DIRECT = (24, 16)


def split(x):
    hi = x.astype(ml_dtypes.bfloat16)
    lo = (x - hi.astype(np.float64)).astype(ml_dtypes.bfloat16)
    return hi, lo


def tables():
    turn = 2.0 * np.pi
    ka = np.repeat(np.arange(17), 8)
    kl = np.tile(np.arange(8), 17)
    a = np.repeat(np.arange(32), 8)
    bh = np.tile(np.arange(8), 32)
    bl = np.repeat(np.arange(4), 32)
    c = np.tile(np.arange(32), 4)
    angle = turn * ((np.outer(ka, a) % 32) / 32.0 + (np.outer(kl, bh) % 8) / 8.0)
    rows_fwd = np.concatenate([np.cos(angle), -np.sin(angle)], axis=0)
    angle = turn * ((np.outer(bl, bl) % 4) / 4.0 + (np.outer(c, c) % 32) / 32.0)
    co, si = np.cos(angle), np.sin(angle)
    lanes_fwd = np.concatenate(
        [np.concatenate([co, -si], axis=1), np.concatenate([si, co], axis=1)], axis=0
    )
    lanes_bwd = np.concatenate(
        [np.concatenate([co, si], axis=1), np.concatenate([-si, co], axis=1)], axis=0
    )
    angle = turn * ((np.outer(a, ka[:PACK]) % 32) / 32.0 + (np.outer(bh, kl[:PACK]) % 8) / 8.0)
    re, im = 2.0 * np.cos(angle), -2.0 * np.sin(angle)
    sign = np.where(a % 2 == 0, 1.0, -1.0)[:, None]
    angle = turn * ((np.outer(bh, np.arange(8)) % 8) / 8.0)
    re[:, :8] = np.cos(angle) + sign * np.sin(angle)
    im[:, :8] = -np.sin(angle) + sign * np.cos(angle)
    rows_bwd = np.concatenate([re, im], axis=1) * 2.0**-15

    def left(x):
        hi, lo = split(x)
        return np.concatenate([hi, hi, lo], axis=1)

    def right(x):
        hi, lo = split(x)
        return np.concatenate([hi, hi, lo], axis=0)

    angle = turn * np.outer(np.arange(8), bl) / 32.0
    twiddle = np.concatenate([np.cos(angle), np.sin(angle)], axis=0).astype(np.float32)
    lane = np.arange(128)
    mirror = (lane // 32) * 32 + (32 - lane % 32) % 32
    reverse = (lane[:, None] == mirror[None, :]).astype(ml_dtypes.bfloat16)
    return (left(rows_fwd), right(lanes_fwd), right(lanes_bwd), left(rows_bwd), twiddle, reverse)


def halves(x):
    hi = x.astype(jnp.bfloat16)
    lo = (x - hi.astype(jnp.float32)).astype(jnp.bfloat16)
    return hi, lo


def dot_left(table, x):
    hi, lo = halves(x)
    return jnp.dot(
        table, jnp.concatenate([hi, lo, hi], axis=0), preferred_element_type=jnp.float32
    )


def dot_right(x, table):
    hi, lo = halves(x)
    return jnp.dot(
        jnp.concatenate([hi, lo, hi], axis=1), table, preferred_element_type=jnp.float32
    )


def by_rows(x, y):
    return jnp.concatenate([x, y], axis=0)


def by_lanes(x, y):
    return jnp.concatenate([x, y], axis=1)


def turned(re, im, cos, sin):
    count = re.shape[0] // 8
    re = re.reshape(count, 8, 128)
    im = im.reshape(count, 8, 128)
    out_re = re * cos[None] - im * sin[None]
    out_im = re * sin[None] + im * cos[None]
    return out_re.reshape(count * 8, 128), out_im.reshape(count * 8, 128)


def collide(x, phi, sym, rows_fwd, lanes_fwd, lanes_bwd, rows_bwd, cos, sin):
    y = dot_left(rows_fwd, by_lanes(x * phi, x))
    wr, wi = turned(y[:HALF, :128], y[HALF:, :128], cos, -sin)
    fr, fi = turned(y[:HALF, 128:], y[HALF:, 128:], cos, -sin)
    s = dot_right(by_rows(by_lanes(wr, wi), by_lanes(fr, fi)), lanes_fwd)
    wr, wi, fr, fi = s[:HALF, :128], s[:HALF, 128:], s[HALF:, :128], s[HALF:, 128:]
    wr, wi = wr * 2.0**-15, wi * 2.0**-15

    def packed(re, im):
        first = re[:8] - im[PACK:]
        second = im[:8] + re[PACK:]
        return by_lanes(by_rows(first, re[8:PACK]), by_rows(second, im[8:PACK]))

    gain = packed(wr * fr - wi * fi, wr * fi + wi * fr)
    loss = packed(sym * fr, sym * fi)
    b = dot_right(by_rows(gain, loss), lanes_bwd)
    gr, gi = turned(b[:PACK, :128], b[:PACK, 128:], cos, sin)
    lr, li = turned(b[PACK:, :128], b[PACK:, 128:], cos, sin)
    z = dot_left(rows_bwd, by_rows(by_lanes(gr, lr), by_lanes(gi, li)))
    return z[:, :128] - x * z[:, 128:]


def kernel(
    space,
    dist_in,
    phi_in,
    khat_in,
    wall_in,
    free_in,
    inject_in,
    rows_fwd_in,
    lanes_fwd_in,
    lanes_bwd_in,
    rows_bwd_in,
    twiddle_in,
    reverse_in,
    deriv_in,
    lift_in,
    normals_in,
    nb_local_in,
    nb_side_in,
    wall_flag_in,
    inj_id_in,
    out,
    dist,
    phi,
    khat,
    wall,
    free,
    inject,
    rows_fwd,
    lanes_fwd,
    lanes_bwd,
    rows_bwd,
    twiddle,
    reverse,
    deriv,
    lift,
    normals,
    nb_local,
    nb_side,
    wall_flag,
    inj_id,
    pool,
    block,
    result,
    back,
    moved,
    diff,
    negwall,
    straight,
    mirrored,
    sym,
    wallsum,
    halo_out,
    halo_in,
    relay,
    sums_out,
    sums_in,
    dist_sem,
    load_sem,
    fwd_send,
    fwd_recv,
    bwd_send,
    bwd_recv,
    halo_send,
    halo_recv,
    relay_send,
    relay_recv,
    relay_ready,
    sums_send,
    sums_recv,
):
    f32 = jnp.float32
    me = lax.axis_index("vel")
    here = lax.axis_index("space")
    parity = lax.rem(here, 2)
    has_above = here < space - 1
    has_below = here > 0
    place = lax.rem(here, LINE)
    turn_up = (place == LINE - 1) & has_above
    turn_down = (place == 0) & has_below
    relay_up = (place == 1) & (here > LINE)
    relay_down = (place == LINE - 2) & (here < space - LINE)
    beside = jnp.where(has_above, 1, 0) + jnp.where(has_below, 1, 0)
    core = lax.rem(me, 2)
    flip = 1 - 2 * core
    across = lax.rem(me + 2, GROUP)
    partners = (across, across + flip, me + flip)

    def rows(start, count=8):
        return pl.ds(pl.multiple_of(start, 8), count)

    def forward(n, q):
        to = partners[q]
        return pltpu.make_async_remote_copy(
            src_ref=pool.at[pl.ds((to * NODES + n) * 8, 8)],
            dst_ref=block.at[pl.ds(n * 32 + me * 8, 8)],
            send_sem=fwd_send.at[n, q],
            recv_sem=fwd_recv.at[n, q],
            device_id={"vel": to},
        )

    def backward(n, q):
        to = partners[q]
        return pltpu.make_async_remote_copy(
            src_ref=result.at[rows(n * BLOCK + to * SLAB, SLAB)],
            dst_ref=back.at[rows((me * NODES + n) * SLAB, SLAB)],
            send_sem=bwd_send.at[n, q],
            recv_sem=bwd_recv.at[n, q],
            device_id={"vel": to},
        )

    def halo(side, count=48):
        return pltpu.make_async_remote_copy(
            src_ref=halo_out.at[side, pl.ds(0, count)],
            dst_ref=halo_in.at[side, pl.ds(0, count)],
            send_sem=halo_send.at[side],
            recv_sem=halo_recv.at[side],
            device_id={"space": lax.rem(here + (space - 1 if side else 1), space)},
        )

    def detour(side):
        first = DIRECT[side]
        return pltpu.make_async_remote_copy(
            src_ref=halo_out.at[side, pl.ds(first, 48 - first)],
            dst_ref=relay.at[pl.ds(0, 48 - first)],
            send_sem=relay_send.at[0],
            recv_sem=relay_recv.at[0],
            device_id={"space": lax.rem(here + (space - 2 if side else 2), space)},
        )

    def passed(side):
        first = DIRECT[side]
        return pltpu.make_async_remote_copy(
            src_ref=relay.at[pl.ds(0, 48 - first)],
            dst_ref=halo_in.at[side, pl.ds(first, 48 - first)],
            send_sem=relay_send.at[1],
            recv_sem=relay_recv.at[1],
            device_id={"space": lax.rem(here + (1 if side else space - 1), space)},
        )

    def sums(q):
        return pltpu.make_async_remote_copy(
            src_ref=sums_out,
            dst_ref=sums_in.at[q],
            send_sem=sums_send.at[q],
            recv_sem=sums_recv.at[q],
            device_id={"vel": partners[q]},
        )

    def dist_load(n):
        part = rows(n * BLOCK, BLOCK)
        return pltpu.make_async_copy(dist_in.at[part], dist.at[part], dist_sem.at[n])

    pairs = (
        (nb_side_in, nb_side),
        (inject_in, inject),
        (free_in, free),
        (normals_in, normals),
        (wall_in, wall),
        (khat_in, khat),
        (reverse_in, reverse),
        (nb_local_in, nb_local),
        (wall_flag_in, wall_flag),
        (inj_id_in, inj_id),
        (deriv_in, deriv),
        (lift_in, lift),
        (phi_in, phi),
        (rows_fwd_in, rows_fwd),
        (lanes_fwd_in, lanes_fwd),
        (twiddle_in, twiddle),
        (lanes_bwd_in, lanes_bwd),
        (rows_bwd_in, rows_bwd),
    )
    loads = [
        pltpu.make_async_copy(source, target, load_sem.at[i])
        for i, (source, target) in enumerate(pairs)
    ]

    barrier = pltpu.get_barrier_semaphore()
    for to in partners:
        pl.semaphore_signal(barrier, inc=1, device_id={"vel": to})
    for n in range(NODES):
        dist_load(n).start()
    for load in loads:
        load.start()

    def greet():
        @pl.when(has_above)
        def _():
            pl.semaphore_signal(barrier, inc=1, device_id={"space": here + 1})

        @pl.when(has_below)
        def _():
            pl.semaphore_signal(barrier, inc=1, device_id={"space": here - 1})

    @pl.when(parity == 1)
    def _():
        pl.semaphore_wait(barrier, 3 + beside)

    @pl.when(parity == 0)
    def _():
        pl.semaphore_wait(barrier, 3)

    greet()

    @pl.loop(0, NODES)
    def _(n):
        dist_load(n).wait()
        for e in range(ELEMS):
            for a in range(8):
                pool[(e * NODES + n) * 8 + a] = dist[
                    pl.ds(n * BLOCK + a * 32 + e, 8, stride=4), :
                ]
        for q in range(3):
            forward(n, q).start()
        for a in range(8):
            block[n * 32 + me * 8 + a] = pool[(me * NODES + n) * 8 + a]

    for load in loads:
        load.wait()

    for q in range(4):
        for a in range(8):
            pool[TABLE + q * 8 + a] = inject[pl.ds(a * 32 + q, 8, stride=4), :]
    for a in range(8):
        pool[TABLE + 32 + a] = free[a * 8 : a * 8 + 8, :]

    sub = lax.broadcasted_iota(jnp.int32, (8, 128), 0)
    lane = lax.broadcasted_iota(jnp.int32, (8, 128), 1)

    def grid(i):
        return SPEED * ((2.0 * i.astype(f32) + 1.0) / 32.0 - 1.0)

    v2 = grid(lane % 32)
    v1 = grid(sub * 4 + lane // 32)

    def normal_speed(j, v0, v1):
        return normals[j, 0] * v0 + normals[j, 1] * v1 + normals[j, 2] * v2

    def partial_sums(i, carry):
        a = i // 4
        v0 = grid(me * 8 + a)
        b = (lax.rem(i, 4) * 2 + sub // 4) * 4 + lane // 32
        got = [dist[rows(n * BLOCK + i * 8), :] for n in range(NODES)]
        new = []
        for j in range(4):
            pos = jnp.maximum(normal_speed(j, v0, grid(b)), 0.0)
            for k in range(6):
                new.append(carry[j * 6 + k] + pos * got[FACES[j][k]])
        return tuple(new)

    zero = jnp.zeros((8, 128), f32)
    nums = lax.fori_loop(0, 32, partial_sums, (zero,) * 24)

    def partial_dens(a, carry):
        v0 = grid(me * 8 + a)
        new = []
        for j in range(4):
            value = jnp.minimum(normal_speed(j, v0, v1), 0.0) * wall[rows(a * 8), :]
            negwall[rows((j * 8 + a) * 8), :] = value
            new.append(carry[j] - value)
        return tuple(new)

    dens = lax.fori_loop(0, 8, partial_dens, (zero,) * 4)
    mine = zero
    for i, x in enumerate(nums):
        x = x + pltpu.roll(x, 4, 0)
        mine = jnp.where(lane == i, jnp.sum(x, axis=1, keepdims=True), mine)
    for j, x in enumerate(dens):
        x = jnp.broadcast_to(jnp.sum(x, axis=0, keepdims=True), (8, 128))
        mine = jnp.where(lane == 24 + j, jnp.sum(x, axis=1, keepdims=True), mine)
    sums_out[...] = mine
    for q in range(3):
        sums(q).start()

    for i in range(8):
        x = khat[:, i * 128 : (i + 1) * 128]
        straight[i * 32 : (i + 1) * 32, :] = x
    x = straight[...]
    x0 = x.astype(jnp.bfloat16)
    x = x - x0.astype(f32)
    x1 = x.astype(jnp.bfloat16)
    x2 = (x - x1.astype(f32)).astype(jnp.bfloat16)
    rev = reverse[...]
    mirrored[...] = (
        jnp.dot(x0, rev, preferred_element_type=f32) + jnp.dot(x1, rev, preferred_element_type=f32)
    ) + jnp.dot(x2, rev, preferred_element_type=f32)
    group = lax.broadcasted_iota(jnp.int32, (32, 128), 1) // 32

    def regroup(source, place):
        total = jnp.zeros((32, 128), f32)
        for kh in range(4):
            kb = place(kh)
            tile, offset = kb // 4, kb % 4
            x = source[tile * 32 : (tile + 1) * 32, :]
            shift = (kh - offset) % 4 * 32
            if shift:
                x = pltpu.roll(x, shift, 1)
            total = jnp.where(group == kh, x, total)
        return total

    for kl in range(8):
        even = regroup(straight, lambda kh: kl + 8 * kh)
        odd = regroup(mirrored, lambda kh: (32 - kl - 8 * kh) % 32)
        moved[pl.ds(kl, 32, stride=8), :] = even
        moved[pl.ds(BLOCK + kl, 32, stride=8), :] = odd
    for ka in range(17):
        other = BLOCK + (32 - ka) % 32 * 8
        sym[ka * 8 : ka * 8 + 8, :] = 0.5 * (
            moved[ka * 8 : ka * 8 + 8, :] + moved[other : other + 8, :]
        )

    def send_halos():
        @pl.when(parity == 0)
        def _():
            pl.semaphore_wait(barrier, beside)

        @pl.when(turn_down)
        def _():
            pl.semaphore_signal(relay_ready, inc=1, device_id={"space": here - 1})

        @pl.when(turn_up)
        def _():
            pl.semaphore_signal(relay_ready, inc=1, device_id={"space": here + 1})

        up_elem = jnp.int32(0)
        down_elem = jnp.int32(0)
        for e in range(ELEMS):
            up_elem = up_elem + jnp.where(nb_side[e, 1] == 2, e, 0)
            down_elem = down_elem + jnp.where(nb_side[e, 0] == 1, e, 0)
        for side, elem, face in ((0, up_elem, 1), (1, down_elem, 0)):
            for k in range(6):
                for a in range(8):
                    halo_out[side, k * 8 + a] = pool[(elem * NODES + FACES[face][k]) * 8 + a]

            turn = turn_down if side else turn_up
            straight_on = (has_below if side else has_above) & jnp.logical_not(turn)

            @pl.when(straight_on)
            def _():
                halo(side).start()

            @pl.when(turn)
            def _():
                halo(side, DIRECT[side]).start()
                pl.semaphore_wait(relay_ready, 1)
                detour(side).start()

    cos = twiddle[0:8, :]
    sin = twiddle[8:16, :]

    @pl.loop(0, NODES)
    def _(n):
        @pl.when(n == 3)
        def _():
            send_halos()

        for q in range(3):
            forward_in(n, q, block, pool, fwd_send, fwd_recv, partners, rows).wait_recv()
        result[rows(n * BLOCK, BLOCK), :] = collide(
            block[pl.ds(n * 32, 32)].reshape(BLOCK, 128),
            phi[...],
            sym[...],
            rows_fwd[...],
            lanes_fwd[...],
            lanes_bwd[...],
            rows_bwd[...],
            cos,
            sin,
        )
        for q in range(3):
            backward(n, q).start()

    for side in range(2):

        @pl.when(relay_down if side else relay_up)
        def _():
            detour(side).wait_recv()
            passed(side).start()

    total = sums_out[...]
    for q in range(3):
        sums(q).wait_recv()
    for q in range(3):
        total = total + sums_in[q]
    for j in range(4):
        mask = zero
        for e in range(ELEMS):
            on = jnp.where(nb_side[e, j] == 3, jnp.where(wall_flag[e, j] == 1, 1.0, 0.0), 0.0)
            mask = jnp.where(sub % 4 == e, on, mask)
        den = jnp.broadcast_to(total[:, 24 + j : 25 + j], (8, 128))
        sigma = [
            jnp.broadcast_to(total[:, j * 6 + k : j * 6 + k + 1], (8, 128)) / den * mask
            for k in range(6)
        ]
        for n in range(NODES):
            part = lift[0, j, n] * sigma[0]
            for k in range(1, 6):
                part = part + lift[k, j, n] * sigma[k]
            wallsum[(j * NODES + n) * 8 : (j * NODES + n) * 8 + 8, :] = part

    for side, face in ((0, 1), (1, 0)):

        turn = turn_up if side else turn_down
        here_in = has_above if side else has_below

        @pl.when(here_in & jnp.logical_not(turn))
        def _():
            halo(side).wait_recv()

        @pl.when(turn)
        def _():
            halo(side, DIRECT[side]).wait_recv()
            passed(side).wait_recv()

        @pl.when(here_in)
        def _():
            for k in range(6):
                start = HALO + (side * NODES + FACES[face][k]) * 8
                for a in range(8):
                    pool[start + a] = halo_in[side, k * 8 + a]

    @pl.loop(0, 8)
    def _(a):
        v0 = grid(me * 8 + a)
        negs = [jnp.minimum(normal_speed(j, v0, v1), 0.0) for j in range(4)]

        @pl.loop(0, ELEMS)
        def _(e):
            for j in range(4):
                side = nb_side[e, j]
                inner = jnp.where(side == 3, 0, 8)
                edge = TABLE + jnp.where(wall_flag[e, j] == 1, inj_id[e, j], 4) * 8
                near = nb_local[e, j] * (NODES * 8)
                far = HALO + jnp.where(side == 2, NODES * 8, 0)
                base = jnp.where(side == 3, edge, jnp.where(side == 0, near, far)) + a
                for k in range(6):
                    outer = pool[base + inner * FACES[j ^ 1][k]]
                    trace = pool[(e * NODES + FACES[j][k]) * 8 + a]
                    diff[j * 6 + k, rows(e * 8), :] = negs[j] * (trace - outer)

        @pl.loop(0, NODES // 2)
        def _(pair):
            acc = [[zero] * ELEMS for _ in range(2)]
            for m in range(NODES):
                for i in range(2):
                    n = pair * 2 + i
                    c = deriv[n, 0, m] * v0 + deriv[n, 1, m] * v1 + deriv[n, 2, m] * v2
                    for e in range(ELEMS):
                        f = pool[(e * NODES + m) * 8 + a]
                        acc[i][e] = acc[i][e] - c * f
            for j in range(4):
                for k in range(6):
                    for i in range(2):
                        c = lift[k, j, pair * 2 + i]
                        for e in range(ELEMS):
                            d = diff[j * 6 + k, e * 8 : e * 8 + 8, :]
                            acc[i][e] = acc[i][e] + c * d
            for i in range(2):
                for e in range(ELEMS):
                    moved[rows((e * NODES + pair * 2 + i) * SLAB + a * 8), :] = acc[i][e]

    @pl.loop(0, ELEMS)
    def _(e):
        @pl.loop(0, NODES)
        def _(n):
            parts = [
                jnp.broadcast_to(wallsum[pl.ds((j * NODES + n) * 8 + e, 1), :], (8, 128))
                for j in range(4)
            ]
            for a in range(8):
                x = moved[rows((e * NODES + n) * SLAB + a * 8), :]
                for j in range(4):
                    x = x - parts[j] * negwall[(j * 8 + a) * 8 : (j * 8 + a) * 8 + 8, :]
                moved[rows((e * NODES + n) * SLAB + a * 8), :] = x

    @pl.loop(0, NODES)
    def _(n):
        for a in range(8):
            out[pl.ds(n * BLOCK + a * 32 + me, 8, stride=4), :] = (
                result[rows(n * BLOCK + me * SLAB + a * 8), :]
                + moved[rows((me * NODES + n) * SLAB + a * 8), :]
            )
        for q in range(3):
            backward_in(n, q, back, result, bwd_send, bwd_recv, partners, rows).wait_recv()
            e = partners[q]
            for a in range(8):
                at = rows((e * NODES + n) * SLAB + a * 8)
                out[pl.ds(n * BLOCK + a * 32 + e, 8, stride=4), :] = back[at, :] + moved[at, :]

    @pl.loop(0, NODES)
    def _(n):
        for q in range(3):
            forward(n, q).wait_send()
            backward(n, q).wait_send()

    for side in range(2):
        turn = turn_down if side else turn_up
        straight_on = (has_below if side else has_above) & jnp.logical_not(turn)

        @pl.when(straight_on)
        def _():
            halo(side).wait_send()

        @pl.when(turn)
        def _():
            halo(side, DIRECT[side]).wait_send()
            detour(side).wait_send()

        @pl.when(relay_down if side else relay_up)
        def _():
            passed(side).wait_send()

    for q in range(3):
        sums(q).wait_send()


def forward_in(n, q, block, pool, send, recv, partners, rows):
    return pltpu.make_async_remote_copy(
        src_ref=pool.at[pl.ds(0, 8)],
        dst_ref=block.at[pl.ds(n * 32 + partners[q] * 8, 8)],
        send_sem=send.at[n, q],
        recv_sem=recv.at[n, q],
        device_id={"vel": partners[q]},
    )


def backward_in(n, q, back, result, send, recv, partners, rows):
    return pltpu.make_async_remote_copy(
        src_ref=result.at[rows(0, SLAB)],
        dst_ref=back.at[rows((partners[q] * NODES + n) * SLAB, SLAB)],
        send_sem=send.at[n, q],
        recv_sem=recv.at[n, q],
        device_id={"vel": partners[q]},
    )


def solution(mesh):
    space = mesh.shape["space"]
    constants = tables()

    def local(
        dist,
        phi,
        khat,
        deriv,
        lift,
        normals,
        wall_maxw,
        free_stream,
        inject,
        nb_local,
        nb_side,
        wall_flag,
        inj_id,
    ):
        lines = dist.transpose(1, 0, 2).reshape(NODES, ELEMS, SLAB, 128)
        lines = lines.transpose(0, 2, 1, 3).reshape(NODES * BLOCK, 128)
        profiles = inject.reshape(4, SLAB, 128).transpose(1, 0, 2).reshape(BLOCK, 128)
        hbm = pl.BlockSpec(memory_space=pltpu.HBM)
        f32 = jnp.float32
        dma = pltpu.SemaphoreType.DMA

        tables = [jnp.asarray(c) for c in constants]
        operands = [
            lines,
            phi.reshape(BLOCK, 128),
            khat,
            wall_maxw.reshape(SLAB, 128),
            free_stream.reshape(SLAB, 128),
            profiles,
            *tables,
            deriv.transpose(1, 0, 2),
            lift.transpose(2, 0, 1),
            normals,
            nb_local,
            nb_side,
            wall_flag,
            inj_id,
        ]

        def body(*refs):
            kernel(space, *refs)

        rate = pl.pallas_call(
            body,
            out_shape=jax.ShapeDtypeStruct((NODES * BLOCK, 128), f32),
            in_specs=[hbm] * len(operands),
            out_specs=pl.BlockSpec(memory_space=pltpu.VMEM),
            scratch_shapes=[pltpu.VMEM(x.shape, x.dtype) for x in operands[:12]]
            + [pltpu.SMEM(x.shape, x.dtype) for x in operands[12:]]
            + [
                pltpu.VMEM((POOL, 8, 128), f32),
                pltpu.VMEM((NODES * 32, 8, 128), f32),
                pltpu.VMEM((NODES * BLOCK, 128), f32),
                pltpu.VMEM((ELEMS * NODES * SLAB, 128), f32),
                pltpu.VMEM((ELEMS * NODES * SLAB, 128), f32),
                pltpu.VMEM((24, ELEMS * 8, 128), f32),
                pltpu.VMEM((4 * SLAB, 128), f32),
                pltpu.VMEM((BLOCK, 128), f32),
                pltpu.VMEM((BLOCK, 128), f32),
                pltpu.VMEM((HALF, 128), f32),
                pltpu.VMEM((4 * NODES * 8, 128), f32),
                pltpu.VMEM((2, 6 * 8, 8, 128), f32),
                pltpu.VMEM((2, 6 * 8, 8, 128), f32),
                pltpu.VMEM((6 * 8, 8, 128), f32),
                pltpu.VMEM((8, 128), f32),
                pltpu.VMEM((3, 8, 128), f32),
                dma((NODES,)),
                dma((len(operands) - 1,)),
                dma((NODES, 3)),
                dma((NODES, 3)),
                dma((NODES, 3)),
                dma((NODES, 3)),
                dma((2,)),
                dma((2,)),
                dma((2,)),
                dma((2,)),
                pltpu.SemaphoreType.REGULAR,
                dma((3,)),
                dma((3,)),
            ],
            compiler_params=pltpu.CompilerParams(
                collective_id=0, has_side_effects=True, vmem_limit_bytes=40 * 2**20
            ),
            name="rate",
        )(*[pltpu.with_memory_space_constraint(x, pltpu.HBM) for x in operands])
        rate = rate.reshape(NODES, SLAB, ELEMS, 128).transpose(0, 2, 1, 3)
        return rate.reshape(NODES, ELEMS, SLAB * 128).transpose(1, 0, 2)

    return jax.shard_map(
        local,
        mesh=mesh,
        in_specs=(
            P("space", None, "vel"),
            P(),
            P(),
            P(),
            P(),
            P(),
            P("vel"),
            P("vel"),
            P(None, "vel"),
            P("space", None),
            P("space", None),
            P("space", None),
            P("space", None),
        ),
        out_specs=P("space", None, "vel"),
        check_vma=False,
    )
```

```python
import math

import jax
import jax.numpy as jnp
import numpy as np
import ml_dtypes
from jax import lax
from jax.experimental import pallas as pl
from jax.experimental.pallas import tpu as pltpu
from jax.sharding import PartitionSpec as P

FACES = ((1, 2, 3, 5, 8, 9), (0, 2, 3, 6, 7, 9), (0, 1, 3, 4, 7, 8), (0, 1, 2, 4, 5, 6))
SPEED = 3.0
NODES = 10
ELEMS = 4
GROUP = 4
SLAB = 64
BLOCK = 256
HALF = 136
PACK = 128
TABLE = ELEMS * NODES * 8
HALO = TABLE + 5 * 8
POOL = HALO + 2 * NODES * 8
LINE = 4
DIRECT = (24, 24)


def split(x):
    hi = x.astype(ml_dtypes.bfloat16)
    lo = (x - hi.astype(np.float64)).astype(ml_dtypes.bfloat16)
    return hi, lo


def tables():
    turn = 2.0 * np.pi
    ka = np.repeat(np.arange(17), 8)
    kl = np.tile(np.arange(8), 17)
    a = np.repeat(np.arange(32), 8)
    bh = np.tile(np.arange(8), 32)
    bl = np.repeat(np.arange(4), 32)
    c = np.tile(np.arange(32), 4)
    angle = turn * ((np.outer(ka, a) % 32) / 32.0 + (np.outer(kl, bh) % 8) / 8.0)
    rows_fwd = np.concatenate([np.cos(angle), -np.sin(angle)], axis=0)
    angle = turn * ((np.outer(bl, bl) % 4) / 4.0 + (np.outer(c, c) % 32) / 32.0)
    co, si = np.cos(angle), np.sin(angle)
    lanes_fwd = np.concatenate(
        [np.concatenate([co, -si], axis=1), np.concatenate([si, co], axis=1)], axis=0
    )
    lanes_bwd = np.concatenate(
        [np.concatenate([co, si], axis=1), np.concatenate([-si, co], axis=1)], axis=0
    )
    angle = turn * ((np.outer(a, ka[:PACK]) % 32) / 32.0 + (np.outer(bh, kl[:PACK]) % 8) / 8.0)
    re, im = 2.0 * np.cos(angle), -2.0 * np.sin(angle)
    sign = np.where(a % 2 == 0, 1.0, -1.0)[:, None]
    angle = turn * ((np.outer(bh, np.arange(8)) % 8) / 8.0)
    re[:, :8] = np.cos(angle) + sign * np.sin(angle)
    im[:, :8] = -np.sin(angle) + sign * np.cos(angle)
    rows_bwd = np.concatenate([re, im], axis=1) * 2.0**-15

    def left(x):
        hi, lo = split(x)
        return np.concatenate([hi, hi, lo], axis=1)

    def right(x):
        hi, lo = split(x)
        return np.concatenate([hi, hi, lo], axis=0)

    angle = turn * np.outer(np.arange(8), bl) / 32.0
    twiddle = np.concatenate([np.cos(angle), np.sin(angle)], axis=0).astype(np.float32)
    lane = np.arange(128)
    mirror = (lane // 32) * 32 + (32 - lane % 32) % 32
    reverse = (lane[:, None] == mirror[None, :]).astype(ml_dtypes.bfloat16)
    return (left(rows_fwd), right(lanes_fwd), right(lanes_bwd), left(rows_bwd), twiddle, reverse)


def halves(x):
    hi = x.astype(jnp.bfloat16)
    lo = (x - hi.astype(jnp.float32)).astype(jnp.bfloat16)
    return hi, lo


def dot_left(table, x):
    hi, lo = halves(x)
    return jnp.dot(
        table, jnp.concatenate([hi, lo, hi], axis=0), preferred_element_type=jnp.float32
    )


def dot_right(x, table):
    hi, lo = halves(x)
    return jnp.dot(
        jnp.concatenate([hi, lo, hi], axis=1), table, preferred_element_type=jnp.float32
    )


def by_rows(x, y):
    return jnp.concatenate([x, y], axis=0)


def by_lanes(x, y):
    return jnp.concatenate([x, y], axis=1)


def turned(re, im, cos, sin):
    count = re.shape[0] // 8
    re = re.reshape(count, 8, 128)
    im = im.reshape(count, 8, 128)
    out_re = re * cos[None] - im * sin[None]
    out_im = re * sin[None] + im * cos[None]
    return out_re.reshape(count * 8, 128), out_im.reshape(count * 8, 128)


def collide(x, phi, sym, rows_fwd, lanes_fwd, lanes_bwd, rows_bwd, cos, sin):
    y = dot_left(rows_fwd, by_lanes(x * phi, x))
    wr, wi = turned(y[:HALF, :128], y[HALF:, :128], cos, -sin)
    fr, fi = turned(y[:HALF, 128:], y[HALF:, 128:], cos, -sin)
    s = dot_right(by_rows(by_lanes(wr, wi), by_lanes(fr, fi)), lanes_fwd)
    wr, wi, fr, fi = s[:HALF, :128], s[:HALF, 128:], s[HALF:, :128], s[HALF:, 128:]
    wr, wi = wr * 2.0**-15, wi * 2.0**-15

    def packed(re, im):
        first = re[:8] - im[PACK:]
        second = im[:8] + re[PACK:]
        return by_lanes(by_rows(first, re[8:PACK]), by_rows(second, im[8:PACK]))

    gain = packed(wr * fr - wi * fi, wr * fi + wi * fr)
    loss = packed(sym * fr, sym * fi)
    b = dot_right(by_rows(gain, loss), lanes_bwd)
    gr, gi = turned(b[:PACK, :128], b[:PACK, 128:], cos, sin)
    lr, li = turned(b[PACK:, :128], b[PACK:, 128:], cos, sin)
    z = dot_left(rows_bwd, by_rows(by_lanes(gr, lr), by_lanes(gi, li)))
    return z[:, :128] - x * z[:, 128:]


def kernel(
    space,
    dist_in,
    phi_in,
    khat_in,
    wall_in,
    free_in,
    inject_in,
    rows_fwd_in,
    lanes_fwd_in,
    lanes_bwd_in,
    rows_bwd_in,
    twiddle_in,
    reverse_in,
    deriv_in,
    lift_in,
    normals_in,
    nb_local_in,
    nb_side_in,
    wall_flag_in,
    inj_id_in,
    out,
    dist,
    phi,
    khat,
    wall,
    free,
    inject,
    rows_fwd,
    lanes_fwd,
    lanes_bwd,
    rows_bwd,
    twiddle,
    reverse,
    deriv,
    lift,
    normals,
    nb_local,
    nb_side,
    wall_flag,
    inj_id,
    pool,
    block,
    result,
    back,
    moved,
    diff,
    negwall,
    straight,
    mirrored,
    sym,
    wallsum,
    halo_out,
    halo_in,
    relay,
    sums_out,
    sums_in,
    dist_sem,
    load_sem,
    fwd_send,
    fwd_recv,
    bwd_send,
    bwd_recv,
    halo_send,
    halo_recv,
    relay_send,
    relay_recv,
    relay_ready,
    sums_send,
    sums_recv,
):
    f32 = jnp.float32
    me = lax.axis_index("vel")
    here = lax.axis_index("space")
    has_above = here < space - 1
    has_below = here > 0
    place = lax.rem(here, LINE)
    turn_up = (place == LINE - 1) & has_above
    turn_down = (place == 0) & has_below
    relay_up = (place == 1) & (here > LINE)
    relay_down = (place == LINE - 2) & (here < space - LINE)
    beside = jnp.where(has_above, 1, 0) + jnp.where(has_below, 1, 0)
    core = lax.rem(me, 2)
    parity = lax.rem(here + core + 1, 2)
    flip = 1 - 2 * core
    across = lax.rem(me + 2, GROUP)
    partners = (across, across + flip, me + flip)

    def rows(start, count=8):
        return pl.ds(pl.multiple_of(start, 8), count)

    def forward(n, q):
        to = partners[q]
        return pltpu.make_async_remote_copy(
            src_ref=pool.at[pl.ds((to * NODES + n) * 8, 8)],
            dst_ref=block.at[pl.ds(n * 32 + me * 8, 8)],
            send_sem=fwd_send.at[n, q],
            recv_sem=fwd_recv.at[n, q],
            device_id={"vel": to},
        )

    def backward(n, q):
        to = partners[q]
        return pltpu.make_async_remote_copy(
            src_ref=result.at[rows(n * BLOCK + to * SLAB, SLAB)],
            dst_ref=back.at[rows((me * NODES + n) * SLAB, SLAB)],
            send_sem=bwd_send.at[n, q],
            recv_sem=bwd_recv.at[n, q],
            device_id={"vel": to},
        )

    def halo(side, count=48):
        return pltpu.make_async_remote_copy(
            src_ref=halo_out.at[side, pl.ds(0, count)],
            dst_ref=halo_in.at[side, pl.ds(0, count)],
            send_sem=halo_send.at[side],
            recv_sem=halo_recv.at[side],
            device_id={"space": lax.rem(here + (space - 1 if side else 1), space)},
        )

    def detour(side):
        first = DIRECT[side]
        return pltpu.make_async_remote_copy(
            src_ref=halo_out.at[side, pl.ds(first, 48 - first)],
            dst_ref=relay.at[pl.ds(0, 48 - first)],
            send_sem=relay_send.at[0],
            recv_sem=relay_recv.at[0],
            device_id={"space": lax.rem(here + (space - 2 if side else 2), space)},
        )

    def passed(side):
        first = DIRECT[side]
        return pltpu.make_async_remote_copy(
            src_ref=relay.at[pl.ds(0, 48 - first)],
            dst_ref=halo_in.at[side, pl.ds(first, 48 - first)],
            send_sem=relay_send.at[1],
            recv_sem=relay_recv.at[1],
            device_id={"space": lax.rem(here + (1 if side else space - 1), space)},
        )

    def sums(q):
        return pltpu.make_async_remote_copy(
            src_ref=sums_out,
            dst_ref=sums_in.at[q],
            send_sem=sums_send.at[q],
            recv_sem=sums_recv.at[q],
            device_id={"vel": partners[q]},
        )

    def dist_load(n):
        part = rows(n * BLOCK, BLOCK)
        return pltpu.make_async_copy(dist_in.at[part], dist.at[part], dist_sem.at[n])

    pairs = (
        (nb_side_in, nb_side),
        (inject_in, inject),
        (free_in, free),
        (normals_in, normals),
        (wall_in, wall),
        (khat_in, khat),
        (reverse_in, reverse),
        (nb_local_in, nb_local),
        (wall_flag_in, wall_flag),
        (inj_id_in, inj_id),
        (deriv_in, deriv),
        (lift_in, lift),
        (phi_in, phi),
        (rows_fwd_in, rows_fwd),
        (lanes_fwd_in, lanes_fwd),
        (twiddle_in, twiddle),
        (lanes_bwd_in, lanes_bwd),
        (rows_bwd_in, rows_bwd),
    )
    loads = [
        pltpu.make_async_copy(source, target, load_sem.at[i])
        for i, (source, target) in enumerate(pairs)
    ]

    barrier = pltpu.get_barrier_semaphore()
    for to in partners:
        pl.semaphore_signal(barrier, inc=1, device_id={"vel": to})
    for n in range(NODES):
        dist_load(n).start()
    for load in loads:
        load.start()

    def greet():
        @pl.when(has_above)
        def _():
            pl.semaphore_signal(barrier, inc=1, device_id={"space": here + 1})

        @pl.when(has_below)
        def _():
            pl.semaphore_signal(barrier, inc=1, device_id={"space": here - 1})

    @pl.when(parity == 1)
    def _():
        pl.semaphore_wait(barrier, 3 + beside)

    @pl.when(parity == 0)
    def _():
        pl.semaphore_wait(barrier, 3)

    greet()

    @pl.loop(0, NODES)
    def _(n):
        dist_load(n).wait()
        for e in range(ELEMS):
            for a in range(8):
                pool[(e * NODES + n) * 8 + a] = dist[
                    pl.ds(n * BLOCK + a * 32 + e, 8, stride=4), :
                ]
        for q in range(3):
            forward(n, q).start()
        for a in range(8):
            block[n * 32 + me * 8 + a] = pool[(me * NODES + n) * 8 + a]

    for load in loads:
        load.wait()

    for q in range(4):
        for a in range(8):
            pool[TABLE + q * 8 + a] = inject[pl.ds(a * 32 + q, 8, stride=4), :]
    for a in range(8):
        pool[TABLE + 32 + a] = free[a * 8 : a * 8 + 8, :]

    sub = lax.broadcasted_iota(jnp.int32, (8, 128), 0)
    lane = lax.broadcasted_iota(jnp.int32, (8, 128), 1)

    def grid(i):
        return SPEED * ((2.0 * i.astype(f32) + 1.0) / 32.0 - 1.0)

    v2 = grid(lane % 32)
    v1 = grid(sub * 4 + lane // 32)

    def normal_speed(j, v0, v1):
        return normals[j, 0] * v0 + normals[j, 1] * v1 + normals[j, 2] * v2

    def partial_sums(i, carry):
        a = i // 4
        v0 = grid(me * 8 + a)
        b = (lax.rem(i, 4) * 2 + sub // 4) * 4 + lane // 32
        got = [dist[rows(n * BLOCK + i * 8), :] for n in range(NODES)]
        new = []
        for j in range(4):
            pos = jnp.maximum(normal_speed(j, v0, grid(b)), 0.0)
            for k in range(6):
                new.append(carry[j * 6 + k] + pos * got[FACES[j][k]])
        return tuple(new)

    zero = jnp.zeros((8, 128), f32)
    nums = lax.fori_loop(0, 32, partial_sums, (zero,) * 24)

    def partial_dens(a, carry):
        v0 = grid(me * 8 + a)
        new = []
        for j in range(4):
            value = jnp.minimum(normal_speed(j, v0, v1), 0.0) * wall[rows(a * 8), :]
            negwall[rows((j * 8 + a) * 8), :] = value
            new.append(carry[j] - value)
        return tuple(new)

    dens = lax.fori_loop(0, 8, partial_dens, (zero,) * 4)
    mine = zero
    for i, x in enumerate(nums):
        x = x + pltpu.roll(x, 4, 0)
        mine = jnp.where(lane == i, jnp.sum(x, axis=1, keepdims=True), mine)
    for j, x in enumerate(dens):
        x = jnp.broadcast_to(jnp.sum(x, axis=0, keepdims=True), (8, 128))
        mine = jnp.where(lane == 24 + j, jnp.sum(x, axis=1, keepdims=True), mine)
    sums_out[...] = mine
    for q in range(3):
        sums(q).start()

    for i in range(8):
        x = khat[:, i * 128 : (i + 1) * 128]
        straight[i * 32 : (i + 1) * 32, :] = x
    x = straight[...]
    x0 = x.astype(jnp.bfloat16)
    x = x - x0.astype(f32)
    x1 = x.astype(jnp.bfloat16)
    x2 = (x - x1.astype(f32)).astype(jnp.bfloat16)
    rev = reverse[...]
    mirrored[...] = (
        jnp.dot(x0, rev, preferred_element_type=f32) + jnp.dot(x1, rev, preferred_element_type=f32)
    ) + jnp.dot(x2, rev, preferred_element_type=f32)
    group = lax.broadcasted_iota(jnp.int32, (32, 128), 1) // 32

    def regroup(source, place):
        total = jnp.zeros((32, 128), f32)
        for kh in range(4):
            kb = place(kh)
            tile, offset = kb // 4, kb % 4
            x = source[tile * 32 : (tile + 1) * 32, :]
            shift = (kh - offset) % 4 * 32
            if shift:
                x = pltpu.roll(x, shift, 1)
            total = jnp.where(group == kh, x, total)
        return total

    for kl in range(8):
        even = regroup(straight, lambda kh: kl + 8 * kh)
        odd = regroup(mirrored, lambda kh: (32 - kl - 8 * kh) % 32)
        moved[pl.ds(kl, 32, stride=8), :] = even
        moved[pl.ds(BLOCK + kl, 32, stride=8), :] = odd
    for ka in range(17):
        other = BLOCK + (32 - ka) % 32 * 8
        sym[ka * 8 : ka * 8 + 8, :] = 0.5 * (
            moved[ka * 8 : ka * 8 + 8, :] + moved[other : other + 8, :]
        )

    def send_halos():
        @pl.when(parity == 0)
        def _():
            pl.semaphore_wait(barrier, beside)

        @pl.when(turn_down)
        def _():
            pl.semaphore_signal(relay_ready, inc=1, device_id={"space": here - 1})

        @pl.when(turn_up)
        def _():
            pl.semaphore_signal(relay_ready, inc=1, device_id={"space": here + 1})

        up_elem = jnp.int32(0)
        down_elem = jnp.int32(0)
        for e in range(ELEMS):
            up_elem = up_elem + jnp.where(nb_side[e, 1] == 2, e, 0)
            down_elem = down_elem + jnp.where(nb_side[e, 0] == 1, e, 0)
        for side, elem, face in ((0, up_elem, 1), (1, down_elem, 0)):
            for k in range(6):
                for a in range(8):
                    halo_out[side, k * 8 + a] = pool[(elem * NODES + FACES[face][k]) * 8 + a]

            turn = turn_down if side else turn_up
            straight_on = (has_below if side else has_above) & jnp.logical_not(turn)

            @pl.when(straight_on)
            def _():
                halo(side).start()

            @pl.when(turn)
            def _():
                halo(side, DIRECT[side]).start()
                pl.semaphore_wait(relay_ready, 1)
                detour(side).start()

    def pass_on():
        for side in range(2):

            @pl.when(relay_down if side else relay_up)
            def _():
                detour(side).wait_recv()
                passed(side).start()

    cos = twiddle[0:8, :]
    sin = twiddle[8:16, :]

    @pl.loop(0, NODES)
    def _(n):
        @pl.when(n == 3)
        def _():
            send_halos()

        @pl.when(n == 9)
        def _():
            pass_on()

        for q in range(3):
            forward_in(n, q, block, pool, fwd_send, fwd_recv, partners, rows).wait_recv()
        result[rows(n * BLOCK, BLOCK), :] = collide(
            block[pl.ds(n * 32, 32)].reshape(BLOCK, 128),
            phi[...],
            sym[...],
            rows_fwd[...],
            lanes_fwd[...],
            lanes_bwd[...],
            rows_bwd[...],
            cos,
            sin,
        )
        for q in range(3):
            backward(n, q).start()

    total = sums_out[...]
    for q in range(3):
        sums(q).wait_recv()
    for q in range(3):
        total = total + sums_in[q]
    for j in range(4):
        mask = zero
        for e in range(ELEMS):
            on = jnp.where(nb_side[e, j] == 3, jnp.where(wall_flag[e, j] == 1, 1.0, 0.0), 0.0)
            mask = jnp.where(sub % 4 == e, on, mask)
        den = jnp.broadcast_to(total[:, 24 + j : 25 + j], (8, 128))
        sigma = [
            jnp.broadcast_to(total[:, j * 6 + k : j * 6 + k + 1], (8, 128)) / den * mask
            for k in range(6)
        ]
        for n in range(NODES):
            part = lift[0, j, n] * sigma[0]
            for k in range(1, 6):
                part = part + lift[k, j, n] * sigma[k]
            wallsum[(j * NODES + n) * 8 : (j * NODES + n) * 8 + 8, :] = part

    for side, face in ((0, 1), (1, 0)):

        turn = turn_up if side else turn_down
        here_in = has_above if side else has_below

        @pl.when(here_in & jnp.logical_not(turn))
        def _():
            halo(side).wait_recv()

        @pl.when(turn)
        def _():
            halo(side, DIRECT[side]).wait_recv()
            passed(side).wait_recv()

        @pl.when(here_in)
        def _():
            for k in range(6):
                start = HALO + (side * NODES + FACES[face][k]) * 8
                for a in range(8):
                    pool[start + a] = halo_in[side, k * 8 + a]

    @pl.loop(0, 8)
    def _(a):
        v0 = grid(me * 8 + a)
        negs = [jnp.minimum(normal_speed(j, v0, v1), 0.0) for j in range(4)]

        @pl.loop(0, ELEMS)
        def _(e):
            for j in range(4):
                side = nb_side[e, j]
                inner = jnp.where(side == 3, 0, 8)
                edge = TABLE + jnp.where(wall_flag[e, j] == 1, inj_id[e, j], 4) * 8
                near = nb_local[e, j] * (NODES * 8)
                far = HALO + jnp.where(side == 2, NODES * 8, 0)
                base = jnp.where(side == 3, edge, jnp.where(side == 0, near, far)) + a
                for k in range(6):
                    outer = pool[base + inner * FACES[j ^ 1][k]]
                    trace = pool[(e * NODES + FACES[j][k]) * 8 + a]
                    diff[j * 6 + k, rows(e * 8), :] = negs[j] * (trace - outer)

        @pl.loop(0, NODES // 2)
        def _(pair):
            acc = [[zero] * ELEMS for _ in range(2)]
            for m in range(NODES):
                for i in range(2):
                    n = pair * 2 + i
                    c = deriv[n, 0, m] * v0 + deriv[n, 1, m] * v1 + deriv[n, 2, m] * v2
                    for e in range(ELEMS):
                        f = pool[(e * NODES + m) * 8 + a]
                        acc[i][e] = acc[i][e] - c * f
            for j in range(4):
                for k in range(6):
                    for i in range(2):
                        c = lift[k, j, pair * 2 + i]
                        for e in range(ELEMS):
                            d = diff[j * 6 + k, e * 8 : e * 8 + 8, :]
                            acc[i][e] = acc[i][e] + c * d
            for i in range(2):
                for e in range(ELEMS):
                    moved[rows((e * NODES + pair * 2 + i) * SLAB + a * 8), :] = acc[i][e]

    @pl.loop(0, ELEMS)
    def _(e):
        @pl.loop(0, NODES)
        def _(n):
            parts = [
                jnp.broadcast_to(wallsum[pl.ds((j * NODES + n) * 8 + e, 1), :], (8, 128))
                for j in range(4)
            ]
            for a in range(8):
                x = moved[rows((e * NODES + n) * SLAB + a * 8), :]
                for j in range(4):
                    x = x - parts[j] * negwall[(j * 8 + a) * 8 : (j * 8 + a) * 8 + 8, :]
                moved[rows((e * NODES + n) * SLAB + a * 8), :] = x

    @pl.loop(0, NODES)
    def _(n):
        for a in range(8):
            out[pl.ds(n * BLOCK + a * 32 + me, 8, stride=4), :] = (
                result[rows(n * BLOCK + me * SLAB + a * 8), :]
                + moved[rows((me * NODES + n) * SLAB + a * 8), :]
            )
        for q in range(3):
            backward_in(n, q, back, result, bwd_send, bwd_recv, partners, rows).wait_recv()
            e = partners[q]
            for a in range(8):
                at = rows((e * NODES + n) * SLAB + a * 8)
                out[pl.ds(n * BLOCK + a * 32 + e, 8, stride=4), :] = back[at, :] + moved[at, :]

    @pl.loop(0, NODES)
    def _(n):
        for q in range(3):
            forward(n, q).wait_send()
            backward(n, q).wait_send()

    for side in range(2):
        turn = turn_down if side else turn_up
        straight_on = (has_below if side else has_above) & jnp.logical_not(turn)

        @pl.when(straight_on)
        def _():
            halo(side).wait_send()

        @pl.when(turn)
        def _():
            halo(side, DIRECT[side]).wait_send()
            detour(side).wait_send()

        @pl.when(relay_down if side else relay_up)
        def _():
            passed(side).wait_send()

    for q in range(3):
        sums(q).wait_send()


def forward_in(n, q, block, pool, send, recv, partners, rows):
    return pltpu.make_async_remote_copy(
        src_ref=pool.at[pl.ds(0, 8)],
        dst_ref=block.at[pl.ds(n * 32 + partners[q] * 8, 8)],
        send_sem=send.at[n, q],
        recv_sem=recv.at[n, q],
        device_id={"vel": partners[q]},
    )


def backward_in(n, q, back, result, send, recv, partners, rows):
    return pltpu.make_async_remote_copy(
        src_ref=result.at[rows(0, SLAB)],
        dst_ref=back.at[rows((partners[q] * NODES + n) * SLAB, SLAB)],
        send_sem=send.at[n, q],
        recv_sem=recv.at[n, q],
        device_id={"vel": partners[q]},
    )


def solution(mesh):
    space = mesh.shape["space"]
    constants = tables()

    def local(
        dist,
        phi,
        khat,
        deriv,
        lift,
        normals,
        wall_maxw,
        free_stream,
        inject,
        nb_local,
        nb_side,
        wall_flag,
        inj_id,
    ):
        lines = dist.transpose(1, 0, 2).reshape(NODES, ELEMS, SLAB, 128)
        lines = lines.transpose(0, 2, 1, 3).reshape(NODES * BLOCK, 128)
        profiles = inject.reshape(4, SLAB, 128).transpose(1, 0, 2).reshape(BLOCK, 128)
        hbm = pl.BlockSpec(memory_space=pltpu.HBM)
        f32 = jnp.float32
        dma = pltpu.SemaphoreType.DMA

        tables = [jnp.asarray(c) for c in constants]
        operands = [
            lines,
            phi.reshape(BLOCK, 128),
            khat,
            wall_maxw.reshape(SLAB, 128),
            free_stream.reshape(SLAB, 128),
            profiles,
            *tables,
            deriv.transpose(1, 0, 2),
            lift.transpose(2, 0, 1),
            normals,
            nb_local,
            nb_side,
            wall_flag,
            inj_id,
        ]

        def body(*refs):
            kernel(space, *refs)

        rate = pl.pallas_call(
            body,
            out_shape=jax.ShapeDtypeStruct((NODES * BLOCK, 128), f32),
            in_specs=[hbm] * len(operands),
            out_specs=pl.BlockSpec(memory_space=pltpu.VMEM),
            scratch_shapes=[pltpu.VMEM(x.shape, x.dtype) for x in operands[:12]]
            + [pltpu.SMEM(x.shape, x.dtype) for x in operands[12:]]
            + [
                pltpu.VMEM((POOL, 8, 128), f32),
                pltpu.VMEM((NODES * 32, 8, 128), f32),
                pltpu.VMEM((NODES * BLOCK, 128), f32),
                pltpu.VMEM((ELEMS * NODES * SLAB, 128), f32),
                pltpu.VMEM((ELEMS * NODES * SLAB, 128), f32),
                pltpu.VMEM((24, ELEMS * 8, 128), f32),
                pltpu.VMEM((4 * SLAB, 128), f32),
                pltpu.VMEM((BLOCK, 128), f32),
                pltpu.VMEM((BLOCK, 128), f32),
                pltpu.VMEM((HALF, 128), f32),
                pltpu.VMEM((4 * NODES * 8, 128), f32),
                pltpu.VMEM((2, 6 * 8, 8, 128), f32),
                pltpu.VMEM((2, 6 * 8, 8, 128), f32),
                pltpu.VMEM((6 * 8, 8, 128), f32),
                pltpu.VMEM((8, 128), f32),
                pltpu.VMEM((3, 8, 128), f32),
                dma((NODES,)),
                dma((len(operands) - 1,)),
                dma((NODES, 3)),
                dma((NODES, 3)),
                dma((NODES, 3)),
                dma((NODES, 3)),
                dma((2,)),
                dma((2,)),
                dma((2,)),
                dma((2,)),
                pltpu.SemaphoreType.REGULAR,
                dma((3,)),
                dma((3,)),
            ],
            compiler_params=pltpu.CompilerParams(
                collective_id=0, has_side_effects=True, vmem_limit_bytes=40 * 2**20
            ),
            name="rate",
        )(*[pltpu.with_memory_space_constraint(x, pltpu.HBM) for x in operands])
        rate = rate.reshape(NODES, SLAB, ELEMS, 128).transpose(0, 2, 1, 3)
        return rate.reshape(NODES, ELEMS, SLAB * 128).transpose(1, 0, 2)

    return jax.shard_map(
        local,
        mesh=mesh,
        in_specs=(
            P("space", None, "vel"),
            P(),
            P(),
            P(),
            P(),
            P(),
            P("vel"),
            P("vel"),
            P(None, "vel"),
            P("space", None),
            P("space", None),
            P("space", None),
            P("space", None),
        ),
        out_specs=P("space", None, "vel"),
        check_vma=False,
    )
```

```python
import math

import jax
import jax.numpy as jnp
import numpy as np
import ml_dtypes
from jax import lax
from jax.experimental import pallas as pl
from jax.experimental.pallas import tpu as pltpu
from jax.sharding import PartitionSpec as P

FACES = ((1, 2, 3, 5, 8, 9), (0, 2, 3, 6, 7, 9), (0, 1, 3, 4, 7, 8), (0, 1, 2, 4, 5, 6))
SPEED = 3.0
NODES = 10
ELEMS = 4
GROUP = 4
SLAB = 64
BLOCK = 256
HALF = 136
PACK = 128
TABLE = ELEMS * NODES * 8
HALO = TABLE + 5 * 8
POOL = HALO + 2 * NODES * 8
LINE = 4
DIRECT = (24, 24)


def split(x):
    hi = x.astype(ml_dtypes.bfloat16)
    lo = (x - hi.astype(np.float64)).astype(ml_dtypes.bfloat16)
    return hi, lo


def tables():
    turn = 2.0 * np.pi
    ka = np.repeat(np.arange(17), 8)
    kl = np.tile(np.arange(8), 17)
    a = np.repeat(np.arange(32), 8)
    bh = np.tile(np.arange(8), 32)
    bl = np.repeat(np.arange(4), 32)
    c = np.tile(np.arange(32), 4)
    angle = turn * ((np.outer(ka, a) % 32) / 32.0 + (np.outer(kl, bh) % 8) / 8.0)
    rows_fwd = np.concatenate([np.cos(angle), -np.sin(angle)], axis=0)
    angle = turn * ((np.outer(bl, bl) % 4) / 4.0 + (np.outer(c, c) % 32) / 32.0)
    co, si = np.cos(angle), np.sin(angle)
    lanes_fwd = np.concatenate(
        [np.concatenate([co, -si], axis=1), np.concatenate([si, co], axis=1)], axis=0
    )
    lanes_bwd = np.concatenate(
        [np.concatenate([co, si], axis=1), np.concatenate([-si, co], axis=1)], axis=0
    )
    angle = turn * ((np.outer(a, ka[:PACK]) % 32) / 32.0 + (np.outer(bh, kl[:PACK]) % 8) / 8.0)
    re, im = 2.0 * np.cos(angle), -2.0 * np.sin(angle)
    sign = np.where(a % 2 == 0, 1.0, -1.0)[:, None]
    angle = turn * ((np.outer(bh, np.arange(8)) % 8) / 8.0)
    re[:, :8] = np.cos(angle) + sign * np.sin(angle)
    im[:, :8] = -np.sin(angle) + sign * np.cos(angle)
    rows_bwd = np.concatenate([re, im], axis=1) * 2.0**-15

    def left(x):
        hi, lo = split(x)
        return np.concatenate([hi, hi, lo], axis=1)

    def right(x):
        hi, lo = split(x)
        return np.concatenate([hi, hi, lo], axis=0)

    angle = turn * np.outer(np.arange(8), bl) / 32.0
    twiddle = np.concatenate([np.cos(angle), np.sin(angle)], axis=0).astype(np.float32)
    lane = np.arange(128)
    mirror = (lane // 32) * 32 + (32 - lane % 32) % 32
    reverse = (lane[:, None] == mirror[None, :]).astype(ml_dtypes.bfloat16)
    return (left(rows_fwd), right(lanes_fwd), right(lanes_bwd), left(rows_bwd), twiddle, reverse)


def halves(x):
    hi = x.astype(jnp.bfloat16)
    lo = (x - hi.astype(jnp.float32)).astype(jnp.bfloat16)
    return hi, lo


def dot_left(table, x):
    hi, lo = halves(x)
    return jnp.dot(
        table, jnp.concatenate([hi, lo, hi], axis=0), preferred_element_type=jnp.float32
    )


def dot_right(x, table):
    hi, lo = halves(x)
    return jnp.dot(
        jnp.concatenate([hi, lo, hi], axis=1), table, preferred_element_type=jnp.float32
    )


def by_rows(x, y):
    return jnp.concatenate([x, y], axis=0)


def by_lanes(x, y):
    return jnp.concatenate([x, y], axis=1)


def turned(re, im, cos, sin):
    count = re.shape[0] // 8
    re = re.reshape(count, 8, 128)
    im = im.reshape(count, 8, 128)
    out_re = re * cos[None] - im * sin[None]
    out_im = re * sin[None] + im * cos[None]
    return out_re.reshape(count * 8, 128), out_im.reshape(count * 8, 128)


def collide(x, phi, sym, rows_fwd, lanes_fwd, lanes_bwd, rows_bwd, cos, sin):
    y = dot_left(rows_fwd, by_lanes(x * phi, x))
    wr, wi = turned(y[:HALF, :128], y[HALF:, :128], cos, -sin)
    fr, fi = turned(y[:HALF, 128:], y[HALF:, 128:], cos, -sin)
    s = dot_right(by_rows(by_lanes(wr, wi), by_lanes(fr, fi)), lanes_fwd)
    wr, wi, fr, fi = s[:HALF, :128], s[:HALF, 128:], s[HALF:, :128], s[HALF:, 128:]
    wr, wi = wr * 2.0**-15, wi * 2.0**-15

    def packed(re, im):
        first = re[:8] - im[PACK:]
        second = im[:8] + re[PACK:]
        return by_lanes(by_rows(first, re[8:PACK]), by_rows(second, im[8:PACK]))

    gain = packed(wr * fr - wi * fi, wr * fi + wi * fr)
    loss = packed(sym * fr, sym * fi)
    b = dot_right(by_rows(gain, loss), lanes_bwd)
    gr, gi = turned(b[:PACK, :128], b[:PACK, 128:], cos, sin)
    lr, li = turned(b[PACK:, :128], b[PACK:, 128:], cos, sin)
    z = dot_left(rows_bwd, by_rows(by_lanes(gr, lr), by_lanes(gi, li)))
    return z[:, :128] - x * z[:, 128:]


def kernel(
    space,
    dist_in,
    phi_in,
    khat_in,
    wall_in,
    free_in,
    inject_in,
    rows_fwd_in,
    lanes_fwd_in,
    lanes_bwd_in,
    rows_bwd_in,
    twiddle_in,
    reverse_in,
    deriv_in,
    lift_in,
    normals_in,
    nb_local_in,
    nb_side_in,
    wall_flag_in,
    inj_id_in,
    out,
    dist,
    phi,
    khat,
    wall,
    free,
    inject,
    rows_fwd,
    lanes_fwd,
    lanes_bwd,
    rows_bwd,
    twiddle,
    reverse,
    deriv,
    lift,
    normals,
    nb_local,
    nb_side,
    wall_flag,
    inj_id,
    pool,
    block,
    result,
    back,
    moved,
    diff,
    negwall,
    straight,
    mirrored,
    sym,
    wallsum,
    halo_out,
    halo_in,
    relay,
    sums_out,
    sums_in,
    dist_sem,
    load_sem,
    fwd_send,
    fwd_recv,
    bwd_send,
    bwd_recv,
    halo_send,
    halo_recv,
    relay_send,
    relay_recv,
    relay_ready,
    sums_send,
    sums_recv,
):
    f32 = jnp.float32
    me = lax.axis_index("vel")
    here = lax.axis_index("space")
    has_above = here < space - 1
    has_below = here > 0
    place = lax.rem(here, LINE)
    turn_up = (place == LINE - 1) & has_above
    turn_down = (place == 0) & has_below
    relay_up = (place == 1) & (here > LINE)
    relay_down = (place == LINE - 2) & (here < space - LINE)
    beside = jnp.where(has_above, 1, 0) + jnp.where(has_below, 1, 0)
    core = lax.rem(me, 2)
    parity = lax.rem(here + core + 1, 2)
    flip = 1 - 2 * core
    across = lax.rem(me + 2, GROUP)
    partners = (across, across + flip, me + flip)

    def rows(start, count=8):
        return pl.ds(pl.multiple_of(start, 8), count)

    def forward(n, q):
        to = partners[q]
        return pltpu.make_async_remote_copy(
            src_ref=pool.at[pl.ds((to * NODES + n) * 8, 8)],
            dst_ref=block.at[pl.ds(n * 32 + me * 8, 8)],
            send_sem=fwd_send.at[n, q],
            recv_sem=fwd_recv.at[n, q],
            device_id={"vel": to},
        )

    def backward(n, q):
        to = partners[q]
        return pltpu.make_async_remote_copy(
            src_ref=result.at[rows(n * BLOCK + to * SLAB, SLAB)],
            dst_ref=back.at[rows((me * NODES + n) * SLAB, SLAB)],
            send_sem=bwd_send.at[n, q],
            recv_sem=bwd_recv.at[n, q],
            device_id={"vel": to},
        )

    def halo(side, count=48):
        return pltpu.make_async_remote_copy(
            src_ref=halo_out.at[side, pl.ds(0, count)],
            dst_ref=halo_in.at[side, pl.ds(0, count)],
            send_sem=halo_send.at[side],
            recv_sem=halo_recv.at[side],
            device_id={"space": lax.rem(here + (space - 1 if side else 1), space)},
        )

    def detour(side):
        first = DIRECT[side]
        return pltpu.make_async_remote_copy(
            src_ref=halo_out.at[side, pl.ds(first, 48 - first)],
            dst_ref=relay.at[pl.ds(0, 48 - first)],
            send_sem=relay_send.at[0],
            recv_sem=relay_recv.at[0],
            device_id={"space": lax.rem(here + (space - 2 if side else 2), space)},
        )

    def passed(side):
        first = DIRECT[side]
        return pltpu.make_async_remote_copy(
            src_ref=relay.at[pl.ds(0, 48 - first)],
            dst_ref=halo_in.at[side, pl.ds(first, 48 - first)],
            send_sem=relay_send.at[1],
            recv_sem=relay_recv.at[1],
            device_id={"space": lax.rem(here + (1 if side else space - 1), space)},
        )

    def sums(q):
        return pltpu.make_async_remote_copy(
            src_ref=sums_out,
            dst_ref=sums_in.at[q],
            send_sem=sums_send.at[q],
            recv_sem=sums_recv.at[q],
            device_id={"vel": partners[q]},
        )

    def dist_load(n):
        part = rows(n * BLOCK, BLOCK)
        return pltpu.make_async_copy(dist_in.at[part], dist.at[part], dist_sem.at[n])

    pairs = (
        (nb_side_in, nb_side),
        (inject_in, inject),
        (free_in, free),
        (normals_in, normals),
        (wall_in, wall),
        (khat_in, khat),
        (reverse_in, reverse),
        (nb_local_in, nb_local),
        (wall_flag_in, wall_flag),
        (inj_id_in, inj_id),
        (deriv_in, deriv),
        (lift_in, lift),
        (phi_in, phi),
        (rows_fwd_in, rows_fwd),
        (lanes_fwd_in, lanes_fwd),
        (twiddle_in, twiddle),
        (lanes_bwd_in, lanes_bwd),
        (rows_bwd_in, rows_bwd),
    )
    loads = [
        pltpu.make_async_copy(source, target, load_sem.at[i])
        for i, (source, target) in enumerate(pairs)
    ]

    barrier = pltpu.get_barrier_semaphore()
    for to in partners:
        pl.semaphore_signal(barrier, inc=1, device_id={"vel": to})
    for n in range(NODES):
        dist_load(n).start()
    for load in loads:
        load.start()

    def greet():
        @pl.when(has_above)
        def _():
            pl.semaphore_signal(barrier, inc=1, device_id={"space": here + 1})

        @pl.when(has_below)
        def _():
            pl.semaphore_signal(barrier, inc=1, device_id={"space": here - 1})

    def repack(n):
        dist_load(n).wait()
        for e in range(ELEMS):
            for a in range(8):
                pool[(e * NODES + n) * 8 + a] = dist[
                    pl.ds(n * BLOCK + a * 32 + e, 8, stride=4), :
                ]

    repack(0)

    @pl.when(parity == 1)
    def _():
        pl.semaphore_wait(barrier, 3 + beside)

    @pl.when(parity == 0)
    def _():
        pl.semaphore_wait(barrier, 3)

    greet()

    def send(n):
        for q in range(3):
            forward(n, q).start()
        for a in range(8):
            block[n * 32 + me * 8 + a] = pool[(me * NODES + n) * 8 + a]

    send(0)

    @pl.loop(1, NODES)
    def _(n):
        repack(n)
        send(n)

    for load in loads:
        load.wait()

    for q in range(4):
        for a in range(8):
            pool[TABLE + q * 8 + a] = inject[pl.ds(a * 32 + q, 8, stride=4), :]
    for a in range(8):
        pool[TABLE + 32 + a] = free[a * 8 : a * 8 + 8, :]

    sub = lax.broadcasted_iota(jnp.int32, (8, 128), 0)
    lane = lax.broadcasted_iota(jnp.int32, (8, 128), 1)

    def grid(i):
        return SPEED * ((2.0 * i.astype(f32) + 1.0) / 32.0 - 1.0)

    v2 = grid(lane % 32)
    v1 = grid(sub * 4 + lane // 32)

    def normal_speed(j, v0, v1):
        return normals[j, 0] * v0 + normals[j, 1] * v1 + normals[j, 2] * v2

    def partial_sums(i, carry):
        a = i // 4
        v0 = grid(me * 8 + a)
        b = (lax.rem(i, 4) * 2 + sub // 4) * 4 + lane // 32
        got = [dist[rows(n * BLOCK + i * 8), :] for n in range(NODES)]
        new = []
        for j in range(4):
            pos = jnp.maximum(normal_speed(j, v0, grid(b)), 0.0)
            for k in range(6):
                new.append(carry[j * 6 + k] + pos * got[FACES[j][k]])
        return tuple(new)

    zero = jnp.zeros((8, 128), f32)
    nums = lax.fori_loop(0, 32, partial_sums, (zero,) * 24)

    def partial_dens(a, carry):
        v0 = grid(me * 8 + a)
        new = []
        for j in range(4):
            value = jnp.minimum(normal_speed(j, v0, v1), 0.0) * wall[rows(a * 8), :]
            negwall[rows((j * 8 + a) * 8), :] = value
            new.append(carry[j] - value)
        return tuple(new)

    dens = lax.fori_loop(0, 8, partial_dens, (zero,) * 4)
    mine = zero
    for i, x in enumerate(nums):
        x = x + pltpu.roll(x, 4, 0)
        mine = jnp.where(lane == i, jnp.sum(x, axis=1, keepdims=True), mine)
    for j, x in enumerate(dens):
        x = jnp.broadcast_to(jnp.sum(x, axis=0, keepdims=True), (8, 128))
        mine = jnp.where(lane == 24 + j, jnp.sum(x, axis=1, keepdims=True), mine)
    sums_out[...] = mine
    for q in range(3):
        sums(q).start()

    for i in range(8):
        x = khat[:, i * 128 : (i + 1) * 128]
        straight[i * 32 : (i + 1) * 32, :] = x
    x = straight[...]
    x0 = x.astype(jnp.bfloat16)
    x = x - x0.astype(f32)
    x1 = x.astype(jnp.bfloat16)
    x2 = (x - x1.astype(f32)).astype(jnp.bfloat16)
    rev = reverse[...]
    mirrored[...] = (
        jnp.dot(x0, rev, preferred_element_type=f32) + jnp.dot(x1, rev, preferred_element_type=f32)
    ) + jnp.dot(x2, rev, preferred_element_type=f32)
    group = lax.broadcasted_iota(jnp.int32, (32, 128), 1) // 32

    def regroup(source, place):
        total = jnp.zeros((32, 128), f32)
        for kh in range(4):
            kb = place(kh)
            tile, offset = kb // 4, kb % 4
            x = source[tile * 32 : (tile + 1) * 32, :]
            shift = (kh - offset) % 4 * 32
            if shift:
                x = pltpu.roll(x, shift, 1)
            total = jnp.where(group == kh, x, total)
        return total

    for kl in range(8):
        even = regroup(straight, lambda kh: kl + 8 * kh)
        odd = regroup(mirrored, lambda kh: (32 - kl - 8 * kh) % 32)
        moved[pl.ds(kl, 32, stride=8), :] = even
        moved[pl.ds(BLOCK + kl, 32, stride=8), :] = odd
    for ka in range(17):
        other = BLOCK + (32 - ka) % 32 * 8
        sym[ka * 8 : ka * 8 + 8, :] = 0.5 * (
            moved[ka * 8 : ka * 8 + 8, :] + moved[other : other + 8, :]
        )

    def send_halos():
        @pl.when(parity == 0)
        def _():
            pl.semaphore_wait(barrier, beside)

        @pl.when(turn_down)
        def _():
            pl.semaphore_signal(relay_ready, inc=1, device_id={"space": here - 1})

        @pl.when(turn_up)
        def _():
            pl.semaphore_signal(relay_ready, inc=1, device_id={"space": here + 1})

        up_elem = jnp.int32(0)
        down_elem = jnp.int32(0)
        for e in range(ELEMS):
            up_elem = up_elem + jnp.where(nb_side[e, 1] == 2, e, 0)
            down_elem = down_elem + jnp.where(nb_side[e, 0] == 1, e, 0)
        for side, elem, face in ((0, up_elem, 1), (1, down_elem, 0)):
            for k in range(6):
                for a in range(8):
                    halo_out[side, k * 8 + a] = pool[(elem * NODES + FACES[face][k]) * 8 + a]

            turn = turn_down if side else turn_up
            straight_on = (has_below if side else has_above) & jnp.logical_not(turn)

            @pl.when(straight_on)
            def _():
                halo(side).start()

            @pl.when(turn)
            def _():
                halo(side, DIRECT[side]).start()
                pl.semaphore_wait(relay_ready, 1)
                detour(side).start()

    def pass_on():
        for side in range(2):

            @pl.when(relay_down if side else relay_up)
            def _():
                detour(side).wait_recv()
                passed(side).start()

    cos = twiddle[0:8, :]
    sin = twiddle[8:16, :]

    @pl.loop(0, NODES)
    def _(n):
        @pl.when(n == 3)
        def _():
            send_halos()

        @pl.when(n == 9)
        def _():
            pass_on()

        for q in range(3):
            forward_in(n, q, block, pool, fwd_send, fwd_recv, partners, rows).wait_recv()
        result[rows(n * BLOCK, BLOCK), :] = collide(
            block[pl.ds(n * 32, 32)].reshape(BLOCK, 128),
            phi[...],
            sym[...],
            rows_fwd[...],
            lanes_fwd[...],
            lanes_bwd[...],
            rows_bwd[...],
            cos,
            sin,
        )
        for q in range(3):
            backward(n, q).start()
        for q in range(3):
            forward(n, q).wait_send()

    total = sums_out[...]
    for q in range(3):
        sums(q).wait_recv()
    for q in range(3):
        total = total + sums_in[q]
    for j in range(4):
        mask = zero
        for e in range(ELEMS):
            on = jnp.where(nb_side[e, j] == 3, jnp.where(wall_flag[e, j] == 1, 1.0, 0.0), 0.0)
            mask = jnp.where(sub % 4 == e, on, mask)
        den = jnp.broadcast_to(total[:, 24 + j : 25 + j], (8, 128))
        sigma = [
            jnp.broadcast_to(total[:, j * 6 + k : j * 6 + k + 1], (8, 128)) / den * mask
            for k in range(6)
        ]
        for n in range(NODES):
            part = lift[0, j, n] * sigma[0]
            for k in range(1, 6):
                part = part + lift[k, j, n] * sigma[k]
            wallsum[(j * NODES + n) * 8 : (j * NODES + n) * 8 + 8, :] = part

    for side, face in ((0, 1), (1, 0)):

        turn = turn_up if side else turn_down
        here_in = has_above if side else has_below

        @pl.when(here_in & jnp.logical_not(turn))
        def _():
            halo(side).wait_recv()

        @pl.when(turn)
        def _():
            halo(side, DIRECT[side]).wait_recv()
            passed(side).wait_recv()

        @pl.when(here_in)
        def _():
            for k in range(6):
                start = HALO + (side * NODES + FACES[face][k]) * 8
                for a in range(8):
                    pool[start + a] = halo_in[side, k * 8 + a]

    @pl.loop(0, 8)
    def _(a):
        v0 = grid(me * 8 + a)
        negs = [jnp.minimum(normal_speed(j, v0, v1), 0.0) for j in range(4)]

        @pl.loop(0, ELEMS)
        def _(e):
            for j in range(4):
                side = nb_side[e, j]
                inner = jnp.where(side == 3, 0, 8)
                edge = TABLE + jnp.where(wall_flag[e, j] == 1, inj_id[e, j], 4) * 8
                near = nb_local[e, j] * (NODES * 8)
                far = HALO + jnp.where(side == 2, NODES * 8, 0)
                base = jnp.where(side == 3, edge, jnp.where(side == 0, near, far)) + a
                for k in range(6):
                    outer = pool[base + inner * FACES[j ^ 1][k]]
                    trace = pool[(e * NODES + FACES[j][k]) * 8 + a]
                    diff[j * 6 + k, rows(e * 8), :] = negs[j] * (trace - outer)

        @pl.loop(0, NODES // 2)
        def _(pair):
            acc = [[zero] * ELEMS for _ in range(2)]
            for m in range(NODES):
                for i in range(2):
                    n = pair * 2 + i
                    c = deriv[n, 0, m] * v0 + deriv[n, 1, m] * v1 + deriv[n, 2, m] * v2
                    for e in range(ELEMS):
                        f = pool[(e * NODES + m) * 8 + a]
                        acc[i][e] = acc[i][e] - c * f
            for j in range(4):
                for k in range(6):
                    for i in range(2):
                        c = lift[k, j, pair * 2 + i]
                        for e in range(ELEMS):
                            d = diff[j * 6 + k, e * 8 : e * 8 + 8, :]
                            acc[i][e] = acc[i][e] + c * d
            for i in range(2):
                for e in range(ELEMS):
                    moved[rows((e * NODES + pair * 2 + i) * SLAB + a * 8), :] = acc[i][e]

    @pl.loop(0, ELEMS)
    def _(e):
        @pl.loop(0, NODES)
        def _(n):
            parts = [
                jnp.broadcast_to(wallsum[pl.ds((j * NODES + n) * 8 + e, 1), :], (8, 128))
                for j in range(4)
            ]
            for a in range(8):
                x = moved[rows((e * NODES + n) * SLAB + a * 8), :]
                for j in range(4):
                    x = x - parts[j] * negwall[(j * 8 + a) * 8 : (j * 8 + a) * 8 + 8, :]
                moved[rows((e * NODES + n) * SLAB + a * 8), :] = x

    @pl.loop(0, NODES)
    def _(n):
        for a in range(8):
            out[pl.ds(n * BLOCK + a * 32 + me, 8, stride=4), :] = (
                result[rows(n * BLOCK + me * SLAB + a * 8), :]
                + moved[rows((me * NODES + n) * SLAB + a * 8), :]
            )
        for q in range(3):
            backward_in(n, q, back, result, bwd_send, bwd_recv, partners, rows).wait_recv()
            e = partners[q]
            for a in range(8):
                at = rows((e * NODES + n) * SLAB + a * 8)
                out[pl.ds(n * BLOCK + a * 32 + e, 8, stride=4), :] = back[at, :] + moved[at, :]
        for q in range(3):
            backward(n, q).wait_send()

    for side in range(2):
        turn = turn_down if side else turn_up
        straight_on = (has_below if side else has_above) & jnp.logical_not(turn)

        @pl.when(straight_on)
        def _():
            halo(side).wait_send()

        @pl.when(turn)
        def _():
            halo(side, DIRECT[side]).wait_send()
            detour(side).wait_send()

        @pl.when(relay_down if side else relay_up)
        def _():
            passed(side).wait_send()

    for q in range(3):
        sums(q).wait_send()


def forward_in(n, q, block, pool, send, recv, partners, rows):
    return pltpu.make_async_remote_copy(
        src_ref=pool.at[pl.ds(0, 8)],
        dst_ref=block.at[pl.ds(n * 32 + partners[q] * 8, 8)],
        send_sem=send.at[n, q],
        recv_sem=recv.at[n, q],
        device_id={"vel": partners[q]},
    )


def backward_in(n, q, back, result, send, recv, partners, rows):
    return pltpu.make_async_remote_copy(
        src_ref=result.at[rows(0, SLAB)],
        dst_ref=back.at[rows((partners[q] * NODES + n) * SLAB, SLAB)],
        send_sem=send.at[n, q],
        recv_sem=recv.at[n, q],
        device_id={"vel": partners[q]},
    )


def solution(mesh):
    space = mesh.shape["space"]
    constants = tables()

    def local(
        dist,
        phi,
        khat,
        deriv,
        lift,
        normals,
        wall_maxw,
        free_stream,
        inject,
        nb_local,
        nb_side,
        wall_flag,
        inj_id,
    ):
        lines = dist.transpose(1, 0, 2).reshape(NODES, ELEMS, SLAB, 128)
        lines = lines.transpose(0, 2, 1, 3).reshape(NODES * BLOCK, 128)
        profiles = inject.reshape(4, SLAB, 128).transpose(1, 0, 2).reshape(BLOCK, 128)
        hbm = pl.BlockSpec(memory_space=pltpu.HBM)
        f32 = jnp.float32
        dma = pltpu.SemaphoreType.DMA

        tables = [jnp.asarray(c) for c in constants]
        operands = [
            lines,
            phi.reshape(BLOCK, 128),
            khat,
            wall_maxw.reshape(SLAB, 128),
            free_stream.reshape(SLAB, 128),
            profiles,
            *tables,
            deriv.transpose(1, 0, 2),
            lift.transpose(2, 0, 1),
            normals,
            nb_local,
            nb_side,
            wall_flag,
            inj_id,
        ]

        def body(*refs):
            kernel(space, *refs)

        rate = pl.pallas_call(
            body,
            out_shape=jax.ShapeDtypeStruct((NODES * BLOCK, 128), f32),
            in_specs=[hbm] * len(operands),
            out_specs=pl.BlockSpec(memory_space=pltpu.VMEM),
            scratch_shapes=[pltpu.VMEM(x.shape, x.dtype) for x in operands[:12]]
            + [pltpu.SMEM(x.shape, x.dtype) for x in operands[12:]]
            + [
                pltpu.VMEM((POOL, 8, 128), f32),
                pltpu.VMEM((NODES * 32, 8, 128), f32),
                pltpu.VMEM((NODES * BLOCK, 128), f32),
                pltpu.VMEM((ELEMS * NODES * SLAB, 128), f32),
                pltpu.VMEM((ELEMS * NODES * SLAB, 128), f32),
                pltpu.VMEM((24, ELEMS * 8, 128), f32),
                pltpu.VMEM((4 * SLAB, 128), f32),
                pltpu.VMEM((BLOCK, 128), f32),
                pltpu.VMEM((BLOCK, 128), f32),
                pltpu.VMEM((HALF, 128), f32),
                pltpu.VMEM((4 * NODES * 8, 128), f32),
                pltpu.VMEM((2, 6 * 8, 8, 128), f32),
                pltpu.VMEM((2, 6 * 8, 8, 128), f32),
                pltpu.VMEM((6 * 8, 8, 128), f32),
                pltpu.VMEM((8, 128), f32),
                pltpu.VMEM((3, 8, 128), f32),
                dma((NODES,)),
                dma((len(operands) - 1,)),
                dma((NODES, 3)),
                dma((NODES, 3)),
                dma((NODES, 3)),
                dma((NODES, 3)),
                dma((2,)),
                dma((2,)),
                dma((2,)),
                dma((2,)),
                pltpu.SemaphoreType.REGULAR,
                dma((3,)),
                dma((3,)),
            ],
            compiler_params=pltpu.CompilerParams(
                collective_id=0, has_side_effects=True, vmem_limit_bytes=40 * 2**20
            ),
            name="rate",
        )(*[pltpu.with_memory_space_constraint(x, pltpu.HBM) for x in operands])
        rate = rate.reshape(NODES, SLAB, ELEMS, 128).transpose(0, 2, 1, 3)
        return rate.reshape(NODES, ELEMS, SLAB * 128).transpose(1, 0, 2)

    return jax.shard_map(
        local,
        mesh=mesh,
        in_specs=(
            P("space", None, "vel"),
            P(),
            P(),
            P(),
            P(),
            P(),
            P("vel"),
            P("vel"),
            P(None, "vel"),
            P("space", None),
            P("space", None),
            P("space", None),
            P("space", None),
        ),
        out_specs=P("space", None, "vel"),
        check_vma=False,
    )
```

```python
import math

import jax
import jax.numpy as jnp
import numpy as np
import ml_dtypes
from jax import lax
from jax.experimental import pallas as pl
from jax.experimental.pallas import tpu as pltpu
from jax.sharding import PartitionSpec as P

FACES = ((1, 2, 3, 5, 8, 9), (0, 2, 3, 6, 7, 9), (0, 1, 3, 4, 7, 8), (0, 1, 2, 4, 5, 6))
SPEED = 3.0
NODES = 10
ELEMS = 4
GROUP = 4
SLAB = 64
BLOCK = 256
HALF = 136
PACK = 128
TABLE = ELEMS * NODES * 8
HALO = TABLE + 5 * 8
POOL = HALO + 2 * NODES * 8
LINE = 4
DIRECT = (28, 24)


def split(x):
    hi = x.astype(ml_dtypes.bfloat16)
    lo = (x - hi.astype(np.float64)).astype(ml_dtypes.bfloat16)
    return hi, lo


def tables():
    turn = 2.0 * np.pi
    ka = np.repeat(np.arange(17), 8)
    kl = np.tile(np.arange(8), 17)
    a = np.repeat(np.arange(32), 8)
    bh = np.tile(np.arange(8), 32)
    bl = np.repeat(np.arange(4), 32)
    c = np.tile(np.arange(32), 4)
    angle = turn * ((np.outer(ka, a) % 32) / 32.0 + (np.outer(kl, bh) % 8) / 8.0)
    rows_fwd = np.concatenate([np.cos(angle), -np.sin(angle)], axis=0)
    angle = turn * ((np.outer(bl, bl) % 4) / 4.0 + (np.outer(c, c) % 32) / 32.0)
    co, si = np.cos(angle), np.sin(angle)
    lanes_fwd = np.concatenate(
        [np.concatenate([co, -si], axis=1), np.concatenate([si, co], axis=1)], axis=0
    )
    lanes_bwd = np.concatenate(
        [np.concatenate([co, si], axis=1), np.concatenate([-si, co], axis=1)], axis=0
    )
    angle = turn * ((np.outer(a, ka[:PACK]) % 32) / 32.0 + (np.outer(bh, kl[:PACK]) % 8) / 8.0)
    re, im = 2.0 * np.cos(angle), -2.0 * np.sin(angle)
    sign = np.where(a % 2 == 0, 1.0, -1.0)[:, None]
    angle = turn * ((np.outer(bh, np.arange(8)) % 8) / 8.0)
    re[:, :8] = np.cos(angle) + sign * np.sin(angle)
    im[:, :8] = -np.sin(angle) + sign * np.cos(angle)
    rows_bwd = np.concatenate([re, im], axis=1) * 2.0**-15

    def left(x):
        hi, lo = split(x)
        return np.concatenate([hi, hi, lo], axis=1)

    def right(x):
        hi, lo = split(x)
        return np.concatenate([hi, hi, lo], axis=0)

    angle = turn * np.outer(np.arange(8), bl) / 32.0
    twiddle = np.concatenate([np.cos(angle), np.sin(angle)], axis=0).astype(np.float32)
    lane = np.arange(128)
    mirror = (lane // 32) * 32 + (32 - lane % 32) % 32
    reverse = (lane[:, None] == mirror[None, :]).astype(ml_dtypes.bfloat16)
    return (left(rows_fwd), right(lanes_fwd), right(lanes_bwd), left(rows_bwd), twiddle, reverse)


def halves(x):
    hi = x.astype(jnp.bfloat16)
    lo = (x - hi.astype(jnp.float32)).astype(jnp.bfloat16)
    return hi, lo


def dot_left(table, x):
    hi, lo = halves(x)
    return jnp.dot(
        table, jnp.concatenate([hi, lo, hi], axis=0), preferred_element_type=jnp.float32
    )


def dot_right(x, table):
    hi, lo = halves(x)
    return jnp.dot(
        jnp.concatenate([hi, lo, hi], axis=1), table, preferred_element_type=jnp.float32
    )


def by_rows(x, y):
    return jnp.concatenate([x, y], axis=0)


def by_lanes(x, y):
    return jnp.concatenate([x, y], axis=1)


def turned(re, im, cos, sin):
    count = re.shape[0] // 8
    re = re.reshape(count, 8, 128)
    im = im.reshape(count, 8, 128)
    out_re = re * cos[None] - im * sin[None]
    out_im = re * sin[None] + im * cos[None]
    return out_re.reshape(count * 8, 128), out_im.reshape(count * 8, 128)


def collide(x, phi, sym, rows_fwd, lanes_fwd, lanes_bwd, rows_bwd, cos, sin):
    y = dot_left(rows_fwd, by_lanes(x * phi, x))
    wr, wi = turned(y[:HALF, :128], y[HALF:, :128], cos, -sin)
    fr, fi = turned(y[:HALF, 128:], y[HALF:, 128:], cos, -sin)
    s = dot_right(by_rows(by_lanes(wr, wi), by_lanes(fr, fi)), lanes_fwd)
    wr, wi, fr, fi = s[:HALF, :128], s[:HALF, 128:], s[HALF:, :128], s[HALF:, 128:]
    wr, wi = wr * 2.0**-15, wi * 2.0**-15

    def packed(re, im):
        first = re[:8] - im[PACK:]
        second = im[:8] + re[PACK:]
        return by_lanes(by_rows(first, re[8:PACK]), by_rows(second, im[8:PACK]))

    gain = packed(wr * fr - wi * fi, wr * fi + wi * fr)
    loss = packed(sym * fr, sym * fi)
    b = dot_right(by_rows(gain, loss), lanes_bwd)
    gr, gi = turned(b[:PACK, :128], b[:PACK, 128:], cos, sin)
    lr, li = turned(b[PACK:, :128], b[PACK:, 128:], cos, sin)
    z = dot_left(rows_bwd, by_rows(by_lanes(gr, lr), by_lanes(gi, li)))
    return z[:, :128] - x * z[:, 128:]


def kernel(
    space,
    dist_in,
    phi_in,
    khat_in,
    wall_in,
    free_in,
    inject_in,
    rows_fwd_in,
    lanes_fwd_in,
    lanes_bwd_in,
    rows_bwd_in,
    twiddle_in,
    reverse_in,
    deriv_in,
    lift_in,
    normals_in,
    nb_local_in,
    nb_side_in,
    wall_flag_in,
    inj_id_in,
    out,
    dist,
    phi,
    khat,
    wall,
    free,
    inject,
    rows_fwd,
    lanes_fwd,
    lanes_bwd,
    rows_bwd,
    twiddle,
    reverse,
    deriv,
    lift,
    normals,
    nb_local,
    nb_side,
    wall_flag,
    inj_id,
    pool,
    block,
    result,
    back,
    moved,
    diff,
    negwall,
    straight,
    mirrored,
    sym,
    wallsum,
    halo_out,
    halo_in,
    relay,
    sums_out,
    sums_in,
    dist_sem,
    load_sem,
    fwd_send,
    fwd_recv,
    bwd_send,
    bwd_recv,
    halo_send,
    halo_recv,
    relay_send,
    relay_recv,
    relay_ready,
    sums_send,
    sums_recv,
):
    f32 = jnp.float32
    me = lax.axis_index("vel")
    here = lax.axis_index("space")
    has_above = here < space - 1
    has_below = here > 0
    place = lax.rem(here, LINE)
    turn_up = (place == LINE - 1) & has_above
    turn_down = (place == 0) & has_below
    relay_up = (place == 1) & (here > LINE)
    relay_down = (place == LINE - 2) & (here < space - LINE)
    beside = jnp.where(has_above, 1, 0) + jnp.where(has_below, 1, 0)
    core = lax.rem(me, 2)
    parity = lax.rem(here + core + 1, 2)
    flip = 1 - 2 * core
    across = lax.rem(me + 2, GROUP)
    partners = (across, across + flip, me + flip)

    def rows(start, count=8):
        return pl.ds(pl.multiple_of(start, 8), count)

    def forward(n, q):
        to = partners[q]
        return pltpu.make_async_remote_copy(
            src_ref=pool.at[pl.ds((to * NODES + n) * 8, 8)],
            dst_ref=block.at[pl.ds(n * 32 + me * 8, 8)],
            send_sem=fwd_send.at[n, q],
            recv_sem=fwd_recv.at[n, q],
            device_id={"vel": to},
        )

    def backward(n, q):
        to = partners[q]
        return pltpu.make_async_remote_copy(
            src_ref=result.at[rows(n * BLOCK + to * SLAB, SLAB)],
            dst_ref=back.at[rows((me * NODES + n) * SLAB, SLAB)],
            send_sem=bwd_send.at[n, q],
            recv_sem=bwd_recv.at[n, q],
            device_id={"vel": to},
        )

    def halo(side, count=48):
        return pltpu.make_async_remote_copy(
            src_ref=halo_out.at[side, pl.ds(0, count)],
            dst_ref=halo_in.at[side, pl.ds(0, count)],
            send_sem=halo_send.at[side],
            recv_sem=halo_recv.at[side],
            device_id={"space": lax.rem(here + (space - 1 if side else 1), space)},
        )

    def detour(side):
        first = DIRECT[side]
        return pltpu.make_async_remote_copy(
            src_ref=halo_out.at[side, pl.ds(first, 48 - first)],
            dst_ref=relay.at[pl.ds(0, 48 - first)],
            send_sem=relay_send.at[0],
            recv_sem=relay_recv.at[0],
            device_id={"space": lax.rem(here + (space - 2 if side else 2), space)},
        )

    def passed(side):
        first = DIRECT[side]
        return pltpu.make_async_remote_copy(
            src_ref=relay.at[pl.ds(0, 48 - first)],
            dst_ref=halo_in.at[side, pl.ds(first, 48 - first)],
            send_sem=relay_send.at[1],
            recv_sem=relay_recv.at[1],
            device_id={"space": lax.rem(here + (1 if side else space - 1), space)},
        )

    def sums(q):
        return pltpu.make_async_remote_copy(
            src_ref=sums_out,
            dst_ref=sums_in.at[q],
            send_sem=sums_send.at[q],
            recv_sem=sums_recv.at[q],
            device_id={"vel": partners[q]},
        )

    def dist_load(n):
        part = rows(n * BLOCK, BLOCK)
        return pltpu.make_async_copy(dist_in.at[part], dist.at[part], dist_sem.at[n])

    pairs = (
        (nb_side_in, nb_side),
        (inject_in, inject),
        (free_in, free),
        (normals_in, normals),
        (wall_in, wall),
        (khat_in, khat),
        (reverse_in, reverse),
        (nb_local_in, nb_local),
        (wall_flag_in, wall_flag),
        (inj_id_in, inj_id),
        (deriv_in, deriv),
        (lift_in, lift),
        (phi_in, phi),
        (rows_fwd_in, rows_fwd),
        (lanes_fwd_in, lanes_fwd),
        (twiddle_in, twiddle),
        (lanes_bwd_in, lanes_bwd),
        (rows_bwd_in, rows_bwd),
    )
    loads = [
        pltpu.make_async_copy(source, target, load_sem.at[i])
        for i, (source, target) in enumerate(pairs)
    ]

    barrier = pltpu.get_barrier_semaphore()
    for to in partners:
        pl.semaphore_signal(barrier, inc=1, device_id={"vel": to})
    for n in range(NODES):
        dist_load(n).start()
    for load in loads:
        load.start()

    def greet():
        @pl.when(has_above)
        def _():
            pl.semaphore_signal(barrier, inc=1, device_id={"space": here + 1})

        @pl.when(has_below)
        def _():
            pl.semaphore_signal(barrier, inc=1, device_id={"space": here - 1})

    def repack(n):
        dist_load(n).wait()
        for e in range(ELEMS):
            for a in range(8):
                pool[(e * NODES + n) * 8 + a] = dist[
                    pl.ds(n * BLOCK + a * 32 + e, 8, stride=4), :
                ]

    repack(0)

    @pl.when(parity == 1)
    def _():
        pl.semaphore_wait(barrier, 3 + beside)

    @pl.when(parity == 0)
    def _():
        pl.semaphore_wait(barrier, 3)

    greet()

    def send(n):
        for q in range(3):
            forward(n, q).start()
        for a in range(8):
            block[n * 32 + me * 8 + a] = pool[(me * NODES + n) * 8 + a]

    send(0)

    @pl.loop(1, NODES)
    def _(n):
        repack(n)
        send(n)

    for load in loads:
        load.wait()

    for q in range(4):
        for a in range(8):
            pool[TABLE + q * 8 + a] = inject[pl.ds(a * 32 + q, 8, stride=4), :]
    for a in range(8):
        pool[TABLE + 32 + a] = free[a * 8 : a * 8 + 8, :]

    sub = lax.broadcasted_iota(jnp.int32, (8, 128), 0)
    lane = lax.broadcasted_iota(jnp.int32, (8, 128), 1)

    def grid(i):
        return SPEED * ((2.0 * i.astype(f32) + 1.0) / 32.0 - 1.0)

    v2 = grid(lane % 32)
    v1 = grid(sub * 4 + lane // 32)

    def normal_speed(j, v0, v1):
        return normals[j, 0] * v0 + normals[j, 1] * v1 + normals[j, 2] * v2

    def partial_sums(i, carry):
        a = i // 4
        v0 = grid(me * 8 + a)
        b = (lax.rem(i, 4) * 2 + sub // 4) * 4 + lane // 32
        got = [dist[rows(n * BLOCK + i * 8), :] for n in range(NODES)]
        new = []
        for j in range(4):
            pos = jnp.maximum(normal_speed(j, v0, grid(b)), 0.0)
            for k in range(6):
                new.append(carry[j * 6 + k] + pos * got[FACES[j][k]])
        return tuple(new)

    zero = jnp.zeros((8, 128), f32)
    nums = lax.fori_loop(0, 32, partial_sums, (zero,) * 24)

    def partial_dens(a, carry):
        v0 = grid(me * 8 + a)
        new = []
        for j in range(4):
            value = jnp.minimum(normal_speed(j, v0, v1), 0.0) * wall[rows(a * 8), :]
            negwall[rows((j * 8 + a) * 8), :] = value
            new.append(carry[j] - value)
        return tuple(new)

    dens = lax.fori_loop(0, 8, partial_dens, (zero,) * 4)
    mine = zero
    for i, x in enumerate(nums):
        x = x + pltpu.roll(x, 4, 0)
        mine = jnp.where(lane == i, jnp.sum(x, axis=1, keepdims=True), mine)
    for j, x in enumerate(dens):
        x = jnp.broadcast_to(jnp.sum(x, axis=0, keepdims=True), (8, 128))
        mine = jnp.where(lane == 24 + j, jnp.sum(x, axis=1, keepdims=True), mine)
    sums_out[...] = mine
    for q in range(3):
        sums(q).start()

    for i in range(8):
        x = khat[:, i * 128 : (i + 1) * 128]
        straight[i * 32 : (i + 1) * 32, :] = x
    x = straight[...]
    x0 = x.astype(jnp.bfloat16)
    x = x - x0.astype(f32)
    x1 = x.astype(jnp.bfloat16)
    x2 = (x - x1.astype(f32)).astype(jnp.bfloat16)
    rev = reverse[...]
    mirrored[...] = (
        jnp.dot(x0, rev, preferred_element_type=f32) + jnp.dot(x1, rev, preferred_element_type=f32)
    ) + jnp.dot(x2, rev, preferred_element_type=f32)
    group = lax.broadcasted_iota(jnp.int32, (32, 128), 1) // 32

    def regroup(source, place):
        total = jnp.zeros((32, 128), f32)
        for kh in range(4):
            kb = place(kh)
            tile, offset = kb // 4, kb % 4
            x = source[tile * 32 : (tile + 1) * 32, :]
            shift = (kh - offset) % 4 * 32
            if shift:
                x = pltpu.roll(x, shift, 1)
            total = jnp.where(group == kh, x, total)
        return total

    for kl in range(8):
        even = regroup(straight, lambda kh: kl + 8 * kh)
        odd = regroup(mirrored, lambda kh: (32 - kl - 8 * kh) % 32)
        moved[pl.ds(kl, 32, stride=8), :] = even
        moved[pl.ds(BLOCK + kl, 32, stride=8), :] = odd
    for ka in range(17):
        other = BLOCK + (32 - ka) % 32 * 8
        sym[ka * 8 : ka * 8 + 8, :] = 0.5 * (
            moved[ka * 8 : ka * 8 + 8, :] + moved[other : other + 8, :]
        )

    def send_halos():
        @pl.when(parity == 0)
        def _():
            pl.semaphore_wait(barrier, beside)

        @pl.when(turn_down)
        def _():
            pl.semaphore_signal(relay_ready, inc=1, device_id={"space": here - 1})

        @pl.when(turn_up)
        def _():
            pl.semaphore_signal(relay_ready, inc=1, device_id={"space": here + 1})

        up_elem = jnp.int32(0)
        down_elem = jnp.int32(0)
        for e in range(ELEMS):
            up_elem = up_elem + jnp.where(nb_side[e, 1] == 2, e, 0)
            down_elem = down_elem + jnp.where(nb_side[e, 0] == 1, e, 0)
        for side, elem, face in ((0, up_elem, 1), (1, down_elem, 0)):
            for k in range(6):
                for a in range(8):
                    halo_out[side, k * 8 + a] = pool[(elem * NODES + FACES[face][k]) * 8 + a]

            turn = turn_down if side else turn_up
            straight_on = (has_below if side else has_above) & jnp.logical_not(turn)

            @pl.when(straight_on)
            def _():
                halo(side).start()

            @pl.when(turn)
            def _():
                halo(side, DIRECT[side]).start()
                pl.semaphore_wait(relay_ready, 1)
                detour(side).start()

    def pass_on():
        for side in range(2):

            @pl.when(relay_down if side else relay_up)
            def _():
                detour(side).wait_recv()
                passed(side).start()

    cos = twiddle[0:8, :]
    sin = twiddle[8:16, :]

    @pl.loop(0, NODES)
    def _(n):
        @pl.when(n == 1)
        def _():
            send_halos()

        @pl.when(n == 9)
        def _():
            pass_on()

        for q in range(3):
            forward_in(n, q, block, pool, fwd_send, fwd_recv, partners, rows).wait_recv()
        result[rows(n * BLOCK, BLOCK), :] = collide(
            block[pl.ds(n * 32, 32)].reshape(BLOCK, 128),
            phi[...],
            sym[...],
            rows_fwd[...],
            lanes_fwd[...],
            lanes_bwd[...],
            rows_bwd[...],
            cos,
            sin,
        )
        for q in range(3):
            backward(n, q).start()
        for q in range(3):
            forward(n, q).wait_send()

    total = sums_out[...]
    for q in range(3):
        sums(q).wait_recv()
    for q in range(3):
        total = total + sums_in[q]
    for j in range(4):
        mask = zero
        for e in range(ELEMS):
            on = jnp.where(nb_side[e, j] == 3, jnp.where(wall_flag[e, j] == 1, 1.0, 0.0), 0.0)
            mask = jnp.where(sub % 4 == e, on, mask)
        den = jnp.broadcast_to(total[:, 24 + j : 25 + j], (8, 128))
        sigma = [
            jnp.broadcast_to(total[:, j * 6 + k : j * 6 + k + 1], (8, 128)) / den * mask
            for k in range(6)
        ]
        for n in range(NODES):
            part = lift[0, j, n] * sigma[0]
            for k in range(1, 6):
                part = part + lift[k, j, n] * sigma[k]
            wallsum[(j * NODES + n) * 8 : (j * NODES + n) * 8 + 8, :] = part

    for side, face in ((0, 1), (1, 0)):

        turn = turn_up if side else turn_down
        here_in = has_above if side else has_below

        @pl.when(here_in & jnp.logical_not(turn))
        def _():
            halo(side).wait_recv()

        @pl.when(turn)
        def _():
            halo(side, DIRECT[side]).wait_recv()
            passed(side).wait_recv()

        @pl.when(here_in)
        def _():
            for k in range(6):
                start = HALO + (side * NODES + FACES[face][k]) * 8
                for a in range(8):
                    pool[start + a] = halo_in[side, k * 8 + a]

    @pl.loop(0, 8)
    def _(a):
        v0 = grid(me * 8 + a)
        negs = [jnp.minimum(normal_speed(j, v0, v1), 0.0) for j in range(4)]

        @pl.loop(0, ELEMS)
        def _(e):
            for j in range(4):
                side = nb_side[e, j]
                inner = jnp.where(side == 3, 0, 8)
                edge = TABLE + jnp.where(wall_flag[e, j] == 1, inj_id[e, j], 4) * 8
                near = nb_local[e, j] * (NODES * 8)
                far = HALO + jnp.where(side == 2, NODES * 8, 0)
                base = jnp.where(side == 3, edge, jnp.where(side == 0, near, far)) + a
                for k in range(6):
                    outer = pool[base + inner * FACES[j ^ 1][k]]
                    trace = pool[(e * NODES + FACES[j][k]) * 8 + a]
                    diff[j * 6 + k, rows(e * 8), :] = negs[j] * (trace - outer)

        @pl.loop(0, NODES // 2)
        def _(pair):
            acc = [[zero] * ELEMS for _ in range(2)]
            for m in range(NODES):
                for i in range(2):
                    n = pair * 2 + i
                    c = deriv[n, 0, m] * v0 + deriv[n, 1, m] * v1 + deriv[n, 2, m] * v2
                    for e in range(ELEMS):
                        f = pool[(e * NODES + m) * 8 + a]
                        acc[i][e] = acc[i][e] - c * f
            for j in range(4):
                for k in range(6):
                    for i in range(2):
                        c = lift[k, j, pair * 2 + i]
                        for e in range(ELEMS):
                            d = diff[j * 6 + k, e * 8 : e * 8 + 8, :]
                            acc[i][e] = acc[i][e] + c * d
            for i in range(2):
                for e in range(ELEMS):
                    moved[rows((e * NODES + pair * 2 + i) * SLAB + a * 8), :] = acc[i][e]

    @pl.loop(0, ELEMS)
    def _(e):
        @pl.loop(0, NODES)
        def _(n):
            parts = [
                jnp.broadcast_to(wallsum[pl.ds((j * NODES + n) * 8 + e, 1), :], (8, 128))
                for j in range(4)
            ]
            for a in range(8):
                x = moved[rows((e * NODES + n) * SLAB + a * 8), :]
                for j in range(4):
                    x = x - parts[j] * negwall[(j * 8 + a) * 8 : (j * 8 + a) * 8 + 8, :]
                moved[rows((e * NODES + n) * SLAB + a * 8), :] = x

    @pl.loop(0, NODES)
    def _(n):
        for a in range(8):
            out[pl.ds(n * BLOCK + a * 32 + me, 8, stride=4), :] = (
                result[rows(n * BLOCK + me * SLAB + a * 8), :]
                + moved[rows((me * NODES + n) * SLAB + a * 8), :]
            )
        for q in range(3):
            backward_in(n, q, back, result, bwd_send, bwd_recv, partners, rows).wait_recv()
            e = partners[q]
            for a in range(8):
                at = rows((e * NODES + n) * SLAB + a * 8)
                out[pl.ds(n * BLOCK + a * 32 + e, 8, stride=4), :] = back[at, :] + moved[at, :]
        for q in range(3):
            backward(n, q).wait_send()

    for side in range(2):
        turn = turn_down if side else turn_up
        straight_on = (has_below if side else has_above) & jnp.logical_not(turn)

        @pl.when(straight_on)
        def _():
            halo(side).wait_send()

        @pl.when(turn)
        def _():
            halo(side, DIRECT[side]).wait_send()
            detour(side).wait_send()

        @pl.when(relay_down if side else relay_up)
        def _():
            passed(side).wait_send()

    for q in range(3):
        sums(q).wait_send()


def forward_in(n, q, block, pool, send, recv, partners, rows):
    return pltpu.make_async_remote_copy(
        src_ref=pool.at[pl.ds(0, 8)],
        dst_ref=block.at[pl.ds(n * 32 + partners[q] * 8, 8)],
        send_sem=send.at[n, q],
        recv_sem=recv.at[n, q],
        device_id={"vel": partners[q]},
    )


def backward_in(n, q, back, result, send, recv, partners, rows):
    return pltpu.make_async_remote_copy(
        src_ref=result.at[rows(0, SLAB)],
        dst_ref=back.at[rows((partners[q] * NODES + n) * SLAB, SLAB)],
        send_sem=send.at[n, q],
        recv_sem=recv.at[n, q],
        device_id={"vel": partners[q]},
    )


def solution(mesh):
    space = mesh.shape["space"]
    constants = tables()

    def local(
        dist,
        phi,
        khat,
        deriv,
        lift,
        normals,
        wall_maxw,
        free_stream,
        inject,
        nb_local,
        nb_side,
        wall_flag,
        inj_id,
    ):
        lines = dist.transpose(1, 0, 2).reshape(NODES, ELEMS, SLAB, 128)
        lines = lines.transpose(0, 2, 1, 3).reshape(NODES * BLOCK, 128)
        profiles = inject.reshape(4, SLAB, 128).transpose(1, 0, 2).reshape(BLOCK, 128)
        hbm = pl.BlockSpec(memory_space=pltpu.HBM)
        f32 = jnp.float32
        dma = pltpu.SemaphoreType.DMA

        tables = [jnp.asarray(c) for c in constants]
        operands = [
            lines,
            phi.reshape(BLOCK, 128),
            khat,
            wall_maxw.reshape(SLAB, 128),
            free_stream.reshape(SLAB, 128),
            profiles,
            *tables,
            deriv.transpose(1, 0, 2),
            lift.transpose(2, 0, 1),
            normals,
            nb_local,
            nb_side,
            wall_flag,
            inj_id,
        ]

        def body(*refs):
            kernel(space, *refs)

        rate = pl.pallas_call(
            body,
            out_shape=jax.ShapeDtypeStruct((NODES * BLOCK, 128), f32),
            in_specs=[hbm] * len(operands),
            out_specs=pl.BlockSpec(memory_space=pltpu.VMEM),
            scratch_shapes=[pltpu.VMEM(x.shape, x.dtype) for x in operands[:12]]
            + [pltpu.SMEM(x.shape, x.dtype) for x in operands[12:]]
            + [
                pltpu.VMEM((POOL, 8, 128), f32),
                pltpu.VMEM((NODES * 32, 8, 128), f32),
                pltpu.VMEM((NODES * BLOCK, 128), f32),
                pltpu.VMEM((ELEMS * NODES * SLAB, 128), f32),
                pltpu.VMEM((ELEMS * NODES * SLAB, 128), f32),
                pltpu.VMEM((24, ELEMS * 8, 128), f32),
                pltpu.VMEM((4 * SLAB, 128), f32),
                pltpu.VMEM((BLOCK, 128), f32),
                pltpu.VMEM((BLOCK, 128), f32),
                pltpu.VMEM((HALF, 128), f32),
                pltpu.VMEM((4 * NODES * 8, 128), f32),
                pltpu.VMEM((2, 6 * 8, 8, 128), f32),
                pltpu.VMEM((2, 6 * 8, 8, 128), f32),
                pltpu.VMEM((6 * 8, 8, 128), f32),
                pltpu.VMEM((8, 128), f32),
                pltpu.VMEM((3, 8, 128), f32),
                dma((NODES,)),
                dma((len(operands) - 1,)),
                dma((NODES, 3)),
                dma((NODES, 3)),
                dma((NODES, 3)),
                dma((NODES, 3)),
                dma((2,)),
                dma((2,)),
                dma((2,)),
                dma((2,)),
                pltpu.SemaphoreType.REGULAR,
                dma((3,)),
                dma((3,)),
            ],
            compiler_params=pltpu.CompilerParams(
                collective_id=0, has_side_effects=True, vmem_limit_bytes=40 * 2**20
            ),
            name="rate",
        )(*[pltpu.with_memory_space_constraint(x, pltpu.HBM) for x in operands])
        rate = rate.reshape(NODES, SLAB, ELEMS, 128).transpose(0, 2, 1, 3)
        return rate.reshape(NODES, ELEMS, SLAB * 128).transpose(1, 0, 2)

    return jax.shard_map(
        local,
        mesh=mesh,
        in_specs=(
            P("space", None, "vel"),
            P(),
            P(),
            P(),
            P(),
            P(),
            P("vel"),
            P("vel"),
            P(None, "vel"),
            P("space", None),
            P("space", None),
            P("space", None),
            P("space", None),
        ),
        out_specs=P("space", None, "vel"),
        check_vma=False,
    )
```
